32 devices in a mesh: shard: 4 (over y, x), context: 8 (over z, core).
Axes of the slice: x: 2, y: 2, z: 4, core: 2. Of those that a mesh axis runs over, the one named last changes fastest.
Arguments:
- inputs: bfloat16 [4096, 2560], P(('shard', 'context')), may hold values from -6 to 6
- doc_ids: int32 [4096], P('shard'), may hold values from 0 to 11, as said below
- cotangent: bfloat16 [4096, 2560], P(('shard', 'context')), may hold values from -6 to 6
- attn_gain: bfloat16 [2560], P('shard'), may hold values from 0.5 to 1.5
- query_weight: bfloat16 [2560, 2560], P('shard'), may hold values from -0.25 to 0.25
- keyval_weight: bfloat16 [2560, 512], P('shard'), may hold values from -0.125 to 0.125
- output_weight: bfloat16 [2560, 2560], P('shard'), may hold values from -1 to 1
- output_bias: bfloat16 [2560], P('shard'), may hold values from -1.796875 to 1.796875
- feed_gain: bfloat16 [2560], P('shard'), may hold values from 0.5 to 1.5
- gate_up_weight: bfloat16 [2560, 15360], P('shard'), may hold values from -0.125 to 0.125
- gate_up_bias: bfloat16 [15360], P('shard'), may hold values from -1.796875 to 1.796875
- down_weight: bfloat16 [7680, 2560], P('shard'), may hold values from -0.0625 to 0.0625
- down_bias: bfloat16 [2560], P('shard'), may hold values from -1.796875 to 1.796875
Outputs:
- block_out: bfloat16 [4096, 2560], P(('shard', 'context'))
- input_grad: float32 [4096, 2560], P(('shard', 'context'))
- attn_gain_grad: float32 [2560], P(('shard', 'context'))
- query_grad: float32 [2560, 2560], P(('shard', 'context'))
- keyval_grad: float32 [2560, 512], P(('shard', 'context'))
- output_weight_grad: float32 [2560, 2560], P(None, ('shard', 'context'))
- output_bias_grad: float32 [2560], P(('shard', 'context'))
- feed_gain_grad: float32 [2560], P(('shard', 'context'))
- gate_up_grad: float32 [2560, 15360], P(('shard', 'context'))
- gate_up_bias_grad: float32 [15360], P(('shard', 'context'))
- down_weight_grad: float32 [7680, 2560], P(None, ('shard', 'context'))
- down_bias_grad: float32 [2560], P(('shard', 'context'))
The draws below stay inside these ranges and needn't reach their ends.
Inputs may be any that keep to these rules, and one draw needn't show every extreme that they name: `doc_ids`: ids never fall along the slots; group g (slots g * 1024 to (g + 1) * 1024 - 1) holds documents 3 g, 3 g + 1 and 3 g + 2, each nonempty, the first and the last shorter than 128 slots.
All inputs are finite; a program needn't handle non-finite values.
Results may differ from the reference program's by a relative error of at most 0.014.
The reference program's roundings to bfloat16 on the way count: a program that leaves them out, or rounds other values in their place, can miss the bound.
Values may be sent and summed in bfloat16 or wider, within the bound.
A program may use at most 640 MiB of HBM per device.

```python
import math
import jax
import jax.numpy as jnp
from jax import lax

D = 2560
HEADS = 10
DH = 256
FF = 7680
WINDOW = 2048
TOK_DEV = 128
GROUP = 1024
TOKENS = 4096


def draw_doc_ids(key, part):
    key = jax.random.fold_in(key, 11)
    groups = TOKENS // GROUP
    first_key, last_key = jax.random.split(key)
    first_cut = jax.random.randint(first_key, (groups, 1), 1, TOK_DEV)
    last_cut = jax.random.randint(last_key, (groups, 1), GROUP - TOK_DEV + 1, GROUP)
    slots = jnp.arange(GROUP, dtype=jnp.int32)[None, :]
    inner = (slots >= first_cut).astype(jnp.int32) + (slots >= last_cut).astype(jnp.int32)
    labels = inner + 3 * jnp.arange(groups, dtype=jnp.int32)[:, None]
    return labels.reshape(TOKENS).astype(jnp.int32)


def level_of(stream_key, extent, cuts, smallest, high):
    factor_of = 1.0
    for axis_at, blocks in cuts:
        heights = jax.random.uniform(jax.random.fold_in(jax.random.fold_in(stream_key, 6), axis_at), (blocks,), jnp.float32, smallest / len(cuts), high / len(cuts))
        factor_of = factor_of * jnp.repeat(jnp.exp(heights), extent[axis_at] // blocks).reshape((-1,) + (1,) * (len(extent) - 1 - axis_at))
    return factor_of


def normal_values(own_key, dims, scale, most, pieces=(), held_as=jnp.bfloat16):
    loudness = level_of(own_key, dims, pieces, -0.22, 0.18) if pieces else 1.0
    values = jax.random.normal(own_key, dims, jnp.float32) * scale * loudness
    return jnp.minimum(jnp.maximum(values, -most), most).astype(held_as)


def setup_inputs(seed: int = 0) -> dict:
    streams_of = jax.random.split(jax.random.key(seed), 14)
    return {
        "inputs": normal_values(streams_of[0], (TOKENS, D), 1.0, 6.0, ((0, 32),)),
        "doc_ids": draw_doc_ids(jax.random.fold_in(streams_of[13], 71), 0),
        "cotangent": normal_values(streams_of[2], (TOKENS, D), 1.0, 6.0, ((0, 32),)),
        "attn_gain": jnp.clip(1.0 + 0.1 * jax.random.normal(streams_of[3], (D,), jnp.float32), 0.5, 1.5).astype(jnp.bfloat16),
        "query_weight": normal_values(streams_of[4], (D, HEADS * DH), (D // 4) ** -0.5, 0.25, ((0, 4),)),
        "keyval_weight": normal_values(streams_of[5], (D, 2 * DH), D ** -0.5, 0.125, ((0, 4),)),
        "output_weight": normal_values(streams_of[6], (HEADS * DH, D), (D // 64) ** -0.5, 1.0, ((0, 4),)),
        "output_bias": normal_values(streams_of[7], (D,), 0.3, 1.796875, ((0, 4),)),
        "feed_gain": jnp.clip(1.0 + 0.1 * jax.random.normal(streams_of[8], (D,), jnp.float32), 0.5, 1.5).astype(jnp.bfloat16),
        "gate_up_weight": normal_values(streams_of[9], (D, 2 * FF), D ** -0.5, 0.125, ((0, 4),)),
        "gate_up_bias": normal_values(streams_of[10], (2 * FF,), 0.3, 1.796875, ((0, 4),)),
        "down_weight": normal_values(streams_of[11], (FF, D), FF ** -0.5, 0.0625, ((0, 4),)),
        "down_bias": normal_values(streams_of[12], (D,), 0.3, 1.796875, ((0, 4),)),
    }


@jax.custom_vjp
def low(v):
    return lax.optimization_barrier(v.astype(jnp.bfloat16)).astype(jnp.float32)

@jax.custom_vjp
def low_back(v):
    return v

def low_keep(v):
    return (low(v), None)

def low_pass(kept, grad):
    return (grad,)

def back_keep(v):
    return (v, None)

def back_low(kept, grad):
    return (low(grad),)
low.defvjp(low_keep, low_pass)
low_back.defvjp(back_keep, back_low)
EPS = 1e-06
NEG = -1e+30
ROPE_LOG = math.log(10000.0)
HIGH = lax.Precision.HIGHEST

def frequencies(head_dim):
    quarter = head_dim // 4
    steps = jnp.arange(quarter).astype(jnp.float32)
    return jnp.exp(-ROPE_LOG * (2.0 * steps) / (head_dim // 2))

def rotate(field, cosine, sine):
    width = field.shape[-1] // 2
    quarter = width // 2
    first = field[..., :quarter]
    second = field[..., quarter:width]
    return jnp.concatenate([first * cosine - second * sine, second * cosine + first * sine, field[..., width:]], axis=-1)

def rms_norm(field, gain):
    return field * lax.rsqrt(lax.optimization_barrier(jnp.mean(field * field, axis=-1, keepdims=True)) + EPS) * gain

def geglu(gate_up):
    half = gate_up.shape[-1] // 2
    return jax.nn.gelu(gate_up[:, :half], approximate=True) * gate_up[:, half:]

def block_forward(params, source, docs):
    attn_gain, query_weight, keyval_weight, output_weight, output_bias, feed_gain, gate_up_weight, gate_up_bias, down_weight, down_bias = params
    attn_in = low(rms_norm(source, attn_gain))
    query_raw = low_back(jnp.dot(attn_in, query_weight, precision=HIGH))
    keyval_raw = low_back(jnp.dot(attn_in, keyval_weight, precision=HIGH))
    slots = jnp.arange(GROUP).astype(jnp.float32)
    angles = slots[:, None] * frequencies(DH)[None, :]
    cosine = jnp.cos(angles)
    sine = jnp.sin(angles)
    queries = low(rotate(query_raw.reshape(GROUP, HEADS, DH), cosine[:, None, :], sine[:, None, :]) * DH ** (-0.5))
    keys = low(rotate(keyval_raw[:, :DH], cosine, sine))
    values = low(keyval_raw[:, DH:])
    pad_keys = jnp.concatenate([jnp.zeros((WINDOW, DH), keys.dtype), keys], axis=0)
    pad_values = jnp.concatenate([jnp.zeros((WINDOW, DH), values.dtype), values], axis=0)
    pad_docs = jnp.concatenate([jnp.full((WINDOW,), -1, jnp.int32), docs.astype(jnp.int32)], axis=0)

    def one_block(start):
        block_queries = lax.dynamic_slice_in_dim(queries, start, TOK_DEV, 0)
        key_block = lax.dynamic_slice_in_dim(pad_keys, start, WINDOW + TOK_DEV, 0)
        value_block = lax.dynamic_slice_in_dim(pad_values, start, WINDOW + TOK_DEV, 0)
        query_docs = lax.dynamic_slice_in_dim(pad_docs, start + WINDOW, TOK_DEV, 0)
        key_docs = lax.dynamic_slice_in_dim(pad_docs, start, WINDOW + TOK_DEV, 0)
        query_slot = start + jnp.arange(TOK_DEV, dtype=jnp.int32)
        key_slot = start - WINDOW + jnp.arange(WINDOW + TOK_DEV, dtype=jnp.int32)
        distance = query_slot[:, None] - key_slot[None, :]
        allowed = (query_docs[:, None] == key_docs[None, :]) & (distance >= 0) & (distance < WINDOW)
        scores = low_back(jnp.einsum('thd,sd->ths', block_queries, key_block, precision=HIGH))
        scores = jnp.where(allowed[:, None, :], scores, NEG)
        weights = jax.nn.softmax(scores, axis=-1)
        mixed = jnp.einsum('ths,sd->thd', low(weights), value_block, precision=HIGH)
        return low(low_back(mixed)).reshape(TOK_DEV, HEADS * DH)
    starts = (jnp.arange(GROUP // TOK_DEV, dtype=jnp.int32) * TOK_DEV).astype(jnp.int32)
    mixed = lax.map(jax.checkpoint(one_block), starts).reshape(GROUP, HEADS * DH)
    attn_out = jnp.dot(mixed, output_weight, precision=HIGH) + output_bias
    resid = source + low_back(attn_out)
    feed_in = low(rms_norm(resid, feed_gain))
    gate_up = low_back(jnp.dot(feed_in, gate_up_weight, precision=HIGH) + gate_up_bias)
    hidden = low(geglu(gate_up))
    feed_out = jnp.dot(hidden, down_weight, precision=HIGH) + down_bias
    return resid + low_back(feed_out)

def reference(inputs, doc_ids, cotangent, attn_gain, query_weight, keyval_weight, output_weight, output_bias, feed_gain, gate_up_weight, gate_up_bias, down_weight, down_bias):
    params = tuple((value.astype(jnp.float32) for value in (attn_gain, query_weight, keyval_weight, output_weight, output_bias, feed_gain, gate_up_weight, gate_up_bias, down_weight, down_bias)))
    groups = TOKENS // GROUP
    docs = doc_ids.reshape(groups, GROUP)

    def whole(source, *weights):

        def per_group(item):
            return block_forward(weights, item[0], item[1])
        return lax.map(jax.checkpoint(per_group), (source.reshape(groups, GROUP, D), docs)).reshape(TOKENS, D)
    result, pull = jax.vjp(whole, inputs.astype(jnp.float32), *params)
    grads = pull(cotangent.astype(jnp.float32))
    return (result.astype(jnp.bfloat16), grads[0], grads[1], grads[2], grads[3], grads[4], grads[5], grads[6], grads[7], grads[8], grads[9], grads[10])
```

```python
import math

import jax
import jax.numpy as jnp
from jax import lax
from jax.experimental import pallas as pl
from jax.experimental.pallas import tpu as pltpu
from jax.sharding import PartitionSpec as P

HEADS = 10
DH = 256
FF = 7680
WINDOW = 2048


EPS = 1e-06
NEG = -1e30
ROPE_LOG = math.log(10000.0)


def frequencies(head_dim):
    quarter = head_dim // 4
    steps = jnp.arange(quarter).astype(jnp.float32)
    return jnp.exp(-ROPE_LOG * (2.0 * steps) / (head_dim // 2))


def rotate(field, cosine, sine):
    width = field.shape[-1] // 2
    quarter = width // 2
    first = field[..., :quarter]
    second = field[..., quarter:width]
    return jnp.concatenate(
        [first * cosine - second * sine, second * cosine + first * sine, field[..., width:]],
        axis=-1,
    )


def rms_norm(field, gain):
    return field * lax.rsqrt(jnp.mean(field * field, axis=-1, keepdims=True) + EPS) * gain


def geglu(gate_up):
    half = gate_up.shape[-1] // 2
    return jax.nn.gelu(gate_up[:, :half], approximate=True) * gate_up[:, half:]


def over_rows(left, right):
    return lax.dot_general(
        left, right, (((0,), (0,)), ((), ())), preferred_element_type=jnp.float32
    )


def against(left, weight):
    return lax.dot_general(
        left, weight, (((1,), (1,)), ((), ())), preferred_element_type=jnp.float32
    )


def regroup(field, shard_count, context_count):
    rows_now, width = field.shape
    owned = width // (shard_count * context_count)
    return (
        field.reshape(rows_now, shard_count, context_count, owned)
        .transpose(0, 2, 1, 3)
        .reshape(rows_now, width)
    )


VMEM_LIMIT = 56 * 1024 * 1024
LANES = 128


def gather(value, axis):
    return lax.all_gather(value, axis, axis=0, tiled=True)


def sibling(value):
    count = lax.axis_size("context")
    return lax.ppermute(value, "context", [(i, i ^ 1) for i in range(count)])


def pair_rows(own, core):
    other = sibling(own)
    return jnp.where(
        core == 0, jnp.concatenate([own, other], axis=0), jnp.concatenate([other, own], axis=0)
    )


def halves(value, core, axis):
    low, high = jnp.split(value, 2, axis=axis)
    return jnp.where(core == 0, low, high), jnp.where(core == 0, high, low)


def swap_rows(value, core):
    mine, theirs = halves(value, core, 0)
    other = sibling(theirs)
    return jnp.where(
        core == 0, jnp.concatenate([mine, other], axis=1), jnp.concatenate([other, mine], axis=1)
    )


def swap_columns(own, core):
    mine, theirs = halves(own, core, 1)
    other = sibling(theirs)
    return jnp.where(
        core == 0, jnp.concatenate([mine, other], axis=0), jnp.concatenate([other, mine], axis=0)
    )


def summed_half(value, core, axis):
    mine, theirs = halves(value, core, axis)
    return mine + sibling(theirs)


def unit_tiles(ff, shards, contexts):
    per_shard = ff // shards // LANES
    return -(-per_shard // contexts), per_shard


def take_units_kernel(start_ref, weight_ref, out_ref):
    out_ref[...] = weight_ref[...]


def take_units(weight, start_tile, shards, width, per_shard):
    rows = weight.shape[0]

    def source(i, start):
        part, rest = i // (shards * width), i % (shards * width)
        return 0, part * shards * per_shard + (rest // width) * per_shard + start[0] + rest % width

    return pl.pallas_call(
        take_units_kernel,
        grid_spec=pltpu.PrefetchScalarGridSpec(
            num_scalar_prefetch=1,
            grid=(2 * shards * width,),
            in_specs=[pl.BlockSpec((rows, LANES), source)],
            out_specs=pl.BlockSpec((rows, LANES), lambda i, start: (0, i)),
        ),
        out_shape=jax.ShapeDtypeStruct((rows, 2 * shards * width * LANES), weight.dtype),
    )(start_tile.reshape(1), weight)


def join_units(pieces, parts, shards, width, per_shard):
    contexts, inner = pieces.shape[0], pieces.shape[1:-1]
    field = pieces.reshape(contexts, *inner, parts, shards, width * LANES)
    kept = []
    for at in range(contexts):
        first = at * width
        if first >= per_shard:
            continue
        start = min(first, per_shard - width)
        stop = min(first + width, per_shard)
        kept.append(field[at, ..., (first - start) * LANES : (stop - start) * LANES])
    return jnp.concatenate(kept, axis=-1).reshape(*inner, parts * shards * per_shard * LANES)


def masked_weights(q, k, mask):
    scores = lax.dot_general(q, k, (((1,), (1,)), ((), ())), preferred_element_type=jnp.float32)
    scores = jnp.where(mask > 0.0, scores, NEG)
    raised = jnp.exp(scores - jnp.max(scores, axis=1, keepdims=True))
    return raised / jnp.sum(raised, axis=1, keepdims=True)


def mix_kernel(mask_ref, q_ref, k_ref, v_ref, out_ref):
    weights = masked_weights(q_ref[...], k_ref[...], mask_ref[...])
    out_ref[...] = jnp.dot(
        weights.astype(jnp.bfloat16), v_ref[...], preferred_element_type=jnp.float32
    ).astype(jnp.bfloat16)


def mix(mask, queries, keys, values):
    rows, width = queries.shape
    slots = keys.shape[0]
    whole = lambda h: (0, 0)
    part = lambda h: (0, h)
    return pl.pallas_call(
        mix_kernel,
        grid=(width // DH,),
        in_specs=[
            pl.BlockSpec((rows, slots), whole),
            pl.BlockSpec((rows, DH), part),
            pl.BlockSpec((slots, DH), whole),
            pl.BlockSpec((slots, DH), whole),
        ],
        out_specs=pl.BlockSpec((rows, DH), part),
        out_shape=jax.ShapeDtypeStruct((rows, width), jnp.bfloat16),
        compiler_params=pltpu.CompilerParams(vmem_limit_bytes=VMEM_LIMIT),
    )(mask, queries, keys, values)


def mix_back_kernel(mask_ref, q_ref, k_ref, v_ref, g_ref, dq_ref, dk_ref, dv_ref):
    q, k, g = q_ref[...], k_ref[...], g_ref[...]
    weights = masked_weights(q, k, mask_ref[...])
    value_score = against(g, v_ref[...])
    delta = jnp.sum(weights * value_score, axis=1, keepdims=True)
    score_back = (weights * (value_score - delta)).astype(jnp.bfloat16)
    dq_ref[...] = jnp.dot(score_back, k, preferred_element_type=jnp.float32)
    key_piece = over_rows(score_back, q)
    value_piece = over_rows(weights.astype(jnp.bfloat16), g)

    @pl.when(pl.program_id(0) == 0)
    def _():
        dk_ref[...] = key_piece
        dv_ref[...] = value_piece

    @pl.when(pl.program_id(0) > 0)
    def _():
        dk_ref[...] += key_piece
        dv_ref[...] += value_piece


def mix_back(mask, queries, keys, values, grad):
    rows, width = queries.shape
    slots = keys.shape[0]
    whole = lambda h: (0, 0)
    part = lambda h: (0, h)
    return pl.pallas_call(
        mix_back_kernel,
        grid=(width // DH,),
        in_specs=[
            pl.BlockSpec((rows, slots), whole),
            pl.BlockSpec((rows, DH), part),
            pl.BlockSpec((slots, DH), whole),
            pl.BlockSpec((slots, DH), whole),
            pl.BlockSpec((rows, DH), part),
        ],
        out_specs=[
            pl.BlockSpec((rows, DH), part),
            pl.BlockSpec((slots, DH), whole),
            pl.BlockSpec((slots, DH), whole),
        ],
        out_shape=[
            jax.ShapeDtypeStruct((rows, width), jnp.float32),
            jax.ShapeDtypeStruct((slots, DH), jnp.float32),
            jax.ShapeDtypeStruct((slots, DH), jnp.float32),
        ],
        compiler_params=pltpu.CompilerParams(vmem_limit_bytes=VMEM_LIMIT),
    )(mask, queries, keys, values, grad)


def body(
    inputs,
    doc_ids,
    cotangent,
    attn_gain,
    query_weight,
    keyval_weight,
    output_weight,
    output_bias,
    feed_gain,
    gate_up_weight,
    gate_up_bias,
    down_weight,
    down_bias,
):
    tok, model = inputs.shape
    shards, contexts = lax.axis_size("shard"), lax.axis_size("context")
    shard, place = lax.axis_index("shard"), lax.axis_index("context")
    core, chip = place % 2, place // 2
    group = tok * contexts
    owned = model // (shards * contexts)
    ff = gate_up_weight.shape[1] // 2
    width, per_shard = unit_tiles(ff, shards, contexts)
    unit_start = jnp.minimum(place * width, per_shard - width)
    units = shards * width * LANES

    vectors = jnp.concatenate([attn_gain, output_bias, feed_gain, down_bias, gate_up_bias])
    vectors = gather(vectors[None], "shard").astype(jnp.float32)
    gain_one, bias_out, gain_two, bias_down = (
        vectors[:, i * (model // shards) : (i + 1) * (model // shards)].reshape(1, model)
        for i in range(4)
    )
    bias_gate_up = vectors[:, 4 * (model // shards) :].reshape(2 * shards, per_shard * LANES)
    bias_gate_up = lax.dynamic_slice_in_dim(
        bias_gate_up, unit_start * LANES, width * LANES, 1
    ).reshape(1, 2 * units)
    keyval_half = gather(halves(keyval_weight, core, 1)[0], "shard")
    query_half = gather(halves(query_weight, core, 1)[0], "shard")
    output_half = gather(halves(output_weight, core, 1)[0], "shard")
    gate_up_part = gather(
        take_units(gate_up_weight, unit_start, shards, width, per_shard), "shard"
    )
    down_part = gather(
        lax.dynamic_slice_in_dim(down_weight, unit_start * LANES, width * LANES, 0), "shard"
    )
    unit_at = unit_start * LANES + jnp.arange(width * LANES, dtype=jnp.int32)
    unit_live = jnp.tile(unit_at >= place * width * LANES, shards)[None, :]

    source = inputs.astype(jnp.float32)
    attn_in = rms_norm(source, gain_one).astype(jnp.bfloat16)
    attn_pair = pair_rows(attn_in, core)
    slots = jnp.arange(group, dtype=jnp.int32)
    pair_slots = chip * (2 * tok) + jnp.arange(2 * tok, dtype=jnp.int32)
    pair_docs = lax.dynamic_slice_in_dim(doc_ids, chip * (2 * tok), 2 * tok)
    distance = pair_slots[:, None] - slots[None, :]
    mask = (
        (pair_docs[:, None] == doc_ids[None, :]) & (distance >= 0) & (distance < WINDOW)
    ).astype(jnp.float32)
    angles = pair_slots.astype(jnp.float32)[:, None] * frequencies(DH)[None, :]
    cosine, sine = jnp.cos(angles), jnp.sin(angles)
    keyval_raw = jnp.dot(attn_pair, keyval_half, preferred_element_type=jnp.float32)
    keyval = jnp.where(core == 0, rotate(keyval_raw, cosine, sine), keyval_raw).astype(jnp.bfloat16)
    keyval = gather(keyval, "context").reshape(contexts // 2, 2, 2 * tok, DH)
    keys, values = keyval[:, 0].reshape(group, DH), keyval[:, 1].reshape(group, DH)
    query_raw = jnp.dot(attn_pair, query_half, preferred_element_type=jnp.float32)
    heads = query_raw.shape[1] // DH
    queries = (
        (
            rotate(query_raw.reshape(2 * tok, heads, DH), cosine[:, None, :], sine[:, None, :])
            * DH ** (-0.5)
        )
        .astype(jnp.bfloat16)
        .reshape(2 * tok, heads * DH)
    )
    mixed_half = mix(mask, queries, keys, values)
    mixed_own = swap_rows(mixed_half, core)
    mixed_pair = pair_rows(mixed_own, core)
    attn_out = swap_rows(
        jnp.dot(mixed_pair, output_half, preferred_element_type=jnp.float32), core
    )
    resid = source + attn_out + bias_out

    feed_in = rms_norm(resid, gain_two).astype(jnp.bfloat16)
    grad_group = gather(cotangent, "context")
    feed_group = gather(feed_in, "context")
    gate_up = jnp.dot(feed_group, gate_up_part, preferred_element_type=jnp.float32) + bias_gate_up
    hidden_grad = against(grad_group, down_part)

    def live_geglu(field):
        return jnp.where(unit_live, geglu(field), 0.0)

    hidden, geglu_pull = jax.vjp(live_geglu, gate_up)
    hidden = hidden.astype(jnp.bfloat16)
    gate_up_low = geglu_pull(hidden_grad)[0].astype(jnp.bfloat16)
    feed_part = against(gate_up_low, gate_up_part).astype(jnp.bfloat16)
    feed_in_grad = lax.psum_scatter(
        feed_part, "context", scatter_dimension=0, tiled=True
    ).astype(jnp.float32)
    down_out = lax.psum_scatter(
        jnp.dot(hidden, down_part, preferred_element_type=jnp.float32).astype(jnp.bfloat16),
        "context",
        scatter_dimension=0,
        tiled=True,
    ).astype(jnp.float32)
    block_out = (resid + down_out + bias_down).astype(jnp.bfloat16)

    grad_out = cotangent.astype(jnp.float32)
    resid_part, gain_two_grad = jax.vjp(rms_norm, resid, gain_two)[1](feed_in_grad)
    resid_grad = grad_out + resid_part
    attn_grad_low = resid_grad.astype(jnp.bfloat16)
    mixed_back = summed_half(
        against(swap_columns(attn_grad_low, core), output_half), core, 1
    ).astype(jnp.bfloat16)
    query_acc, key_acc, value_acc = mix_back(mask, queries, keys, values, mixed_back)
    keyval_acc = jnp.stack(
        [key_acc.reshape(contexts // 2, 2 * tok, DH), value_acc.reshape(contexts // 2, 2 * tok, DH)],
        axis=1,
    ).reshape(2 * group, DH)
    keyval_acc = lax.psum_scatter(keyval_acc, "context", scatter_dimension=0, tiled=True)
    keyval_back = jnp.where(core == 0, rotate(keyval_acc, cosine, -sine), keyval_acc).astype(
        jnp.bfloat16
    )
    query_back = (
        rotate(query_acc.reshape(2 * tok, heads, DH), cosine[:, None, :], -sine[:, None, :])
        * DH ** (-0.5)
    ).reshape(2 * tok, heads * DH).astype(jnp.bfloat16)
    attn_in_grad = summed_half(
        against(query_back, query_half) + against(keyval_back, keyval_half), core, 0
    )
    input_part, gain_one_grad = jax.vjp(rms_norm, source, gain_one)[1](attn_in_grad)
    input_grad = resid_grad + input_part

    gate_up_sum = lax.psum_scatter(
        over_rows(feed_group, gate_up_low).astype(jnp.bfloat16),
        "shard",
        scatter_dimension=0,
        tiled=True,
    )
    down_sum = lax.psum_scatter(
        over_rows(grad_group, hidden).astype(jnp.bfloat16),
        "shard",
        scatter_dimension=0,
        tiled=True,
    )

    def to_owners(field):
        return lax.all_to_all(
            field.reshape(contexts, owned, field.shape[1]), "context", split_axis=0, concat_axis=0
        ).astype(jnp.float32)

    gate_up_grad = join_units(to_owners(gate_up_sum), 2, shards, width, per_shard)
    down_weight_grad = join_units(to_owners(down_sum), 1, shards, width, per_shard).T

    def token_rows(field):
        return lax.all_to_all(
            regroup(field, shards, contexts), "context", split_axis=1, concat_axis=0, tiled=True
        )

    back_own = jnp.concatenate(
        [swap_rows(query_back, core), swap_rows(keyval_back, core)], axis=1
    )
    back_group = gather(back_own, "context")
    mixed_group = gather(mixed_own, "context")
    attn_sum = lax.psum_scatter(
        jnp.concatenate(
            [
                over_rows(token_rows(attn_in), back_group),
                over_rows(token_rows(attn_grad_low), mixed_group),
            ],
            axis=1,
        ).astype(jnp.bfloat16),
        "shard",
        scatter_dimension=0,
        tiled=True,
    ).astype(jnp.float32)
    head_cols = HEADS * DH
    query_grad = attn_sum[:, :head_cols]
    keyval_grad = attn_sum[:, head_cols : head_cols + 2 * DH]
    output_weight_grad = attn_sum[:, head_cols + 2 * DH :].T

    sums = jnp.concatenate(
        [
            gain_one_grad.reshape(model),
            jnp.sum(attn_grad_low.astype(jnp.float32), axis=0),
            gain_two_grad.reshape(model),
            jnp.sum(grad_out, axis=0),
            jnp.sum(gate_up_low.astype(jnp.float32), axis=0),
        ]
    )
    sums = lax.all_gather(sums, ("shard", "context"), axis=0, tiled=False)
    device = shard * contexts + place
    own = [
        jnp.sum(
            lax.dynamic_slice_in_dim(sums[:, i * model : (i + 1) * model], device * owned, owned, 1),
            axis=0,
        )
        for i in range(4)
    ]
    unit_sums = jnp.sum(sums[:, 4 * model :].reshape(shards, contexts, 2 * units), axis=0)
    unit_sums = join_units(unit_sums, 2, shards, width, per_shard)
    unit_owned = 2 * ff // (shards * contexts)
    gate_up_bias_grad = lax.dynamic_slice_in_dim(unit_sums, device * unit_owned, unit_owned)
    return (
        block_out,
        input_grad,
        own[0],
        query_grad,
        keyval_grad,
        output_weight_grad,
        own[1],
        own[2],
        gate_up_grad,
        gate_up_bias_grad,
        down_weight_grad,
        own[3],
    )


def solution(mesh):
    placed = (
        P(("shard", "context"), None),
        P("shard"),
        P(("shard", "context"), None),
        P("shard"),
        P("shard", None),
        P("shard", None),
        P("shard", None),
        P("shard"),
        P("shard"),
        P("shard", None),
        P("shard"),
        P("shard", None),
        P("shard"),
    )
    return jax.shard_map(
        body,
        mesh=mesh,
        in_specs=placed,
        out_specs=(
            P(("shard", "context"), None),
            P(("shard", "context"), None),
            P(("shard", "context")),
            P(("shard", "context"), None),
            P(("shard", "context"), None),
            P(None, ("shard", "context")),
            P(("shard", "context")),
            P(("shard", "context")),
            P(("shard", "context"), None),
            P(("shard", "context")),
            P(None, ("shard", "context")),
            P(("shard", "context")),
        ),
        check_vma=False,
    )
```

```python
import functools
import math

import jax
import jax.numpy as jnp
from jax import lax
from jax.experimental import pallas as pl
from jax.experimental.pallas import tpu as pltpu
from jax.sharding import PartitionSpec as P

HEADS = 10
DH = 256
FF = 7680
WINDOW = 2048


EPS = 1e-06
NEG = -1e30
ROPE_LOG = math.log(10000.0)


def frequencies(head_dim):
    quarter = head_dim // 4
    steps = jnp.arange(quarter).astype(jnp.float32)
    return jnp.exp(-ROPE_LOG * (2.0 * steps) / (head_dim // 2))


def rotate(field, cosine, sine):
    width = field.shape[-1] // 2
    quarter = width // 2
    first = field[..., :quarter]
    second = field[..., quarter:width]
    return jnp.concatenate(
        [first * cosine - second * sine, second * cosine + first * sine, field[..., width:]],
        axis=-1,
    )


def rms_norm(field, gain):
    return field * lax.rsqrt(jnp.mean(field * field, axis=-1, keepdims=True) + EPS) * gain


def geglu(gate_up):
    half = gate_up.shape[-1] // 2
    return jax.nn.gelu(gate_up[:, :half], approximate=True) * gate_up[:, half:]


def over_rows(left, right):
    return lax.dot_general(
        left, right, (((0,), (0,)), ((), ())), preferred_element_type=jnp.float32
    )


def against(left, weight):
    return lax.dot_general(
        left, weight, (((1,), (1,)), ((), ())), preferred_element_type=jnp.float32
    )


def regroup(field, shard_count, context_count):
    rows_now, width = field.shape
    owned = width // (shard_count * context_count)
    return (
        field.reshape(rows_now, shard_count, context_count, owned)
        .transpose(0, 2, 1, 3)
        .reshape(rows_now, width)
    )


VMEM_LIMIT = 56 * 1024 * 1024
LANES = 128
MESH = pl.DeviceIdType.MESH
GELU = 0.7978845608028654
CUBE = 0.044715


def gather(value, axis):
    return lax.all_gather(value, axis, axis=0, tiled=True)


def across(value, bit):
    count = lax.axis_size("shard")
    return lax.ppermute(value, "shard", [(i, i ^ bit) for i in range(count)])


def shard_gather(block, shard):
    rows = block.shape[0]
    near, next_near = across(block, 1), across(block, 2)
    far = jnp.concatenate(
        [across(next_near[: rows // 2], 1), across(near[rows // 2 :], 2)], axis=0
    )
    whole = jnp.zeros((4 * rows, block.shape[1]), block.dtype)
    for bits, part in enumerate((block, near, next_near, far)):
        whole = lax.dynamic_update_slice_in_dim(whole, part, (shard ^ bits) * rows, 0)
    return whole


def vector_gather(own, shard):
    near, next_near = across(own, 1), across(own, 2)
    far = across(near, 2)
    found = jnp.stack([own, near, next_near, far])
    return jnp.stack([lax.dynamic_index_in_dim(found, shard ^ j, 0, False) for j in range(4)])


def shard_sum(parts):
    half = parts[0].shape[1] // 2

    def two_hops(pieces, first, second):
        own, passed = pieces[0], pieces[second]
        got = across(jnp.concatenate([pieces[first], pieces[3]], axis=0), first).astype(jnp.float32)
        rows = own.shape[0]
        passed = (passed.astype(jnp.float32) + got[rows:]).astype(jnp.bfloat16)
        return own.astype(jnp.float32) + got[:rows] + across(passed, second).astype(jnp.float32)

    return jnp.concatenate(
        [
            two_hops([p[:, :half] for p in parts], 1, 2),
            two_hops([p[:, half:] for p in parts], 2, 1),
        ],
        axis=1,
    )


def over_shard_rows(left, right, shard):
    rows = left.shape[1] // 4
    return [
        over_rows(lax.dynamic_slice_in_dim(left, (shard ^ bits) * rows, rows, 1), right).astype(
            jnp.bfloat16
        )
        for bits in range(4)
    ]


def after(value, *earlier):
    return lax.optimization_barrier((value, *earlier))[0]


def sibling(value):
    count = lax.axis_size("context")
    return lax.ppermute(value, "context", [(i, i ^ 1) for i in range(count)])


def pair_rows(own, core):
    other = sibling(own)
    return jnp.where(
        core == 0, jnp.concatenate([own, other], axis=0), jnp.concatenate([other, own], axis=0)
    )


def halves(value, core, axis):
    low, high = jnp.split(value, 2, axis=axis)
    return jnp.where(core == 0, low, high), jnp.where(core == 0, high, low)


def swap_rows(value, core):
    mine, theirs = halves(value, core, 0)
    other = sibling(theirs)
    return jnp.where(
        core == 0, jnp.concatenate([mine, other], axis=1), jnp.concatenate([other, mine], axis=1)
    )


def swap_columns(own, core):
    mine, theirs = halves(own, core, 1)
    other = sibling(theirs)
    return jnp.where(
        core == 0, jnp.concatenate([mine, other], axis=0), jnp.concatenate([other, mine], axis=0)
    )


def summed_half(value, core, axis):
    mine, theirs = halves(value, core, axis)
    return mine + sibling(theirs)


def unit_tiles(ff, shards, contexts):
    per_shard = ff // shards // LANES
    return -(-per_shard // contexts), per_shard


def join_units(pieces, parts, shards, width, per_shard):
    contexts, inner = pieces.shape[0], pieces.shape[1:-1]
    field = pieces.reshape(contexts, *inner, parts, shards, width * LANES)
    kept = []
    for at in range(contexts):
        first = at * width
        if first >= per_shard:
            continue
        start = min(first, per_shard - width)
        stop = min(first + width, per_shard)
        kept.append(field[at, ..., (first - start) * LANES : (stop - start) * LANES])
    return jnp.concatenate(kept, axis=-1).reshape(*inner, parts * shards * per_shard * LANES)


def shard_places():
    here = lax.axis_index("shard")
    return here, here + 1 - 2 * lax.rem(here, 2), lax.rem(here + 2, 4), 3 - here


def greet(*places):
    barrier = pltpu.get_barrier_semaphore()
    for place in places:
        pl.semaphore_signal(barrier, 1, device_id={"shard": place}, device_id_type=MESH)
    pl.semaphore_wait(barrier, len(places))


def to_shard(source, target, send, receive, place):
    return pltpu.make_async_remote_copy(
        src_ref=source,
        dst_ref=target,
        send_sem=send,
        recv_sem=receive,
        device_id={"shard": place},
        device_id_type=MESH,
    )


def gather_kernel(cuts, *refs):
    count = len(cuts)
    sources, wholes = refs[:count], refs[count : 2 * count]
    send, receive, local, send_on, receive_on = refs[2 * count :]
    here, along_x, along_y, far = shard_places()
    greet(along_x, along_y)

    def block(i, place, start, rows):
        return pl.ds(pl.multiple_of(place * cuts[i][0] + start, 16), rows)

    kept, sent = [], []
    for i, (rows, pieces) in enumerate(cuts):
        for j, (row, column, wide, into) in enumerate(pieces()):
            piece = sources[i].at[pl.ds(row, rows), pl.ds(column, wide)]
            target = wholes[i].at[block(i, here, 0, rows), pl.ds(into, wide)]
            kept.append(pltpu.make_async_copy(piece, target, local.at[i, j]))
            kept[-1].start()
            for hop, place in enumerate((along_x, along_y)):
                sent.append(to_shard(piece, target, send.at[i, j, hop], receive.at[i, j, hop], place))
                sent[-1].start()
    for i, (rows, pieces) in enumerate(cuts):
        half = rows // 2
        for j, (row, column, wide, into) in enumerate(pieces()):
            for hop, place in enumerate((along_x, along_y)):
                came = wholes[i].at[block(i, place, 0, rows), pl.ds(into, wide)]
                to_shard(came, came, send.at[i, j, hop], receive.at[i, j, hop], place).wait_recv()
        for hop, (place, owner, start) in enumerate(((along_x, along_y, 0), (along_y, along_x, half))):
            part = wholes[i].at[block(i, owner, start, half)]
            sent.append(to_shard(part, part, send_on.at[i, hop], receive_on.at[i, hop], place))
            sent[-1].start()
    for i, (rows, pieces) in enumerate(cuts):
        half = rows // 2
        for hop, (place, start) in enumerate(((along_x, 0), (along_y, half))):
            came = wholes[i].at[block(i, far, start, half)]
            to_shard(came, came, send_on.at[i, hop], receive_on.at[i, hop], place).wait_recv()
    for copy in kept:
        copy.wait()
    for copy in sent:
        copy.wait_send()


def gather_cuts(arrays, cuts, shapes, number):
    count = len(arrays)
    most = 8
    return pl.pallas_call(
        functools.partial(gather_kernel, cuts),
        in_specs=[pl.BlockSpec(memory_space=pl.ANY)] * count,
        out_specs=[pl.BlockSpec(memory_space=pl.ANY)] * count,
        out_shape=[jax.ShapeDtypeStruct(shape, jnp.bfloat16) for shape in shapes],
        scratch_shapes=[
            pltpu.SemaphoreType.DMA((count, most, 2)),
            pltpu.SemaphoreType.DMA((count, most, 2)),
            pltpu.SemaphoreType.DMA((count, most)),
            pltpu.SemaphoreType.DMA((count, 2)),
            pltpu.SemaphoreType.DMA((count, 2)),
        ],
        cost_estimate=pl.CostEstimate(
            flops=0, transcendentals=0, bytes_accessed=20 * sum(a * b for a, b in shapes)
        ),
        compiler_params=pltpu.CompilerParams(collective_id=number, has_side_effects=True),
    )(*arrays)


def product_sum_kernel(left_ref, right_ref, out_ref, own, made, first, passed, last, send, receive):
    here, along_x, along_y, far = shard_places()
    rows, wide = out_ref.shape
    half = wide // 2
    sides = (pl.ds(0, half), pl.ds(half, half))
    ways = ((along_x, along_y), (along_y, along_x))

    def product(place, side):
        columns = pl.ds(pl.multiple_of(place * rows, LANES), rows)
        return over_rows(left_ref[:, columns], right_ref[:, sides[side]])

    greet(along_x, along_y)
    copies = []

    def push(source, target, slot, place):
        copies.append(to_shard(source, target, send.at[slot], receive.at[slot], place))
        copies[-1].start()

    for side in range(2):
        made[0, side] = product(far, side).astype(jnp.bfloat16)
        push(made.at[0, side], passed.at[side], side, ways[side][0])
    for side in range(2):
        made[1, side] = product(ways[side][0], side).astype(jnp.bfloat16)
        push(made.at[1, side], first.at[side], 2 + side, ways[side][0])
    for side in range(2):
        kept = product(ways[side][1], side)
        copies[side].wait_recv()
        made[2, side] = (kept + passed[side].astype(jnp.float32)).astype(jnp.bfloat16)
        push(made.at[2, side], last.at[side], 4 + side, ways[side][1])
    for side in range(2):
        own[:, sides[side]] = product(here, side)
    for side in range(2):
        copies[2 + side].wait_recv()
        own[:, sides[side]] += first[side].astype(jnp.float32)
    for side in range(2):
        copies[4 + side].wait_recv()
        out_ref[:, sides[side]] = (own[:, sides[side]] + last[side].astype(jnp.float32)).astype(
            jnp.bfloat16
        )
    for copy in copies:
        copy.wait_send()


def product_sum(left, right, number):
    rows, wide = left.shape[1] // 4, right.shape[1]
    return pl.pallas_call(
        product_sum_kernel,
        in_specs=[pl.BlockSpec(memory_space=pltpu.VMEM)] * 2,
        out_specs=pl.BlockSpec(memory_space=pltpu.VMEM),
        out_shape=jax.ShapeDtypeStruct((rows, wide), jnp.bfloat16),
        scratch_shapes=[
            pltpu.VMEM((rows, wide), jnp.float32),
            pltpu.VMEM((3, 2, rows, wide // 2), jnp.bfloat16),
            pltpu.VMEM((2, rows, wide // 2), jnp.bfloat16),
            pltpu.VMEM((2, rows, wide // 2), jnp.bfloat16),
            pltpu.VMEM((2, rows, wide // 2), jnp.bfloat16),
            pltpu.SemaphoreType.DMA((6,)),
            pltpu.SemaphoreType.DMA((6,)),
        ],
        cost_estimate=pl.CostEstimate(
            flops=2 * left.shape[0] * left.shape[1] * wide,
            transcendentals=0,
            bytes_accessed=200 * rows * wide,
        ),
        compiler_params=pltpu.CompilerParams(
            collective_id=number, has_side_effects=True, vmem_limit_bytes=VMEM_LIMIT
        ),
    )(left, right)


def masked_weights(q, k, mask):
    scores = lax.dot_general(q, k, (((1,), (1,)), ((), ())), preferred_element_type=jnp.float32)
    scores = jnp.where(mask > 0.0, scores, NEG)
    raised = jnp.exp(scores - jnp.max(scores, axis=1, keepdims=True))
    return raised / jnp.sum(raised, axis=1, keepdims=True)


def mix_kernel(mask_ref, q_ref, k_ref, v_ref, out_ref):
    weights = masked_weights(q_ref[...], k_ref[...], mask_ref[...])
    out_ref[...] = jnp.dot(
        weights.astype(jnp.bfloat16), v_ref[...], preferred_element_type=jnp.float32
    ).astype(jnp.bfloat16)


def mix(mask, queries, keys, values):
    rows, width = queries.shape
    slots = keys.shape[0]
    whole = lambda h: (0, 0)
    part = lambda h: (0, h)
    return pl.pallas_call(
        mix_kernel,
        grid=(width // DH,),
        in_specs=[
            pl.BlockSpec((rows, slots), whole),
            pl.BlockSpec((rows, DH), part),
            pl.BlockSpec((slots, DH), whole),
            pl.BlockSpec((slots, DH), whole),
        ],
        out_specs=pl.BlockSpec((rows, DH), part),
        out_shape=jax.ShapeDtypeStruct((rows, width), jnp.bfloat16),
        compiler_params=pltpu.CompilerParams(vmem_limit_bytes=VMEM_LIMIT),
    )(mask, queries, keys, values)


def mix_back_kernel(mask_ref, q_ref, k_ref, v_ref, g_ref, dq_ref, dk_ref, dv_ref):
    q, k, g = q_ref[...], k_ref[...], g_ref[...]
    weights = masked_weights(q, k, mask_ref[...])
    value_score = against(g, v_ref[...])
    delta = jnp.sum(weights * value_score, axis=1, keepdims=True)
    score_back = (weights * (value_score - delta)).astype(jnp.bfloat16)
    dq_ref[...] = jnp.dot(score_back, k, preferred_element_type=jnp.float32)
    key_piece = over_rows(score_back, q)
    value_piece = over_rows(weights.astype(jnp.bfloat16), g)

    @pl.when(pl.program_id(0) == 0)
    def _():
        dk_ref[...] = key_piece
        dv_ref[...] = value_piece

    @pl.when(pl.program_id(0) > 0)
    def _():
        dk_ref[...] += key_piece
        dv_ref[...] += value_piece


def mix_back(mask, queries, keys, values, grad):
    rows, width = queries.shape
    slots = keys.shape[0]
    whole = lambda h: (0, 0)
    part = lambda h: (0, h)
    return pl.pallas_call(
        mix_back_kernel,
        grid=(width // DH,),
        in_specs=[
            pl.BlockSpec((rows, slots), whole),
            pl.BlockSpec((rows, DH), part),
            pl.BlockSpec((slots, DH), whole),
            pl.BlockSpec((slots, DH), whole),
            pl.BlockSpec((rows, DH), part),
        ],
        out_specs=[
            pl.BlockSpec((rows, DH), part),
            pl.BlockSpec((slots, DH), whole),
            pl.BlockSpec((slots, DH), whole),
        ],
        out_shape=[
            jax.ShapeDtypeStruct((rows, width), jnp.float32),
            jax.ShapeDtypeStruct((slots, DH), jnp.float32),
            jax.ShapeDtypeStruct((slots, DH), jnp.float32),
        ],
        compiler_params=pltpu.CompilerParams(vmem_limit_bytes=VMEM_LIMIT),
    )(mask, queries, keys, values, grad)


def feed_kernel(feed_ref, grad_ref, gate_ref, up_ref, down_ref, bias_gate_ref, bias_up_ref, live_ref,
                hidden_ref, gate_back_ref, up_back_ref, gate_sum_ref, up_sum_ref):
    rows = feed_ref.shape[0]
    step = min(rows, 256)

    @pl.when(pl.program_id(1) == 0)
    def _():
        gate_sum_ref[...] = jnp.zeros_like(gate_sum_ref)
        up_sum_ref[...] = jnp.zeros_like(up_sum_ref)

    def part(i, carry):
        at = pl.ds(pl.multiple_of(i * step, step), step)
        feed = feed_ref[at, :]
        gate = jnp.dot(feed, gate_ref[...], preferred_element_type=jnp.float32) + bias_gate_ref[...]
        up = jnp.dot(feed, up_ref[...], preferred_element_type=jnp.float32) + bias_up_ref[...]
        back = against(grad_ref[at, :], down_ref[...])
        live = live_ref[...]
        square = gate * gate
        bend = jnp.tanh(GELU * gate * (1.0 + CUBE * square))
        half = 0.5 * (1.0 + bend)
        gelu = gate * half * live
        slope = half + 0.5 * gate * (1.0 - bend * bend) * (GELU * (1.0 + 3.0 * CUBE * square))
        hidden_ref[at, :] = (gelu * up).astype(jnp.bfloat16)
        gate_back = (back * up * slope * live).astype(jnp.bfloat16)
        up_back = (back * gelu).astype(jnp.bfloat16)
        gate_back_ref[at, :] = gate_back
        up_back_ref[at, :] = up_back
        gate_sum_ref[...] += jnp.sum(gate_back.astype(jnp.float32), axis=0, keepdims=True)
        up_sum_ref[...] += jnp.sum(up_back.astype(jnp.float32), axis=0, keepdims=True)
        return carry

    lax.fori_loop(0, rows // step, part, 0)


def feed(feed_group, grad_group, gate_up, down, bias, live):
    rows, model = feed_group.shape
    units = down.shape[0]
    wide = min(units, 256)
    blocks = units // wide
    tall = min(rows, 1024)
    buffers = {"pipeline_mode": pl.Buffered(1)} if tall == rows else {}
    tokens = lambda j, i: (i, 0)
    column = lambda j, i: (0, j)
    later = lambda j, i: (0, j + blocks)
    made = lambda j, i: (i, j)
    return pl.pallas_call(
        feed_kernel,
        grid=(blocks, rows // tall),
        in_specs=[
            pl.BlockSpec((tall, model), tokens, **buffers),
            pl.BlockSpec((tall, model), tokens, **buffers),
            pl.BlockSpec((model, wide), column),
            pl.BlockSpec((model, wide), later),
            pl.BlockSpec((wide, model), lambda j, i: (j, 0)),
            pl.BlockSpec((1, wide), column),
            pl.BlockSpec((1, wide), later),
            pl.BlockSpec((1, wide), column),
        ],
        out_specs=[
            pl.BlockSpec((tall, wide), made),
            pl.BlockSpec((tall, wide), made),
            pl.BlockSpec((tall, wide), made),
            pl.BlockSpec((1, wide), column),
            pl.BlockSpec((1, wide), column),
        ],
        out_shape=[
            jax.ShapeDtypeStruct((rows, units), jnp.bfloat16),
            jax.ShapeDtypeStruct((rows, units), jnp.bfloat16),
            jax.ShapeDtypeStruct((rows, units), jnp.bfloat16),
            jax.ShapeDtypeStruct((1, units), jnp.float32),
            jax.ShapeDtypeStruct((1, units), jnp.float32),
        ],
        compiler_params=pltpu.CompilerParams(vmem_limit_bytes=VMEM_LIMIT),
    )(feed_group, grad_group, gate_up, gate_up, down, bias, bias, live)


def body(
    inputs,
    doc_ids,
    cotangent,
    attn_gain,
    query_weight,
    keyval_weight,
    output_weight,
    output_bias,
    feed_gain,
    gate_up_weight,
    gate_up_bias,
    down_weight,
    down_bias,
):
    tok, model = inputs.shape
    shards, contexts = lax.axis_size("shard"), lax.axis_size("context")
    shard, place = lax.axis_index("shard"), lax.axis_index("context")
    core, chip = place % 2, place // 2
    group = tok * contexts
    owned = model // (shards * contexts)
    ff = gate_up_weight.shape[1] // 2
    width, per_shard = unit_tiles(ff, shards, contexts)
    unit_start = jnp.minimum(place * width, per_shard - width)
    units = shards * width * LANES

    vectors = jnp.concatenate([attn_gain, output_bias, feed_gain, down_bias, gate_up_bias])
    vectors = vector_gather(vectors, shard).astype(jnp.float32)
    gain_one, bias_out, gain_two, bias_down = (
        vectors[:, i * (model // shards) : (i + 1) * (model // shards)].reshape(1, model)
        for i in range(4)
    )
    bias_gate_up = vectors[:, 4 * (model // shards) :].reshape(2 * shards, per_shard * LANES)
    bias_gate_up = lax.dynamic_slice_in_dim(
        bias_gate_up, unit_start * LANES, width * LANES, 1
    ).reshape(1, 2 * units)
    shard_rows = model // shards
    core_cols, core_heads = keyval_weight.shape[1] // 2, query_weight.shape[1] // 2

    def cut_of(wide):
        def pieces():
            column = lax.rem(lax.axis_index("context"), 2) * wide
            return [(0, pl.multiple_of(column, LANES), wide, 0)]

        return shard_rows, pieces

    block = width * LANES

    def first_unit():
        return jnp.minimum(lax.axis_index("context") * width, per_shard - width) * LANES

    def gate_up_pieces():
        return [
            (0, pl.multiple_of(j * per_shard * LANES + first_unit(), LANES), block, j * block)
            for j in range(2 * shards)
        ]

    def down_pieces():
        return [(pl.multiple_of(first_unit(), LANES), 0, model, 0)]

    keyval_half, query_half = gather_cuts(
        (after(keyval_weight, vectors), query_weight),
        (cut_of(core_cols), cut_of(core_heads)),
        ((model, core_cols), (model, core_heads)),
        0,
    )
    output_half = shard_gather(
        after(halves(output_weight, core, 1)[0], keyval_half, query_half), shard
    )
    unit_at = unit_start * LANES + jnp.arange(width * LANES, dtype=jnp.int32)
    unit_live = jnp.tile(unit_at >= place * width * LANES, shards)[None, :].astype(jnp.float32)

    source = inputs.astype(jnp.float32)
    attn_in = rms_norm(source, gain_one).astype(jnp.bfloat16)
    attn_pair = pair_rows(attn_in, core)
    slots = jnp.arange(group, dtype=jnp.int32)
    pair_slots = chip * (2 * tok) + jnp.arange(2 * tok, dtype=jnp.int32)
    pair_docs = lax.dynamic_slice_in_dim(doc_ids, chip * (2 * tok), 2 * tok)
    distance = pair_slots[:, None] - slots[None, :]
    mask = (
        (pair_docs[:, None] == doc_ids[None, :]) & (distance >= 0) & (distance < WINDOW)
    ).astype(jnp.float32)
    angles = pair_slots.astype(jnp.float32)[:, None] * frequencies(DH)[None, :]
    cosine, sine = jnp.cos(angles), jnp.sin(angles)
    keyval_raw = jnp.dot(attn_pair, keyval_half, preferred_element_type=jnp.float32)
    keyval = jnp.where(core == 0, rotate(keyval_raw, cosine, sine), keyval_raw).astype(jnp.bfloat16)
    grad_group = gather(cotangent, "context")
    keyval = gather(after(keyval, grad_group), "context").reshape(contexts // 2, 2, 2 * tok, DH)
    keys, values = keyval[:, 0].reshape(group, DH), keyval[:, 1].reshape(group, DH)
    query_raw = jnp.dot(attn_pair, query_half, preferred_element_type=jnp.float32)
    heads = query_raw.shape[1] // DH
    queries = (
        (
            rotate(query_raw.reshape(2 * tok, heads, DH), cosine[:, None, :], sine[:, None, :])
            * DH ** (-0.5)
        )
        .astype(jnp.bfloat16)
        .reshape(2 * tok, heads * DH)
    )
    mixed_half = mix(mask, queries, keys, values)
    mixed_own = swap_rows(mixed_half, core)
    mixed_pair = pair_rows(mixed_own, core)
    attn_out = swap_rows(
        jnp.dot(mixed_pair, output_half, preferred_element_type=jnp.float32), core
    )
    resid = source + attn_out + bias_out

    feed_in = rms_norm(resid, gain_two).astype(jnp.bfloat16)
    mixed_group = gather(mixed_own, "context")
    feed_group = gather(feed_in, "context")
    gate_up_part, down_part = gather_cuts(
        (gate_up_weight, after(down_weight, feed_in)),
        ((shard_rows, gate_up_pieces), (block, down_pieces)),
        ((model, 2 * units), (units, model)),
        1,
    )
    hidden, gate_back, up_back, gate_sums, up_sums = feed(
        feed_group, grad_group, gate_up_part, down_part, bias_gate_up, unit_live
    )
    gate_up_low = jnp.concatenate([gate_back, up_back], axis=1)
    feed_part = against(gate_up_low, gate_up_part).astype(jnp.bfloat16)
    feed_in_grad = lax.psum_scatter(feed_part, "context", scatter_dimension=0, tiled=True)
    down_sum = product_sum(grad_group, after(hidden, feed_part), 2)
    feed_in_grad = after(feed_in_grad, down_sum).astype(jnp.float32)

    grad_out = cotangent.astype(jnp.float32)
    resid_part, gain_two_grad = jax.vjp(rms_norm, resid, gain_two)[1](feed_in_grad)
    resid_grad = grad_out + resid_part
    attn_grad_low = resid_grad.astype(jnp.bfloat16)
    mixed_back = summed_half(
        against(swap_columns(attn_grad_low, core), output_half), core, 1
    ).astype(jnp.bfloat16)
    query_acc, key_acc, value_acc = mix_back(mask, queries, keys, values, mixed_back)
    keyval_acc = jnp.stack(
        [key_acc.reshape(contexts // 2, 2 * tok, DH), value_acc.reshape(contexts // 2, 2 * tok, DH)],
        axis=1,
    ).reshape(2 * group, DH)
    down_part_out = jnp.dot(
        after(hidden, keyval_acc), down_part, preferred_element_type=jnp.float32
    ).astype(jnp.bfloat16)
    gate_sum = product_sum(feed_group, after(gate_back, keyval_acc), 2)
    keyval_acc = lax.psum_scatter(keyval_acc, "context", scatter_dimension=0, tiled=True)
    keyval_acc = after(keyval_acc, gate_sum, down_part_out)
    down_out = lax.psum_scatter(
        after(down_part_out, keyval_acc), "context", scatter_dimension=0, tiled=True
    ).astype(jnp.float32)
    block_out = (resid + down_out + bias_down).astype(jnp.bfloat16)
    keyval_back = jnp.where(core == 0, rotate(keyval_acc, cosine, -sine), keyval_acc).astype(
        jnp.bfloat16
    )
    query_back = (
        rotate(query_acc.reshape(2 * tok, heads, DH), cosine[:, None, :], -sine[:, None, :])
        * DH ** (-0.5)
    ).reshape(2 * tok, heads * DH).astype(jnp.bfloat16)
    attn_in_grad = summed_half(
        against(query_back, query_half) + against(keyval_back, keyval_half), core, 0
    )
    input_part, gain_one_grad = jax.vjp(rms_norm, source, gain_one)[1](attn_in_grad)
    input_grad = resid_grad + input_part

    def to_owners(field):
        return lax.all_to_all(
            field.reshape(contexts, owned, field.shape[1]), "context", split_axis=0, concat_axis=0
        ).astype(jnp.float32)

    def whole_units(field):
        return join_units(to_owners(field), 1, shards, width, per_shard)

    down_weight_grad = whole_units(down_sum).T

    def token_rows(field):
        return lax.all_to_all(
            regroup(field, shards, contexts), "context", split_axis=1, concat_axis=0, tiled=True
        )

    back_own = jnp.concatenate(
        [swap_rows(query_back, core), swap_rows(keyval_back, core)], axis=1
    )
    back_group = gather(back_own, "context")
    up_sum = product_sum(feed_group, after(up_back, back_own), 2)
    back_group = after(back_group, up_sum)
    gate_up_grad = jnp.concatenate([whole_units(gate_sum), whole_units(up_sum)], axis=1)
    attn_rows, attn_grad_rows = token_rows(attn_in), token_rows(attn_grad_low)
    attn_sum = jnp.concatenate(
        [
            shard_sum(over_shard_rows(attn_rows, back_group, shard)),
            shard_sum(over_shard_rows(attn_grad_rows, mixed_group, shard)),
        ],
        axis=1,
    )
    head_cols = HEADS * DH
    query_grad = attn_sum[:, :head_cols]
    keyval_grad = attn_sum[:, head_cols : head_cols + 2 * DH]
    output_weight_grad = attn_sum[:, head_cols + 2 * DH :].T

    sums = jnp.concatenate(
        [
            gain_one_grad.reshape(model),
            jnp.sum(attn_grad_low.astype(jnp.float32), axis=0),
            gain_two_grad.reshape(model),
            jnp.sum(grad_out, axis=0),
            gate_sums.reshape(units),
            up_sums.reshape(units),
        ]
    )
    sums = sums + across(sums, 1)
    sums = sums + across(sums, 2)
    sums = gather(sums[None], "context")
    device = shard * contexts + place
    own = [
        jnp.sum(
            lax.dynamic_slice_in_dim(sums[:, i * model : (i + 1) * model], device * owned, owned, 1),
            axis=0,
        )
        for i in range(4)
    ]
    unit_sums = join_units(sums[:, 4 * model :], 2, shards, width, per_shard)
    unit_owned = 2 * ff // (shards * contexts)
    gate_up_bias_grad = lax.dynamic_slice_in_dim(unit_sums, device * unit_owned, unit_owned)
    return (
        block_out,
        input_grad,
        own[0],
        query_grad,
        keyval_grad,
        output_weight_grad,
        own[1],
        own[2],
        gate_up_grad,
        gate_up_bias_grad,
        down_weight_grad,
        own[3],
    )


def solution(mesh):
    placed = (
        P(("shard", "context"), None),
        P("shard"),
        P(("shard", "context"), None),
        P("shard"),
        P("shard", None),
        P("shard", None),
        P("shard", None),
        P("shard"),
        P("shard"),
        P("shard", None),
        P("shard"),
        P("shard", None),
        P("shard"),
    )
    return jax.shard_map(
        body,
        mesh=mesh,
        in_specs=placed,
        out_specs=(
            P(("shard", "context"), None),
            P(("shard", "context"), None),
            P(("shard", "context")),
            P(("shard", "context"), None),
            P(("shard", "context"), None),
            P(None, ("shard", "context")),
            P(("shard", "context")),
            P(("shard", "context")),
            P(("shard", "context"), None),
            P(("shard", "context")),
            P(None, ("shard", "context")),
            P(("shard", "context")),
        ),
        check_vma=False,
    )
```

```python
import functools
import math

import jax
import jax.numpy as jnp
from jax import lax
from jax.experimental import pallas as pl
from jax.experimental.pallas import tpu as pltpu
from jax.sharding import PartitionSpec as P

HEADS = 10
DH = 256
FF = 7680
WINDOW = 2048


EPS = 1e-06
NEG = -1e30
ROPE_LOG = math.log(10000.0)


def frequencies(head_dim):
    quarter = head_dim // 4
    steps = jnp.arange(quarter).astype(jnp.float32)
    return jnp.exp(-ROPE_LOG * (2.0 * steps) / (head_dim // 2))


def rotate(field, cosine, sine):
    width = field.shape[-1] // 2
    quarter = width // 2
    first = field[..., :quarter]
    second = field[..., quarter:width]
    return jnp.concatenate(
        [first * cosine - second * sine, second * cosine + first * sine, field[..., width:]],
        axis=-1,
    )


def rms_norm(field, gain):
    return field * lax.rsqrt(jnp.mean(field * field, axis=-1, keepdims=True) + EPS) * gain


def geglu(gate_up):
    half = gate_up.shape[-1] // 2
    return jax.nn.gelu(gate_up[:, :half], approximate=True) * gate_up[:, half:]


def over_rows(left, right):
    return lax.dot_general(
        left, right, (((0,), (0,)), ((), ())), preferred_element_type=jnp.float32
    )


def against(left, weight):
    return lax.dot_general(
        left, weight, (((1,), (1,)), ((), ())), preferred_element_type=jnp.float32
    )


VMEM_LIMIT = 56 * 1024 * 1024
LANES = 128
MESH = pl.DeviceIdType.MESH
GELU = 0.7978845608028654
CUBE = 0.044715


def gather(value, axis):
    return lax.all_gather(value, axis, axis=0, tiled=True)


def across(value, bit):
    count = lax.axis_size("shard")
    return lax.ppermute(value, "shard", [(i, i ^ bit) for i in range(count)])


def shard_gather(block, shard):
    rows = block.shape[0]
    near, next_near = across(block, 1), across(block, 2)
    far = jnp.concatenate(
        [across(next_near[: rows // 2], 1), across(near[rows // 2 :], 2)], axis=0
    )
    whole = jnp.zeros((4 * rows, block.shape[1]), block.dtype)
    for bits, part in enumerate((block, near, next_near, far)):
        whole = lax.dynamic_update_slice_in_dim(whole, part, (shard ^ bits) * rows, 0)
    return whole


def vector_gather(own, shard):
    near, next_near = across(own, 1), across(own, 2)
    far = across(near, 2)
    found = jnp.stack([own, near, next_near, far])
    return jnp.stack([lax.dynamic_index_in_dim(found, shard ^ j, 0, False) for j in range(4)])


def after(value, *earlier):
    return lax.optimization_barrier((value, *earlier))[0]


def sibling(value):
    count = lax.axis_size("context")
    return lax.ppermute(value, "context", [(i, i ^ 1) for i in range(count)])


def pair_rows(own, core):
    other = sibling(own)
    return jnp.where(
        core == 0, jnp.concatenate([own, other], axis=0), jnp.concatenate([other, own], axis=0)
    )


def halves(value, core, axis):
    low, high = jnp.split(value, 2, axis=axis)
    return jnp.where(core == 0, low, high), jnp.where(core == 0, high, low)


def swap_rows(value, core):
    mine, theirs = halves(value, core, 0)
    other = sibling(theirs)
    return jnp.where(
        core == 0, jnp.concatenate([mine, other], axis=1), jnp.concatenate([other, mine], axis=1)
    )


def swap_columns(own, core):
    mine, theirs = halves(own, core, 1)
    other = sibling(theirs)
    return jnp.where(
        core == 0, jnp.concatenate([mine, other], axis=0), jnp.concatenate([other, mine], axis=0)
    )


def summed_half(value, core, axis):
    mine, theirs = halves(value, core, axis)
    return mine + sibling(theirs)


def unit_tiles(ff, shards, contexts):
    per_shard = ff // shards // LANES
    return -(-per_shard // contexts), per_shard


def join_units(pieces, parts, shards, width, per_shard):
    contexts, inner = pieces.shape[0], pieces.shape[1:-1]
    field = pieces.reshape(contexts, *inner, parts, shards, width * LANES)
    kept = []
    for at in range(contexts):
        first = at * width
        if first >= per_shard:
            continue
        start = min(first, per_shard - width)
        stop = min(first + width, per_shard)
        kept.append(field[at, ..., (first - start) * LANES : (stop - start) * LANES])
    return jnp.concatenate(kept, axis=-1).reshape(*inner, parts * shards * per_shard * LANES)


def unit_pieces(contexts, shards, width, per_shard):
    found = []
    for at in range(contexts):
        first = at * width
        if first >= per_shard:
            continue
        start, stop = min(first, per_shard - width), min(first + width, per_shard)
        for shard in range(shards):
            found.append(
                (
                    at,
                    (shard * width + first - start) * LANES,
                    (stop - first) * LANES,
                    (shard * per_shard + first) * LANES,
                )
            )
    return found


def lay_kernel(pieces, *refs):
    *sources, out_ref = refs
    units = out_ref.shape[1] // len(sources)
    for part, source in enumerate(sources):
        for at, column, wide, first in pieces:
            out_ref[:, part * units + first : part * units + first + wide] = source[
                at, :, column : column + wide
            ].astype(jnp.float32)


def lay_kernel_turned(pieces, source, out_ref):
    for at, column, wide, first in pieces:
        out_ref[first : first + wide, :] = source[at, :, column : column + wide].astype(jnp.float32).T


def lay(fields, pieces, units, turned=False):
    rows = fields[0].shape[1]
    shape = (units, rows) if turned else (rows, len(fields) * units)
    return pl.pallas_call(
        functools.partial(lay_kernel_turned if turned else lay_kernel, pieces),
        in_specs=[pl.BlockSpec(memory_space=pltpu.VMEM)] * len(fields),
        out_specs=pl.BlockSpec(memory_space=pltpu.VMEM),
        out_shape=jax.ShapeDtypeStruct(shape, jnp.float32),
        compiler_params=pltpu.CompilerParams(vmem_limit_bytes=VMEM_LIMIT),
    )(*fields)


def shard_places():
    here = lax.axis_index("shard")
    return here, here + 1 - 2 * lax.rem(here, 2), lax.rem(here + 2, 4), 3 - here


def greet(shards, contexts=()):
    barrier = pltpu.get_barrier_semaphore()
    for axis, places in (("shard", shards), ("context", contexts)):
        for place in places:
            pl.semaphore_signal(barrier, 1, device_id={axis: place}, device_id_type=MESH)
    pl.semaphore_wait(barrier, len(shards) + len(contexts))


def to_device(axis, source, target, send, receive, place):
    return pltpu.make_async_remote_copy(
        src_ref=source,
        dst_ref=target,
        send_sem=send,
        recv_sem=receive,
        device_id={axis: place},
        device_id_type=MESH,
    )


def gather_kernel(cuts, *refs):
    count = len(cuts)
    sources, wholes = refs[:count], refs[count : 2 * count]
    send, receive, local, send_on, receive_on = refs[2 * count :]
    here, along_x, along_y, far = shard_places()
    greet((along_x, along_y))

    def block(i, place, start, rows):
        return pl.ds(pl.multiple_of(place * cuts[i][0] + start, 16), rows)

    kept, sent = [], []
    for i, (rows, pieces) in enumerate(cuts):
        for j, (row, column, wide, into) in enumerate(pieces()):
            piece = sources[i].at[pl.ds(row, rows), pl.ds(column, wide)]
            target = wholes[i].at[block(i, here, 0, rows), pl.ds(into, wide)]
            kept.append(pltpu.make_async_copy(piece, target, local.at[i, j]))
            kept[-1].start()
            for hop, place in enumerate((along_x, along_y)):
                sent.append(to_device("shard", piece, target, send.at[i, j, hop], receive.at[i, j, hop], place))
                sent[-1].start()
    for i, (rows, pieces) in enumerate(cuts):
        half = rows // 2
        for j, (row, column, wide, into) in enumerate(pieces()):
            for hop, place in enumerate((along_x, along_y)):
                came = wholes[i].at[block(i, place, 0, rows), pl.ds(into, wide)]
                to_device("shard", came, came, send.at[i, j, hop], receive.at[i, j, hop], place).wait_recv()
        for hop, (place, owner, start) in enumerate(((along_x, along_y, 0), (along_y, along_x, half))):
            part = wholes[i].at[block(i, owner, start, half)]
            sent.append(to_device("shard", part, part, send_on.at[i, hop], receive_on.at[i, hop], place))
            sent[-1].start()
    for i, (rows, pieces) in enumerate(cuts):
        half = rows // 2
        for hop, (place, start) in enumerate(((along_x, 0), (along_y, half))):
            came = wholes[i].at[block(i, far, start, half)]
            to_device("shard", came, came, send_on.at[i, hop], receive_on.at[i, hop], place).wait_recv()
    for copy in kept:
        copy.wait()
    for copy in sent:
        copy.wait_send()


def gather_cuts(arrays, cuts, shapes, number):
    count = len(arrays)
    most = 8
    return pl.pallas_call(
        functools.partial(gather_kernel, cuts),
        in_specs=[pl.BlockSpec(memory_space=pl.ANY)] * count,
        out_specs=[pl.BlockSpec(memory_space=pl.ANY)] * count,
        out_shape=[jax.ShapeDtypeStruct(shape, jnp.bfloat16) for shape in shapes],
        scratch_shapes=[
            pltpu.SemaphoreType.DMA((count, most, 2)),
            pltpu.SemaphoreType.DMA((count, most, 2)),
            pltpu.SemaphoreType.DMA((count, most)),
            pltpu.SemaphoreType.DMA((count, 2)),
            pltpu.SemaphoreType.DMA((count, 2)),
        ],
        cost_estimate=pl.CostEstimate(
            flops=0, transcendentals=0, bytes_accessed=20 * sum(a * b for a, b in shapes)
        ),
        compiler_params=pltpu.CompilerParams(collective_id=number, has_side_effects=True),
    )(*arrays)


class Product:
    def __init__(self, left, right):
        self.rows, self.wide = left[1] // 4, right[1]
        half = -(-self.wide // (2 * LANES)) * LANES
        self.sides = ((0, half), (half, self.wide - half))

    def scratch(self):
        shapes = [pltpu.VMEM((self.rows, self.wide), jnp.float32)]
        for _, wide in self.sides:
            shapes += [pltpu.VMEM((3, self.rows, wide), jnp.bfloat16)] * 2
        return shapes + [pltpu.SemaphoreType.DMA((6,)), pltpu.SemaphoreType.DMA((6,))]

    def run(self, left, right, out, own, made_a, came_a, made_b, came_b, send, receive):
        here, along_x, along_y, far = shard_places()
        ways = ((along_x, along_y), (along_y, along_x))
        made, came = (made_a, made_b), (came_a, came_b)
        columns = [pl.ds(start, wide) for start, wide in self.sides]
        copies = []

        def product(place, side):
            block = pl.ds(pl.multiple_of(place * self.rows, LANES), self.rows)
            return over_rows(left[:, block], right[:, columns[side]])

        def push(step, side, place):
            slot = 2 * step + side
            copies.append(
                to_device(
                    "shard",
                    made[side].at[step],
                    came[side].at[step],
                    send.at[slot],
                    receive.at[slot],
                    place,
                )
            )
            copies[-1].start()

        for side in range(2):
            made[side][0] = product(far, side).astype(jnp.bfloat16)
            push(0, side, ways[side][0])
        for side in range(2):
            made[side][1] = product(ways[side][0], side).astype(jnp.bfloat16)
            push(1, side, ways[side][0])
        for side in range(2):
            kept = product(ways[side][1], side)
            copies[side].wait_recv()
            made[side][2] = (kept + came[side][0].astype(jnp.float32)).astype(jnp.bfloat16)
            push(2, side, ways[side][1])
        for side in range(2):
            own[:, columns[side]] = product(here, side)
        for side in range(2):
            copies[2 + side].wait_recv()
            own[:, columns[side]] += came[side][1].astype(jnp.float32)
        for side in range(2):
            copies[4 + side].wait_recv()
            out[:, columns[side]] = (own[:, columns[side]] + came[side][2].astype(jnp.float32)).astype(
                jnp.bfloat16
            )
        return copies


class Exchange:
    def __init__(self, count, stride):
        self.count, self.stride = count, stride

    def scratch(self):
        return [pltpu.SemaphoreType.DMA((self.count,))] * 2 + [pltpu.SemaphoreType.DMA]

    def peers(self):
        me = lax.axis_index("context")
        slot, rest = me // self.stride, lax.rem(me, self.stride)
        places = [lax.rem(slot + k, self.count) for k in range(self.count)]
        return places, [place * self.stride + rest for place in places]

    def start(self, blocks, out, send, receive, local):
        slots, devices = self.peers()
        kept = pltpu.make_async_copy(blocks(slots[0]), out.at[slots[0]], local)
        kept.start()
        copies = []
        for k in range(1, self.count):
            copies.append(
                to_device(
                    "context", blocks(slots[k]), out.at[slots[0]], send.at[k], receive.at[k], devices[k]
                )
            )
            copies[-1].start()

        def finish():
            kept.wait()
            for k in range(1, self.count):
                source = slots[self.count - k]
                to_device(
                    "context", out.at[source], out.at[source], send.at[k], receive.at[k], devices[k]
                ).wait_recv()
            for copy in copies:
                copy.wait_send()

        return finish


def work_kernel(products, exchanges, chained, *refs):
    refs = list(refs)

    def take(count):
        taken = refs[:count]
        del refs[:count]
        return taken

    operands = [take(2) for _ in products]
    arrays = take(len(exchanges) - (1 if chained else 0))
    results = take(len(products))
    moved = take(len(exchanges))
    product_scratch = [take(len(p.scratch())) for p in products]
    exchange_scratch = [take(len(e.scratch())) for e in exchanges]
    _, along_x, along_y, _ = shard_places()
    everyone = max(exchanges, key=lambda e: e.count).peers()[1][1:] if exchanges else []
    greet((along_x, along_y), everyone)
    finishes, copies = [], []
    for exchange, array, out, scratch in zip(exchanges, arrays, moved, exchange_scratch):
        finishes.append(exchange.start(lambda j, array=array: array.at[j], out, *scratch))
    for product, (left, right), out, scratch in zip(products, operands, results, product_scratch):
        copies += product.run(left, right, out, *scratch)
    if chained:
        rows = products[0].rows // exchanges[-1].count
        finishes.append(
            exchanges[-1].start(
                lambda j: results[0].at[pl.ds(pl.multiple_of(j * rows, 16), rows)],
                moved[-1],
                *exchange_scratch[-1],
            )
        )
    for copy in copies:
        copy.wait_send()
    for finish in finishes:
        finish()


def work(number, products=(), exchanges=(), chained=False):
    contexts = lax.axis_size("context")
    made = [Product(left.shape, right.shape) for left, right in products]
    swaps = [Exchange(array.shape[0], contexts // array.shape[0]) for array in exchanges]
    results = [jax.ShapeDtypeStruct((p.rows, p.wide), jnp.bfloat16) for p in made]
    moved = [jax.ShapeDtypeStruct(array.shape, array.dtype) for array in exchanges]
    if chained:
        swaps.append(Exchange(contexts, 1))
        moved.append(
            jax.ShapeDtypeStruct((contexts, made[0].rows // contexts, made[0].wide), jnp.bfloat16)
        )
    scratch = [shape for part in made + swaps for shape in part.scratch()]
    vmem = pl.BlockSpec(memory_space=pltpu.VMEM)
    hbm = pl.BlockSpec(memory_space=pl.ANY)
    outs = pl.pallas_call(
        functools.partial(work_kernel, made, swaps, chained),
        in_specs=[vmem] * (2 * len(made)) + [hbm] * len(exchanges),
        out_specs=[vmem] * len(made) + [hbm] * len(swaps),
        out_shape=results + moved,
        scratch_shapes=scratch,
        cost_estimate=pl.CostEstimate(flops=0, transcendentals=0, bytes_accessed=150_000_000),
        compiler_params=pltpu.CompilerParams(
            collective_id=number, has_side_effects=True, vmem_limit_bytes=VMEM_LIMIT
        ),
    )(*[operand for pair in products for operand in pair], *exchanges)
    return outs[: len(made)], outs[len(made) :]


def masked_weights(q, k, mask):
    scores = lax.dot_general(q, k, (((1,), (1,)), ((), ())), preferred_element_type=jnp.float32)
    scores = jnp.where(mask > 0.0, scores, NEG)
    raised = jnp.exp(scores - jnp.max(scores, axis=1, keepdims=True))
    return raised / jnp.sum(raised, axis=1, keepdims=True)


def mix_kernel(mask_ref, q_ref, k_ref, v_ref, out_ref):
    weights = masked_weights(q_ref[...], k_ref[...], mask_ref[...])
    out_ref[...] = jnp.dot(
        weights.astype(jnp.bfloat16), v_ref[...], preferred_element_type=jnp.float32
    ).astype(jnp.bfloat16)


def mix(mask, queries, keys, values):
    rows, width = queries.shape
    slots = keys.shape[0]
    whole = lambda h: (0, 0)
    part = lambda h: (0, h)
    return pl.pallas_call(
        mix_kernel,
        grid=(width // DH,),
        in_specs=[
            pl.BlockSpec((rows, slots), whole),
            pl.BlockSpec((rows, DH), part),
            pl.BlockSpec((slots, DH), whole),
            pl.BlockSpec((slots, DH), whole),
        ],
        out_specs=pl.BlockSpec((rows, DH), part),
        out_shape=jax.ShapeDtypeStruct((rows, width), jnp.bfloat16),
        compiler_params=pltpu.CompilerParams(vmem_limit_bytes=VMEM_LIMIT),
    )(mask, queries, keys, values)


def mix_back_kernel(mask_ref, q_ref, k_ref, v_ref, g_ref, dq_ref, dk_ref, dv_ref):
    q, k, g = q_ref[...], k_ref[...], g_ref[...]
    weights = masked_weights(q, k, mask_ref[...])
    value_score = against(g, v_ref[...])
    delta = jnp.sum(weights * value_score, axis=1, keepdims=True)
    score_back = (weights * (value_score - delta)).astype(jnp.bfloat16)
    dq_ref[...] = jnp.dot(score_back, k, preferred_element_type=jnp.float32)
    key_piece = over_rows(score_back, q)
    value_piece = over_rows(weights.astype(jnp.bfloat16), g)

    @pl.when(pl.program_id(0) == 0)
    def _():
        dk_ref[...] = key_piece
        dv_ref[...] = value_piece

    @pl.when(pl.program_id(0) > 0)
    def _():
        dk_ref[...] += key_piece
        dv_ref[...] += value_piece


def mix_back(mask, queries, keys, values, grad):
    rows, width = queries.shape
    slots = keys.shape[0]
    whole = lambda h: (0, 0)
    part = lambda h: (0, h)
    return pl.pallas_call(
        mix_back_kernel,
        grid=(width // DH,),
        in_specs=[
            pl.BlockSpec((rows, slots), whole),
            pl.BlockSpec((rows, DH), part),
            pl.BlockSpec((slots, DH), whole),
            pl.BlockSpec((slots, DH), whole),
            pl.BlockSpec((rows, DH), part),
        ],
        out_specs=[
            pl.BlockSpec((rows, DH), part),
            pl.BlockSpec((slots, DH), whole),
            pl.BlockSpec((slots, DH), whole),
        ],
        out_shape=[
            jax.ShapeDtypeStruct((rows, width), jnp.float32),
            jax.ShapeDtypeStruct((slots, DH), jnp.float32),
            jax.ShapeDtypeStruct((slots, DH), jnp.float32),
        ],
        compiler_params=pltpu.CompilerParams(vmem_limit_bytes=VMEM_LIMIT),
    )(mask, queries, keys, values, grad)


def feed_kernel(feed_ref, grad_ref, gate_ref, up_ref, down_ref, bias_gate_ref, bias_up_ref, live_ref,
                hidden_ref, gate_back_ref, up_back_ref, gate_sum_ref, up_sum_ref):
    rows = feed_ref.shape[0]
    step = min(rows, 256)

    @pl.when(pl.program_id(1) == 0)
    def _():
        gate_sum_ref[...] = jnp.zeros_like(gate_sum_ref)
        up_sum_ref[...] = jnp.zeros_like(up_sum_ref)

    def part(i, carry):
        at = pl.ds(pl.multiple_of(i * step, step), step)
        feed = feed_ref[at, :]
        gate = jnp.dot(feed, gate_ref[...], preferred_element_type=jnp.float32) + bias_gate_ref[...]
        up = jnp.dot(feed, up_ref[...], preferred_element_type=jnp.float32) + bias_up_ref[...]
        back = against(grad_ref[at, :], down_ref[...])
        live = live_ref[...]
        square = gate * gate
        bend = jnp.tanh(GELU * gate * (1.0 + CUBE * square))
        half = 0.5 * (1.0 + bend)
        gelu = gate * half * live
        slope = half + 0.5 * gate * (1.0 - bend * bend) * (GELU * (1.0 + 3.0 * CUBE * square))
        hidden_ref[at, :] = (gelu * up).astype(jnp.bfloat16)
        gate_back = (back * up * slope * live).astype(jnp.bfloat16)
        up_back = (back * gelu).astype(jnp.bfloat16)
        gate_back_ref[at, :] = gate_back
        up_back_ref[at, :] = up_back
        gate_sum_ref[...] += jnp.sum(gate_back.astype(jnp.float32), axis=0, keepdims=True)
        up_sum_ref[...] += jnp.sum(up_back.astype(jnp.float32), axis=0, keepdims=True)
        return carry

    lax.fori_loop(0, rows // step, part, 0)


def feed(feed_group, grad_group, gate_up, down, bias, live):
    rows, model = feed_group.shape
    units = down.shape[0]
    wide = min(units, 256)
    blocks = units // wide
    tall = min(rows, 1024)
    buffers = {"pipeline_mode": pl.Buffered(1)} if tall == rows else {}
    tokens = lambda j, i: (i, 0)
    column = lambda j, i: (0, j)
    later = lambda j, i: (0, j + blocks)
    made = lambda j, i: (i, j)
    return pl.pallas_call(
        feed_kernel,
        grid=(blocks, rows // tall),
        in_specs=[
            pl.BlockSpec((tall, model), tokens, **buffers),
            pl.BlockSpec((tall, model), tokens, **buffers),
            pl.BlockSpec((model, wide), column),
            pl.BlockSpec((model, wide), later),
            pl.BlockSpec((wide, model), lambda j, i: (j, 0)),
            pl.BlockSpec((1, wide), column),
            pl.BlockSpec((1, wide), later),
            pl.BlockSpec((1, wide), column),
        ],
        out_specs=[
            pl.BlockSpec((tall, wide), made),
            pl.BlockSpec((tall, wide), made),
            pl.BlockSpec((tall, wide), made),
            pl.BlockSpec((1, wide), column),
            pl.BlockSpec((1, wide), column),
        ],
        out_shape=[
            jax.ShapeDtypeStruct((rows, units), jnp.bfloat16),
            jax.ShapeDtypeStruct((rows, units), jnp.bfloat16),
            jax.ShapeDtypeStruct((rows, units), jnp.bfloat16),
            jax.ShapeDtypeStruct((1, units), jnp.float32),
            jax.ShapeDtypeStruct((1, units), jnp.float32),
        ],
        compiler_params=pltpu.CompilerParams(vmem_limit_bytes=VMEM_LIMIT),
    )(feed_group, grad_group, gate_up, gate_up, down, bias, bias, live)


def body(
    inputs,
    doc_ids,
    cotangent,
    attn_gain,
    query_weight,
    keyval_weight,
    output_weight,
    output_bias,
    feed_gain,
    gate_up_weight,
    gate_up_bias,
    down_weight,
    down_bias,
):
    tok, model = inputs.shape
    shards, contexts = lax.axis_size("shard"), lax.axis_size("context")
    shard, place = lax.axis_index("shard"), lax.axis_index("context")
    core, chip = place % 2, place // 2
    group = tok * contexts
    owned = model // (shards * contexts)
    ff = gate_up_weight.shape[1] // 2
    width, per_shard = unit_tiles(ff, shards, contexts)
    unit_start = jnp.minimum(place * width, per_shard - width)
    units = shards * width * LANES

    vectors = jnp.concatenate([attn_gain, output_bias, feed_gain, down_bias, gate_up_bias])
    vectors = vector_gather(vectors, shard).astype(jnp.float32)
    gain_one, bias_out, gain_two, bias_down = (
        vectors[:, i * (model // shards) : (i + 1) * (model // shards)].reshape(1, model)
        for i in range(4)
    )
    bias_gate_up = vectors[:, 4 * (model // shards) :].reshape(2 * shards, per_shard * LANES)
    bias_gate_up = lax.dynamic_slice_in_dim(
        bias_gate_up, unit_start * LANES, width * LANES, 1
    ).reshape(1, 2 * units)
    shard_rows = model // shards
    core_cols, core_heads = keyval_weight.shape[1] // 2, query_weight.shape[1] // 2

    def cut_of(wide):
        def pieces():
            column = lax.rem(lax.axis_index("context"), 2) * wide
            return [(0, pl.multiple_of(column, LANES), wide, 0)]

        return shard_rows, pieces

    block = width * LANES

    def first_unit():
        return jnp.minimum(lax.axis_index("context") * width, per_shard - width) * LANES

    def gate_up_pieces():
        return [
            (0, pl.multiple_of(j * per_shard * LANES + first_unit(), LANES), block, j * block)
            for j in range(2 * shards)
        ]

    def down_pieces():
        return [(pl.multiple_of(first_unit(), LANES), 0, model, 0)]

    keyval_half, query_half = gather_cuts(
        (after(keyval_weight, vectors), query_weight),
        (cut_of(core_cols), cut_of(core_heads)),
        ((model, core_cols), (model, core_heads)),
        0,
    )
    output_half = shard_gather(
        after(halves(output_weight, core, 1)[0], keyval_half, query_half), shard
    )
    unit_at = unit_start * LANES + jnp.arange(width * LANES, dtype=jnp.int32)
    unit_live = jnp.tile(unit_at >= place * width * LANES, shards)[None, :].astype(jnp.float32)

    source = inputs.astype(jnp.float32)
    attn_in = rms_norm(source, gain_one).astype(jnp.bfloat16)
    attn_pair = pair_rows(attn_in, core)
    slots = jnp.arange(group, dtype=jnp.int32)
    pair_slots = chip * (2 * tok) + jnp.arange(2 * tok, dtype=jnp.int32)
    pair_docs = lax.dynamic_slice_in_dim(doc_ids, chip * (2 * tok), 2 * tok)
    distance = pair_slots[:, None] - slots[None, :]
    mask = (
        (pair_docs[:, None] == doc_ids[None, :]) & (distance >= 0) & (distance < WINDOW)
    ).astype(jnp.float32)
    angles = pair_slots.astype(jnp.float32)[:, None] * frequencies(DH)[None, :]
    cosine, sine = jnp.cos(angles), jnp.sin(angles)
    keyval_raw = jnp.dot(attn_pair, keyval_half, preferred_element_type=jnp.float32)
    keyval = jnp.where(core == 0, rotate(keyval_raw, cosine, sine), keyval_raw).astype(jnp.bfloat16)
    grad_group = gather(cotangent, "context")
    keyval = gather(after(keyval, grad_group), "context").reshape(contexts // 2, 2, 2 * tok, DH)
    keys, values = keyval[:, 0].reshape(group, DH), keyval[:, 1].reshape(group, DH)
    query_raw = jnp.dot(attn_pair, query_half, preferred_element_type=jnp.float32)
    heads = query_raw.shape[1] // DH
    queries = (
        (
            rotate(query_raw.reshape(2 * tok, heads, DH), cosine[:, None, :], sine[:, None, :])
            * DH ** (-0.5)
        )
        .astype(jnp.bfloat16)
        .reshape(2 * tok, heads * DH)
    )
    mixed_half = mix(mask, queries, keys, values)
    mixed_own = swap_rows(mixed_half, core)
    mixed_pair = pair_rows(mixed_own, core)
    attn_out = swap_rows(
        jnp.dot(mixed_pair, output_half, preferred_element_type=jnp.float32), core
    )
    attn_group = gather(after(attn_in, keyval), "context")
    resid = source + after(attn_out, attn_group) + bias_out

    feed_in = rms_norm(resid, gain_two).astype(jnp.bfloat16)
    mixed_group = gather(mixed_own, "context")
    feed_group = gather(feed_in, "context")
    gate_up_part, down_part = gather_cuts(
        (gate_up_weight, after(down_weight, feed_in)),
        ((shard_rows, gate_up_pieces), (block, down_pieces)),
        ((model, 2 * units), (units, model)),
        1,
    )
    hidden, gate_back, up_back, gate_sums, up_sums = feed(
        feed_group, after(grad_group, mixed_group), gate_up_part, down_part, bias_gate_up, unit_live
    )
    gate_up_low = jnp.concatenate([gate_back, up_back], axis=1)
    feed_part = against(gate_up_low, gate_up_part).astype(jnp.bfloat16)
    feed_in_grad = lax.psum_scatter(feed_part, "context", scatter_dimension=0, tiled=True)
    (down_sum,), _ = work(2, [(grad_group, after(hidden, feed_part))])
    down_part_out = jnp.dot(
        after(hidden, down_sum), down_part, preferred_element_type=jnp.float32
    ).astype(jnp.bfloat16)
    feed_in_grad = after(feed_in_grad, down_part_out)
    down_out = lax.psum_scatter(
        after(down_part_out, feed_in_grad), "context", scatter_dimension=0, tiled=True
    ).astype(jnp.float32)
    block_out = (resid + down_out + bias_down).astype(jnp.bfloat16)
    feed_in_grad = feed_in_grad.astype(jnp.float32)

    grad_out = cotangent.astype(jnp.float32)
    resid_part, gain_two_grad = jax.vjp(rms_norm, resid, gain_two)[1](feed_in_grad)
    resid_grad = grad_out + resid_part
    attn_grad_low = resid_grad.astype(jnp.bfloat16)
    mixed_back = summed_half(
        against(swap_columns(attn_grad_low, core), output_half), core, 1
    ).astype(jnp.bfloat16)
    query_acc, key_acc, value_acc = mix_back(mask, queries, keys, values, mixed_back)
    keyval_acc = jnp.stack(
        [key_acc.reshape(contexts // 2, 2 * tok, DH), value_acc.reshape(contexts // 2, 2 * tok, DH)],
        axis=1,
    ).reshape(contexts, 2 * tok, DH).astype(jnp.bfloat16)
    rows_wide = -(-owned // LANES) * LANES
    attn_grad_rows = jnp.pad(
        attn_grad_low.reshape(tok, shards, contexts, owned).transpose(2, 0, 1, 3),
        ((0, 0), (0, 0), (0, 0), (0, rows_wide - owned)),
    ).reshape(contexts, tok, shards * rows_wide)
    (gate_sum,), (keyval_acc, attn_grad_rows) = work(
        3, [(feed_group, gate_back)], [keyval_acc, attn_grad_rows]
    )
    attn_grad_rows = attn_grad_rows.reshape(group, shards * rows_wide)
    keyval_acc = jnp.sum(keyval_acc.astype(jnp.float32), axis=0)
    keyval_back = jnp.where(core == 0, rotate(keyval_acc, cosine, -sine), keyval_acc).astype(
        jnp.bfloat16
    )
    query_back = (
        rotate(query_acc.reshape(2 * tok, heads, DH), cosine[:, None, :], -sine[:, None, :])
        * DH ** (-0.5)
    ).reshape(2 * tok, heads * DH).astype(jnp.bfloat16)
    attn_in_grad = summed_half(
        against(query_back, query_half) + against(keyval_back, keyval_half), core, 0
    )
    input_part, gain_one_grad = jax.vjp(rms_norm, source, gain_one)[1](attn_in_grad)
    input_grad = resid_grad + input_part

    chips = contexts // 2

    def by_chips(field):
        return field.reshape(2 * tok, chips, field.shape[1] // chips).transpose(1, 0, 2)

    def by_owners(field):
        return field.reshape(contexts, owned, field.shape[1])

    head_part, keyval_part = query_back.shape[1] // chips, keyval_back.shape[1] // chips
    spare = max(2 * LANES - head_part - keyval_part, 0)
    back_cols = jnp.concatenate([by_chips(query_back), by_chips(keyval_back)], axis=2)
    back_cols = jnp.pad(back_cols, ((0, 0), (0, 0), (0, spare)))
    moving = [back_cols, by_owners(down_sum), by_owners(gate_sum)]
    if group <= 1024:
        (up_sum, output_sum), (back_cols, down_rows, gate_rows) = work(
            4, [(feed_group, up_back), (attn_grad_rows, mixed_group)], moving
        )
    else:
        (up_sum,), (back_cols, down_rows, gate_rows) = work(4, [(feed_group, up_back)], moving)
        (output_sum,), _ = work(6, [(attn_grad_rows, mixed_group)])
    back_cols = back_cols.reshape(group, back_cols.shape[2])

    sums = jnp.concatenate(
        [
            gain_one_grad.reshape(model),
            jnp.sum(attn_grad_low.astype(jnp.float32), axis=0),
            gain_two_grad.reshape(model),
            jnp.sum(grad_out, axis=0),
            gate_sums.reshape(units),
            up_sums.reshape(units),
        ]
    )
    sums = sums + across(sums, 1)
    sums = sums + across(sums, 2)
    mine = [
        lax.dynamic_index_in_dim(
            sums[i * model : (i + 1) * model].reshape(shards, contexts, owned), shard, 0, False
        )
        for i in range(4)
    ]
    wide = 4 * owned + 2 * units
    tall = -(-wide // (8 * LANES)) * LANES
    vectors = jnp.concatenate(
        mine
        + [
            jnp.broadcast_to(sums[4 * model :], (contexts, 2 * units)),
            jnp.zeros((contexts, 8 * tall - wide), jnp.float32),
        ],
        axis=1,
    ).reshape(contexts, 8, tall)
    if owned % 16 == 0:
        _, (up_rows, vectors, back_rows) = work(
            5, [(attn_group, back_cols)], [by_owners(up_sum), vectors], True
        )
    else:
        (back_sum,), (up_rows, vectors) = work(
            5, [(attn_group, back_cols)], [by_owners(up_sum), vectors]
        )
        _, (back_rows,) = work(7, [], [by_owners(back_sum)])
    vectors = vectors.reshape(contexts, 8 * tall)
    own = jnp.sum(vectors[:, : 4 * owned], axis=0).reshape(4, owned)
    unit_sums = join_units(
        vectors[:, 4 * owned : wide], 2, shards, width, per_shard
    )
    unit_owned = 2 * ff // (shards * contexts)
    gate_up_bias_grad = lax.dynamic_slice_in_dim(
        unit_sums, (shard * contexts + place) * unit_owned, unit_owned
    )
    pieces = unit_pieces(contexts, shards, width, per_shard)
    down_weight_grad = lay([down_rows], pieces, ff, True)
    gate_up_grad = lay([gate_rows, up_rows], pieces, ff)
    def by_columns(field):
        return (
            field.reshape(chips, 2, owned, field.shape[2])
            .transpose(2, 1, 0, 3)
            .reshape(owned, contexts * field.shape[2])
            .astype(jnp.float32)
        )

    query_grad = by_columns(back_rows[:, :, :head_part])
    keyval_grad = by_columns(back_rows[:, :, head_part : head_part + keyval_part])
    output_weight_grad = output_sum[:owned].astype(jnp.float32).T
    return (
        block_out,
        input_grad,
        own[0],
        query_grad,
        keyval_grad,
        output_weight_grad,
        own[1],
        own[2],
        gate_up_grad,
        gate_up_bias_grad,
        down_weight_grad,
        own[3],
    )


def solution(mesh):
    placed = (
        P(("shard", "context"), None),
        P("shard"),
        P(("shard", "context"), None),
        P("shard"),
        P("shard", None),
        P("shard", None),
        P("shard", None),
        P("shard"),
        P("shard"),
        P("shard", None),
        P("shard"),
        P("shard", None),
        P("shard"),
    )
    return jax.shard_map(
        body,
        mesh=mesh,
        in_specs=placed,
        out_specs=(
            P(("shard", "context"), None),
            P(("shard", "context"), None),
            P(("shard", "context")),
            P(("shard", "context"), None),
            P(("shard", "context"), None),
            P(None, ("shard", "context")),
            P(("shard", "context")),
            P(("shard", "context")),
            P(("shard", "context"), None),
            P(("shard", "context")),
            P(None, ("shard", "context")),
            P(("shard", "context")),
        ),
        check_vma=False,
    )
```

```python
import functools
import math

import jax
import jax.numpy as jnp
from jax import lax
from jax.experimental import pallas as pl
from jax.experimental.pallas import tpu as pltpu
from jax.sharding import PartitionSpec as P

HEADS = 10
DH = 256
FF = 7680
WINDOW = 2048


EPS = 1e-06
NEG = -1e30
ROPE_LOG = math.log(10000.0)


def frequencies(head_dim):
    quarter = head_dim // 4
    steps = jnp.arange(quarter).astype(jnp.float32)
    return jnp.exp(-ROPE_LOG * (2.0 * steps) / (head_dim // 2))


def rotate(field, cosine, sine):
    width = field.shape[-1] // 2
    quarter = width // 2
    first = field[..., :quarter]
    second = field[..., quarter:width]
    return jnp.concatenate(
        [first * cosine - second * sine, second * cosine + first * sine, field[..., width:]],
        axis=-1,
    )


def rms_norm(field, gain):
    return field * lax.rsqrt(jnp.mean(field * field, axis=-1, keepdims=True) + EPS) * gain


def geglu(gate_up):
    half = gate_up.shape[-1] // 2
    return jax.nn.gelu(gate_up[:, :half], approximate=True) * gate_up[:, half:]


def over_rows(left, right):
    return lax.dot_general(
        left, right, (((0,), (0,)), ((), ())), preferred_element_type=jnp.float32
    )


def against(left, weight):
    return lax.dot_general(
        left, weight, (((1,), (1,)), ((), ())), preferred_element_type=jnp.float32
    )


VMEM_LIMIT = 56 * 1024 * 1024
LANES = 128
MESH = pl.DeviceIdType.MESH
GELU = 0.7978845608028654
CUBE = 0.044715


def gather(value, axis):
    return lax.all_gather(value, axis, axis=0, tiled=True)


def across(value, bit):
    count = lax.axis_size("shard")
    return lax.ppermute(value, "shard", [(i, i ^ bit) for i in range(count)])


def after(value, *earlier):
    return lax.optimization_barrier((value, *earlier))[0]


def sibling(value):
    count = lax.axis_size("context")
    return lax.ppermute(value, "context", [(i, i ^ 1) for i in range(count)])


def halves(value, core, axis):
    low, high = jnp.split(value, 2, axis=axis)
    return jnp.where(core == 0, low, high), jnp.where(core == 0, high, low)


def swap_rows(value, core):
    mine, theirs = halves(value, core, 0)
    other = sibling(theirs)
    return jnp.where(
        core == 0, jnp.concatenate([mine, other], axis=1), jnp.concatenate([other, mine], axis=1)
    )


def swap_columns(own, core):
    mine, theirs = halves(own, core, 1)
    other = sibling(theirs)
    return jnp.where(
        core == 0, jnp.concatenate([mine, other], axis=0), jnp.concatenate([other, mine], axis=0)
    )


def summed_half(value, core, axis):
    mine, theirs = halves(value, core, axis)
    return mine + sibling(theirs)


def unit_tiles(ff, shards, contexts):
    per_shard = ff // shards // LANES
    return -(-per_shard // contexts), per_shard


def join_units(pieces, parts, shards, width, per_shard):
    contexts, inner = pieces.shape[0], pieces.shape[1:-1]
    field = pieces.reshape(contexts, *inner, parts, shards, width * LANES)
    kept = []
    for at in range(contexts):
        first = at * width
        if first >= per_shard:
            continue
        start = min(first, per_shard - width)
        stop = min(first + width, per_shard)
        kept.append(field[at, ..., (first - start) * LANES : (stop - start) * LANES])
    return jnp.concatenate(kept, axis=-1).reshape(*inner, parts * shards * per_shard * LANES)


def unit_pieces(contexts, shards, width, per_shard):
    found = []
    for at in range(contexts):
        first = at * width
        if first >= per_shard:
            continue
        start, stop = min(first, per_shard - width), min(first + width, per_shard)
        for shard in range(shards):
            found.append(
                (
                    at,
                    (shard * width + first - start) * LANES,
                    (stop - first) * LANES,
                    (shard * per_shard + first) * LANES,
                )
            )
    return found


def lay_kernel(pieces, *refs):
    *sources, out_ref = refs
    units = out_ref.shape[1] // len(sources)
    for part, source in enumerate(sources):
        for at, column, wide, first in pieces:
            out_ref[:, part * units + first : part * units + first + wide] = source[
                at, :, column : column + wide
            ].astype(jnp.float32)


def lay_kernel_turned(pieces, source, out_ref):
    for at, column, wide, first in pieces:
        out_ref[first : first + wide, :] = source[at, :, column : column + wide].astype(jnp.float32).T


def lay(fields, pieces, units, turned=False):
    rows = fields[0].shape[1]
    shape = (units, rows) if turned else (rows, len(fields) * units)
    return pl.pallas_call(
        functools.partial(lay_kernel_turned if turned else lay_kernel, pieces),
        in_specs=[pl.BlockSpec(memory_space=pltpu.VMEM)] * len(fields),
        out_specs=pl.BlockSpec(memory_space=pltpu.VMEM),
        out_shape=jax.ShapeDtypeStruct(shape, jnp.float32),
        compiler_params=pltpu.CompilerParams(vmem_limit_bytes=VMEM_LIMIT),
    )(*fields)


def shard_places():
    here = lax.axis_index("shard")
    return here, here + 1 - 2 * lax.rem(here, 2), lax.rem(here + 2, 4), 3 - here


def greet(shards, contexts=()):
    barrier = pltpu.get_barrier_semaphore()
    for axis, places in (("shard", shards), ("context", contexts)):
        for place in places:
            pl.semaphore_signal(barrier, 1, device_id={axis: place}, device_id_type=MESH)
    pl.semaphore_wait(barrier, len(shards) + len(contexts))


def to_device(axis, source, target, send, receive, place):
    return pltpu.make_async_remote_copy(
        src_ref=source,
        dst_ref=target,
        send_sem=send,
        recv_sem=receive,
        device_id={axis: place},
        device_id_type=MESH,
    )


class Gather:
    def __init__(self, rows, pieces):
        self.rows, self.pieces = rows, pieces

    def scratch(self):
        most = 2 * (len(self.pieces()) // 2) or 1
        return [
            pltpu.SemaphoreType.DMA((most, 2)),
            pltpu.SemaphoreType.DMA((most, 2)),
            pltpu.SemaphoreType.DMA((most,)),
            pltpu.SemaphoreType.DMA((2,)),
            pltpu.SemaphoreType.DMA((2,)),
        ]

    def bind(self, source, whole, send, receive, local, send_on, receive_on):
        self.source, self.whole, self.local = source, whole, local
        self.send, self.receive, self.send_on, self.receive_on = send, receive, send_on, receive_on
        self.here, along_x, along_y, self.far = shard_places()
        self.near = (along_x, along_y)
        self.kept, self.sent = [], []

    def block(self, place, start, rows):
        return pl.ds(pl.multiple_of(place * self.rows + start, 16), rows)

    def post(self):
        for j, (row, column, wide, into) in enumerate(self.pieces()):
            piece = self.source.at[pl.ds(row, self.rows), pl.ds(column, wide)]
            target = self.whole.at[self.block(self.here, 0, self.rows), pl.ds(into, wide)]
            self.kept.append(pltpu.make_async_copy(piece, target, self.local.at[j]))
            self.kept[-1].start()
            for hop, place in enumerate(self.near):
                self.push(piece, target, self.send.at[j, hop], self.receive.at[j, hop], place)

    def push(self, source, target, send, receive, place):
        self.sent.append(to_device("shard", source, target, send, receive, place))
        self.sent[-1].start()

    def pass_on(self):
        half = self.rows // 2
        for j, (_, _, wide, into) in enumerate(self.pieces()):
            for hop, place in enumerate(self.near):
                came = self.whole.at[self.block(place, 0, self.rows), pl.ds(into, wide)]
                to_device(
                    "shard", came, came, self.send.at[j, hop], self.receive.at[j, hop], place
                ).wait_recv()
        for hop in range(2):
            part = self.whole.at[self.block(self.near[1 - hop], hop * half, half)]
            self.push(part, part, self.send_on.at[hop], self.receive_on.at[hop], self.near[hop])

    def finish(self):
        half = self.rows // 2
        for hop in range(2):
            came = self.whole.at[self.block(self.far, hop * half, half)]
            to_device(
                "shard", came, came, self.send_on.at[hop], self.receive_on.at[hop], self.near[hop]
            ).wait_recv()
        for copy in self.kept:
            copy.wait()

    def close(self):
        for copy in self.sent:
            copy.wait_send()


class Spread:
    def __init__(self, chips):
        self.chips = chips

    def scratch(self):
        return [pltpu.SemaphoreType.DMA((self.chips,))] * 4 + [pltpu.SemaphoreType.DMA]

    def bind(self, own, group, send, receive, send_on, receive_on, local):
        self.own, self.group, self.local = own, group, local
        self.send, self.receive, self.send_on, self.receive_on = send, receive, send_on, receive_on
        self.me = lax.axis_index("context")
        self.chip, self.core = self.me // 2, lax.rem(self.me, 2)
        self.mate = self.me + 1 - 2 * self.core
        self.sent = []

    def push(self, source, target, send, receive, place):
        self.sent.append(to_device("context", source, target, send, receive, place))
        self.sent[-1].start()

    def came(self, k, core):
        return 2 * lax.rem(self.chip + self.chips - k, self.chips) + core

    def post(self):
        self.kept = pltpu.make_async_copy(self.own, self.group.at[self.me], self.local)
        self.kept.start()
        for k in range(1, self.chips):
            place = 2 * lax.rem(self.chip + k, self.chips) + self.core
            self.push(self.own, self.group.at[self.me], self.send.at[k], self.receive.at[k], place)
        self.push(
            self.own, self.group.at[self.me], self.send_on.at[0], self.receive_on.at[0], self.mate
        )

    def pass_on(self):
        for k in range(1, self.chips):
            block = self.group.at[self.came(k, self.core)]
            to_device(
                "context", block, block, self.send.at[k], self.receive.at[k], self.mate
            ).wait_recv()
            self.push(block, block, self.send_on.at[k], self.receive_on.at[k], self.mate)

    def finish(self):
        self.kept.wait()
        for k in range(self.chips):
            block = self.group.at[self.came(k, 1 - self.core)]
            to_device(
                "context", block, block, self.send_on.at[k], self.receive_on.at[k], self.mate
            ).wait_recv()
        for copy in self.sent:
            copy.wait_send()


def opening_kernel(gathers, spreads, *refs):
    refs = list(refs)

    def take(count):
        taken = refs[:count]
        del refs[:count]
        return taken

    sources = take(len(gathers))
    source_ref, mask_ref, cosine_ref, sine_ref = take(4)
    wholes = take(len(gathers))
    queries_ref, keyval_ref, resid_ref = take(3)
    groups = take(2)
    pair, attn, small, big, keyval, mixed, mixed_own, feed_own, out, out_came, vectors = take(11)
    swap_send, swap_receive, load, keyval_send, keyval_receive = take(5)
    for gather_of, source, whole in zip(gathers, sources, wholes):
        gather_of.bind(source, whole, *take(5))
    for spread, own, group in zip(spreads, (mixed_own, feed_own), groups):
        spread.bind(own, group, *take(5))
    me, contexts = lax.axis_index("context"), lax.axis_size("context")
    chip, core = me // 2, lax.rem(me, 2)
    mate = me + 1 - 2 * core
    tok, model = source_ref.shape
    rows = 2 * tok
    half = model // 2
    others = [lax.rem(me + k, contexts) for k in range(1, contexts)]
    greet(gathers[0].near, others)
    vector_of, keyval_of, query_of, output_of, gate_up_of, down_of = gathers
    swaps = []

    def swap(step, source, target):
        swaps.append(
            to_device("context", source, target, swap_send.at[step], swap_receive.at[step], mate)
        )
        swaps[-1].start()

    def fetch(step, whole, target):
        copy = pltpu.make_async_copy(whole, target, load.at[step])
        copy.start()
        copy.wait()

    vector_of.post()
    keyval_of.post()
    query_of.post()
    pair[core] = source_ref[...]
    swap(0, source_ref, pair.at[core])

    vector_of.pass_on()
    vector_of.finish()
    fetch(0, vector_of.whole, vectors)

    def vector(row):
        tall = vector_of.rows
        return jnp.concatenate(
            [vectors[j * tall + row : j * tall + row + 1, :] for j in range(4)], axis=1
        ).astype(jnp.float32)

    swaps[0].wait_recv()
    attn[...] = rms_norm(
        pair[...].reshape(rows, model).astype(jnp.float32), vector(0)
    ).astype(jnp.bfloat16)

    keyval_of.pass_on()
    keyval_of.finish()
    fetch(1, keyval_of.whole, small)
    cosine, sine = cosine_ref[...], sine_ref[...]

    def turned(field):
        return field * cosine + pltpu.roll(field, DH // 4, 1) * sine

    raw = jnp.dot(attn[...], small[...], preferred_element_type=jnp.float32)
    at = pl.ds(pl.multiple_of(chip * rows, rows), rows)
    keyval[core, at, : DH // 2] = jnp.where(
        core == 0, turned(raw[:, : DH // 2]), raw[:, : DH // 2]
    ).astype(jnp.bfloat16)
    keyval[core, at, DH // 2 :] = raw[:, DH // 2 :].astype(jnp.bfloat16)
    keyval_sent = []
    for k in range(1, contexts):
        block = keyval.at[core, at]
        keyval_sent.append(
            to_device(
                "context", block, block, keyval_send.at[k], keyval_receive.at[k], others[k - 1]
            )
        )
        keyval_sent[-1].start()

    query_of.pass_on()
    query_of.finish()
    output_of.post()
    fetch(2, query_of.whole, big)
    heads = half // DH
    for h in range(heads):
        raw = jnp.dot(
            attn[...], big[:, h * DH : (h + 1) * DH], preferred_element_type=jnp.float32
        ) * DH ** (-0.5)
        queries_ref[:, h * DH : h * DH + DH // 2] = turned(raw[:, : DH // 2]).astype(jnp.bfloat16)
        queries_ref[:, h * DH + DH // 2 : (h + 1) * DH] = raw[:, DH // 2 :].astype(jnp.bfloat16)
    for k in range(1, contexts):
        place = lax.rem(me + contexts - k, contexts)
        block = keyval.at[
            lax.rem(place, 2), pl.ds(pl.multiple_of((place // 2) * rows, rows), rows)
        ]
        to_device(
            "context", block, block, keyval_send.at[k], keyval_receive.at[k], others[k - 1]
        ).wait_recv()
    for h in range(heads):
        weights = masked_weights(queries_ref[:, h * DH : (h + 1) * DH], keyval[0], mask_ref[...])
        mixed[core, :, h * DH : (h + 1) * DH] = jnp.dot(
            weights.astype(jnp.bfloat16), keyval[1], preferred_element_type=jnp.float32
        ).astype(jnp.bfloat16)
    swap(1, mixed.at[core], mixed.at[core])

    output_of.pass_on()
    output_of.finish()
    gate_up_of.post()
    down_of.post()
    fetch(3, output_of.whole, big)
    swaps[1].wait_recv()
    out[...] = jnp.dot(mixed[0], big[:half], preferred_element_type=jnp.float32) + jnp.dot(
        mixed[1], big[half:], preferred_element_type=jnp.float32
    )
    mine = pl.ds(pl.multiple_of(core * tok, tok), tok)
    theirs = pl.ds(pl.multiple_of((1 - core) * tok, tok), tok)
    swap(2, out.at[theirs], out_came)
    mixed_own[:, :half] = mixed[0, mine]
    mixed_own[:, half:] = mixed[1, mine]
    swaps[2].wait_recv()
    low = jnp.where(core == 0, out[mine], out_came[...])
    high = jnp.where(core == 0, out_came[...], out[mine])
    resid = (
        source_ref[...].astype(jnp.float32) + jnp.concatenate([low, high], axis=1) + vector(1)
    )
    resid_ref[...] = resid
    feed_own[...] = rms_norm(resid, vector(2)).astype(jnp.bfloat16)
    spreads[1].post()
    spreads[0].post()
    keyval_ref[...] = keyval[...]
    gate_up_of.pass_on()
    down_of.pass_on()
    spreads[1].pass_on()
    spreads[0].pass_on()
    for part in spreads:
        part.finish()
    gate_up_of.finish()
    down_of.finish()
    for gather_of in gathers:
        gather_of.close()
    for copy in swaps + keyval_sent:
        copy.wait_send()


def opening(number, cuts, source, mask, cosine, sine):
    contexts = lax.axis_size("context")
    tok, model = source.shape
    slots = mask.shape[1]
    half = model // 2
    gathers = [Gather(rows, pieces) for _, rows, pieces, _ in cuts]
    spreads = [Spread(contexts // 2), Spread(contexts // 2)]
    low, full = jnp.bfloat16, jnp.float32
    dma = pltpu.SemaphoreType.DMA
    tall, wide = cuts[0][1], cuts[0][3]
    outs = pl.pallas_call(
        functools.partial(opening_kernel, gathers, spreads),
        in_specs=[pl.BlockSpec(memory_space=pl.ANY)] * len(cuts)
        + [pl.BlockSpec(memory_space=pltpu.VMEM)] * 4,
        out_specs=[pl.BlockSpec(memory_space=pl.ANY)] * len(cuts)
        + [pl.BlockSpec(memory_space=pltpu.VMEM)] * 3
        + [pl.BlockSpec(memory_space=pl.ANY)] * 2,
        out_shape=[jax.ShapeDtypeStruct((4 * rows, columns), low) for _, rows, _, columns in cuts]
        + [
            jax.ShapeDtypeStruct((2 * tok, half), low),
            jax.ShapeDtypeStruct((2, slots, DH), low),
            jax.ShapeDtypeStruct((tok, model), full),
        ]
        + [jax.ShapeDtypeStruct((contexts, tok, model), low)] * 2,
        scratch_shapes=[
            pltpu.VMEM((2, tok, model), low),
            pltpu.VMEM((2 * tok, model), low),
            pltpu.VMEM((model, cuts[1][3]), low),
            pltpu.VMEM((model, half), low),
            pltpu.VMEM((2, slots, DH), low),
            pltpu.VMEM((2, 2 * tok, half), low),
            pltpu.VMEM((tok, model), low),
            pltpu.VMEM((tok, model), low),
            pltpu.VMEM((2 * tok, half), full),
            pltpu.VMEM((tok, half), full),
            pltpu.VMEM((4 * tall, wide), low),
            dma((3,)),
            dma((3,)),
            dma((4,)),
            dma((contexts,)),
            dma((contexts,)),
        ]
        + [shape for part in gathers + spreads for shape in part.scratch()],
        cost_estimate=pl.CostEstimate(flops=0, transcendentals=0, bytes_accessed=700_000_000),
        compiler_params=pltpu.CompilerParams(
            collective_id=number, has_side_effects=True, vmem_limit_bytes=VMEM_LIMIT
        ),
    )(*[array for array, _, _, _ in cuts], source, mask, cosine, sine)
    return outs[: len(cuts)], outs[len(cuts) :]


class Product:
    def __init__(self, left, right):
        self.rows, self.wide = left[1] // 4, right[1]
        half = -(-self.wide // (2 * LANES)) * LANES
        self.sides = ((0, half), (half, self.wide - half))

    def scratch(self):
        shapes = [pltpu.VMEM((self.rows, self.wide), jnp.float32)]
        for _, wide in self.sides:
            shapes += [pltpu.VMEM((3, self.rows, wide), jnp.bfloat16)] * 2
        return shapes + [pltpu.SemaphoreType.DMA((6,)), pltpu.SemaphoreType.DMA((6,))]

    def run(self, left, right, out, own, made_a, came_a, made_b, came_b, send, receive):
        here, along_x, along_y, far = shard_places()
        ways = ((along_x, along_y), (along_y, along_x))
        made, came = (made_a, made_b), (came_a, came_b)
        columns = [pl.ds(start, wide) for start, wide in self.sides]
        copies = []

        def product(place, side):
            block = pl.ds(pl.multiple_of(place * self.rows, LANES), self.rows)
            return over_rows(left[:, block], right[:, columns[side]])

        def push(step, side, place):
            slot = 2 * step + side
            copies.append(
                to_device(
                    "shard",
                    made[side].at[step],
                    came[side].at[step],
                    send.at[slot],
                    receive.at[slot],
                    place,
                )
            )
            copies[-1].start()

        for side in range(2):
            made[side][0] = product(far, side).astype(jnp.bfloat16)
            push(0, side, ways[side][0])
        for side in range(2):
            made[side][1] = product(ways[side][0], side).astype(jnp.bfloat16)
            push(1, side, ways[side][0])
        for side in range(2):
            kept = product(ways[side][1], side)
            copies[side].wait_recv()
            made[side][2] = (kept + came[side][0].astype(jnp.float32)).astype(jnp.bfloat16)
            push(2, side, ways[side][1])
        for side in range(2):
            own[:, columns[side]] = product(here, side)
        for side in range(2):
            copies[2 + side].wait_recv()
            own[:, columns[side]] += came[side][1].astype(jnp.float32)
        for side in range(2):
            copies[4 + side].wait_recv()
            out[:, columns[side]] = (own[:, columns[side]] + came[side][2].astype(jnp.float32)).astype(
                jnp.bfloat16
            )
        return copies


class Exchange:
    def __init__(self, count, stride):
        self.count, self.stride = count, stride

    def scratch(self):
        return [pltpu.SemaphoreType.DMA((self.count,))] * 2 + [pltpu.SemaphoreType.DMA]

    def peers(self):
        me = lax.axis_index("context")
        slot, rest = me // self.stride, lax.rem(me, self.stride)
        places = [lax.rem(slot + k, self.count) for k in range(self.count)]
        return places, [place * self.stride + rest for place in places]

    def start(self, blocks, out, send, receive, local):
        slots, devices = self.peers()
        kept = pltpu.make_async_copy(blocks(slots[0]), out.at[slots[0]], local)
        kept.start()
        copies = []
        for k in range(1, self.count):
            copies.append(
                to_device(
                    "context", blocks(slots[k]), out.at[slots[0]], send.at[k], receive.at[k], devices[k]
                )
            )
            copies[-1].start()

        def finish():
            kept.wait()
            for k in range(1, self.count):
                source = slots[self.count - k]
                to_device(
                    "context", out.at[source], out.at[source], send.at[k], receive.at[k], devices[k]
                ).wait_recv()
            for copy in copies:
                copy.wait_send()

        return finish


def work_kernel(products, exchanges, chained, *refs):
    refs = list(refs)

    def take(count):
        taken = refs[:count]
        del refs[:count]
        return taken

    operands = [take(2) for _ in products]
    arrays = take(len(exchanges) - (1 if chained else 0))
    results = take(len(products))
    moved = take(len(exchanges))
    product_scratch = [take(len(p.scratch())) for p in products]
    exchange_scratch = [take(len(e.scratch())) for e in exchanges]
    _, along_x, along_y, _ = shard_places()
    everyone = max(exchanges, key=lambda e: e.count).peers()[1][1:] if exchanges else []
    greet((along_x, along_y), everyone)
    finishes, copies = [], []
    for exchange, array, out, scratch in zip(exchanges, arrays, moved, exchange_scratch):
        finishes.append(exchange.start(lambda j, array=array: array.at[j], out, *scratch))
    for product, (left, right), out, scratch in zip(products, operands, results, product_scratch):
        copies += product.run(left, right, out, *scratch)
    if chained:
        rows = products[0].rows // exchanges[-1].count
        finishes.append(
            exchanges[-1].start(
                lambda j: results[0].at[pl.ds(pl.multiple_of(j * rows, 16), rows)],
                moved[-1],
                *exchange_scratch[-1],
            )
        )
    for copy in copies:
        copy.wait_send()
    for finish in finishes:
        finish()


def work(number, products=(), exchanges=(), chained=False):
    contexts = lax.axis_size("context")
    made = [Product(left.shape, right.shape) for left, right in products]
    swaps = [Exchange(array.shape[0], contexts // array.shape[0]) for array in exchanges]
    results = [jax.ShapeDtypeStruct((p.rows, p.wide), jnp.bfloat16) for p in made]
    moved = [jax.ShapeDtypeStruct(array.shape, array.dtype) for array in exchanges]
    if chained:
        swaps.append(Exchange(contexts, 1))
        moved.append(
            jax.ShapeDtypeStruct((contexts, made[0].rows // contexts, made[0].wide), jnp.bfloat16)
        )
    scratch = [shape for part in made + swaps for shape in part.scratch()]
    vmem = pl.BlockSpec(memory_space=pltpu.VMEM)
    hbm = pl.BlockSpec(memory_space=pl.ANY)
    outs = pl.pallas_call(
        functools.partial(work_kernel, made, swaps, chained),
        in_specs=[vmem] * (2 * len(made)) + [hbm] * len(exchanges),
        out_specs=[vmem] * len(made) + [hbm] * len(swaps),
        out_shape=results + moved,
        scratch_shapes=scratch,
        cost_estimate=pl.CostEstimate(flops=0, transcendentals=0, bytes_accessed=150_000_000),
        compiler_params=pltpu.CompilerParams(
            collective_id=number, has_side_effects=True, vmem_limit_bytes=VMEM_LIMIT
        ),
    )(*[operand for pair in products for operand in pair], *exchanges)
    return outs[: len(made)], outs[len(made) :]


def masked_weights(q, k, mask):
    scores = lax.dot_general(q, k, (((1,), (1,)), ((), ())), preferred_element_type=jnp.float32)
    scores = jnp.where(mask > 0.0, scores, NEG)
    raised = jnp.exp(scores - jnp.max(scores, axis=1, keepdims=True))
    return raised / jnp.sum(raised, axis=1, keepdims=True)


def mix_back_kernel(mask_ref, q_ref, k_ref, v_ref, g_ref, dq_ref, dk_ref, dv_ref):
    q, k, g = q_ref[...], k_ref[...], g_ref[...]
    weights = masked_weights(q, k, mask_ref[...])
    value_score = against(g, v_ref[...])
    delta = jnp.sum(weights * value_score, axis=1, keepdims=True)
    score_back = (weights * (value_score - delta)).astype(jnp.bfloat16)
    dq_ref[...] = jnp.dot(score_back, k, preferred_element_type=jnp.float32)
    key_piece = over_rows(score_back, q)
    value_piece = over_rows(weights.astype(jnp.bfloat16), g)

    @pl.when(pl.program_id(0) == 0)
    def _():
        dk_ref[...] = key_piece
        dv_ref[...] = value_piece

    @pl.when(pl.program_id(0) > 0)
    def _():
        dk_ref[...] += key_piece
        dv_ref[...] += value_piece


def mix_back(mask, queries, keys, values, grad):
    rows, width = queries.shape
    slots = keys.shape[0]
    whole = lambda h: (0, 0)
    part = lambda h: (0, h)
    return pl.pallas_call(
        mix_back_kernel,
        grid=(width // DH,),
        in_specs=[
            pl.BlockSpec((rows, slots), whole),
            pl.BlockSpec((rows, DH), part),
            pl.BlockSpec((slots, DH), whole),
            pl.BlockSpec((slots, DH), whole),
            pl.BlockSpec((rows, DH), part),
        ],
        out_specs=[
            pl.BlockSpec((rows, DH), part),
            pl.BlockSpec((slots, DH), whole),
            pl.BlockSpec((slots, DH), whole),
        ],
        out_shape=[
            jax.ShapeDtypeStruct((rows, width), jnp.float32),
            jax.ShapeDtypeStruct((slots, DH), jnp.float32),
            jax.ShapeDtypeStruct((slots, DH), jnp.float32),
        ],
        compiler_params=pltpu.CompilerParams(vmem_limit_bytes=VMEM_LIMIT),
    )(mask, queries, keys, values, grad)


def feed_kernel(feed_ref, grad_ref, gate_ref, up_ref, down_ref, bias_gate_ref, bias_up_ref, live_ref,
                hidden_ref, gate_back_ref, up_back_ref, gate_sum_ref, up_sum_ref):
    rows = feed_ref.shape[0]
    step = min(rows, 256)

    @pl.when(pl.program_id(1) == 0)
    def _():
        gate_sum_ref[...] = jnp.zeros_like(gate_sum_ref)
        up_sum_ref[...] = jnp.zeros_like(up_sum_ref)

    def part(i, carry):
        at = pl.ds(pl.multiple_of(i * step, step), step)
        feed = feed_ref[at, :]
        gate = jnp.dot(feed, gate_ref[...], preferred_element_type=jnp.float32) + bias_gate_ref[...]
        up = jnp.dot(feed, up_ref[...], preferred_element_type=jnp.float32) + bias_up_ref[...]
        back = against(grad_ref[at, :], down_ref[...])
        live = live_ref[...]
        square = gate * gate
        bend = jnp.tanh(GELU * gate * (1.0 + CUBE * square))
        half = 0.5 * (1.0 + bend)
        gelu = gate * half * live
        slope = half + 0.5 * gate * (1.0 - bend * bend) * (GELU * (1.0 + 3.0 * CUBE * square))
        hidden_ref[at, :] = (gelu * up).astype(jnp.bfloat16)
        gate_back = (back * up * slope * live).astype(jnp.bfloat16)
        up_back = (back * gelu).astype(jnp.bfloat16)
        gate_back_ref[at, :] = gate_back
        up_back_ref[at, :] = up_back
        gate_sum_ref[...] += jnp.sum(gate_back.astype(jnp.float32), axis=0, keepdims=True)
        up_sum_ref[...] += jnp.sum(up_back.astype(jnp.float32), axis=0, keepdims=True)
        return carry

    lax.fori_loop(0, rows // step, part, 0)


def feed(feed_group, grad_group, gate_up, down, bias, live):
    rows, model = feed_group.shape
    units = down.shape[0]
    wide = min(units, 256)
    blocks = units // wide
    tall = min(rows, 1024)
    buffers = {"pipeline_mode": pl.Buffered(1)} if tall == rows else {}
    tokens = lambda j, i: (i, 0)
    column = lambda j, i: (0, j)
    later = lambda j, i: (0, j + blocks)
    made = lambda j, i: (i, j)
    return pl.pallas_call(
        feed_kernel,
        grid=(blocks, rows // tall),
        in_specs=[
            pl.BlockSpec((tall, model), tokens, **buffers),
            pl.BlockSpec((tall, model), tokens, **buffers),
            pl.BlockSpec((model, wide), column),
            pl.BlockSpec((model, wide), later),
            pl.BlockSpec((wide, model), lambda j, i: (j, 0)),
            pl.BlockSpec((1, wide), column),
            pl.BlockSpec((1, wide), later),
            pl.BlockSpec((1, wide), column),
        ],
        out_specs=[
            pl.BlockSpec((tall, wide), made),
            pl.BlockSpec((tall, wide), made),
            pl.BlockSpec((tall, wide), made),
            pl.BlockSpec((1, wide), column),
            pl.BlockSpec((1, wide), column),
        ],
        out_shape=[
            jax.ShapeDtypeStruct((rows, units), jnp.bfloat16),
            jax.ShapeDtypeStruct((rows, units), jnp.bfloat16),
            jax.ShapeDtypeStruct((rows, units), jnp.bfloat16),
            jax.ShapeDtypeStruct((1, units), jnp.float32),
            jax.ShapeDtypeStruct((1, units), jnp.float32),
        ],
        compiler_params=pltpu.CompilerParams(vmem_limit_bytes=VMEM_LIMIT),
    )(feed_group, grad_group, gate_up, gate_up, down, bias, bias, live)


def body(
    inputs,
    doc_ids,
    cotangent,
    attn_gain,
    query_weight,
    keyval_weight,
    output_weight,
    output_bias,
    feed_gain,
    gate_up_weight,
    gate_up_bias,
    down_weight,
    down_bias,
):
    tok, model = inputs.shape
    shards, contexts = lax.axis_size("shard"), lax.axis_size("context")
    shard, place = lax.axis_index("shard"), lax.axis_index("context")
    core, chip = place % 2, place // 2
    group = tok * contexts
    owned = model // (shards * contexts)
    ff = gate_up_weight.shape[1] // 2
    width, per_shard = unit_tiles(ff, shards, contexts)
    unit_start = jnp.minimum(place * width, per_shard - width)
    units = shards * width * LANES

    shard_rows = model // shards
    block = width * LANES

    def half_of(wide):
        def pieces():
            column = lax.rem(lax.axis_index("context"), 2) * wide
            return [(0, pl.multiple_of(column, LANES), wide, 0)]

        return pieces

    def first_unit():
        return jnp.minimum(lax.axis_index("context") * width, per_shard - width) * LANES

    def gate_up_pieces():
        return [
            (0, pl.multiple_of(j * per_shard * LANES + first_unit(), LANES), block, j * block)
            for j in range(2 * shards)
        ]

    def down_pieces():
        return [(pl.multiple_of(first_unit(), LANES), 0, model, 0)]

    unit_at = unit_start * LANES + jnp.arange(block, dtype=jnp.int32)
    unit_live = jnp.tile(unit_at >= place * block, shards)[None, :].astype(jnp.float32)
    slots = jnp.arange(group, dtype=jnp.int32)
    pair_slots = chip * (2 * tok) + jnp.arange(2 * tok, dtype=jnp.int32)
    pair_docs = lax.dynamic_slice_in_dim(doc_ids, chip * (2 * tok), 2 * tok)
    distance = pair_slots[:, None] - slots[None, :]
    mask = (
        (pair_docs[:, None] == doc_ids[None, :]) & (distance >= 0) & (distance < WINDOW)
    ).astype(jnp.float32)
    angles = pair_slots.astype(jnp.float32)[:, None] * frequencies(DH)[None, :]
    cosine, sine = jnp.cos(angles), jnp.sin(angles)
    vectors = jnp.concatenate([attn_gain, output_bias, feed_gain, down_bias, gate_up_bias])
    vector_rows = vectors.shape[0] // shard_rows
    vector_tall = -(-vector_rows // 32) * 32
    vectors = jnp.pad(
        vectors.reshape(vector_rows, shard_rows), ((0, vector_tall - vector_rows), (0, 0))
    )
    core_cols, core_heads = keyval_weight.shape[1] // 2, query_weight.shape[1] // 2
    (vectors, keyval_half, query_half, output_half, gate_up_part, down_part), (
        queries, keyval, resid, mixed_group, feed_group
    ) = opening(
        0,
        (
            (vectors, vector_tall, lambda: [(0, 0, shard_rows, 0)], shard_rows),
            (keyval_weight, shard_rows, half_of(core_cols), core_cols),
            (query_weight, shard_rows, half_of(core_heads), core_heads),
            (output_weight, shard_rows, half_of(model // 2), model // 2),
            (gate_up_weight, shard_rows, gate_up_pieces, 2 * units),
            (down_weight, block, down_pieces, model),
        ),
        inputs,
        mask,
        jnp.concatenate([cosine, cosine], axis=1),
        jnp.concatenate([-sine, sine], axis=1),
    )
    grad_group = gather(cotangent, "context")
    source_group = gather(inputs, "context")
    vectors = vectors.reshape(shards, vector_tall, shard_rows).astype(jnp.float32)
    gain_one, gain_two, bias_down = (vectors[:, i].reshape(1, model) for i in (0, 2, 3))
    bias_gate_up = vectors[:, 4:vector_rows].reshape(2 * shards, per_shard * LANES)
    bias_gate_up = lax.dynamic_slice_in_dim(
        bias_gate_up, unit_start * LANES, block, 1
    ).reshape(1, 2 * units)
    source = inputs.astype(jnp.float32)
    keys, values = keyval[0], keyval[1]
    heads = core_heads // DH
    mixed_group, feed_group = mixed_group.reshape(group, model), feed_group.reshape(group, model)

    hidden, gate_back, up_back, gate_sums, up_sums = feed(
        feed_group, after(grad_group, source_group), gate_up_part, down_part, bias_gate_up, unit_live
    )
    gate_up_low = jnp.concatenate([gate_back, up_back], axis=1)
    feed_part = against(gate_up_low, gate_up_part).astype(jnp.bfloat16)
    feed_in_grad = lax.psum_scatter(feed_part, "context", scatter_dimension=0, tiled=True)
    (down_sum,), _ = work(2, [(grad_group, after(hidden, feed_part))])
    down_part_out = jnp.dot(
        after(hidden, down_sum), down_part, preferred_element_type=jnp.float32
    ).astype(jnp.bfloat16)
    feed_in_grad = after(feed_in_grad, down_part_out)
    down_out = lax.psum_scatter(
        after(down_part_out, feed_in_grad), "context", scatter_dimension=0, tiled=True
    ).astype(jnp.float32)
    block_out = (resid + down_out + bias_down).astype(jnp.bfloat16)
    feed_in_grad = feed_in_grad.astype(jnp.float32)

    grad_out = cotangent.astype(jnp.float32)
    resid_part, gain_two_grad = jax.vjp(rms_norm, resid, gain_two)[1](feed_in_grad)
    resid_grad = grad_out + resid_part
    attn_grad_low = resid_grad.astype(jnp.bfloat16)
    mixed_back = summed_half(
        against(swap_columns(attn_grad_low, core), output_half), core, 1
    ).astype(jnp.bfloat16)
    query_acc, key_acc, value_acc = mix_back(mask, queries, keys, values, mixed_back)
    keyval_acc = jnp.stack(
        [key_acc.reshape(contexts // 2, 2 * tok, DH), value_acc.reshape(contexts // 2, 2 * tok, DH)],
        axis=1,
    ).reshape(contexts, 2 * tok, DH).astype(jnp.bfloat16)
    rows_wide = -(-owned // LANES) * LANES
    attn_grad_rows = jnp.pad(
        attn_grad_low.reshape(tok, shards, contexts, owned).transpose(2, 0, 1, 3),
        ((0, 0), (0, 0), (0, 0), (0, rows_wide - owned)),
    ).reshape(contexts, tok, shards * rows_wide)
    (gate_sum,), (keyval_acc, attn_grad_rows) = work(
        3, [(feed_group, gate_back)], [keyval_acc, attn_grad_rows]
    )
    attn_grad_rows = attn_grad_rows.reshape(group, shards * rows_wide)
    keyval_acc = jnp.sum(keyval_acc.astype(jnp.float32), axis=0)
    keyval_back = jnp.where(core == 0, rotate(keyval_acc, cosine, -sine), keyval_acc).astype(
        jnp.bfloat16
    )
    query_back = (
        rotate(query_acc.reshape(2 * tok, heads, DH), cosine[:, None, :], -sine[:, None, :])
        * DH ** (-0.5)
    ).reshape(2 * tok, heads * DH).astype(jnp.bfloat16)
    attn_in_grad = summed_half(
        against(query_back, query_half) + against(keyval_back, keyval_half), core, 0
    )
    input_part, gain_one_grad = jax.vjp(rms_norm, source, gain_one)[1](attn_in_grad)
    input_grad = resid_grad + input_part

    chips = contexts // 2

    def by_chips(field):
        return field.reshape(2 * tok, chips, field.shape[1] // chips).transpose(1, 0, 2)

    def by_owners(field):
        return field.reshape(contexts, owned, field.shape[1])

    attn_group = rms_norm(source_group.astype(jnp.float32), gain_one).astype(jnp.bfloat16)
    head_part, keyval_part = query_back.shape[1] // chips, keyval_back.shape[1] // chips
    spare = max(2 * LANES - head_part - keyval_part, 0)
    back_cols = jnp.concatenate([by_chips(query_back), by_chips(keyval_back)], axis=2)
    back_cols = jnp.pad(back_cols, ((0, 0), (0, 0), (0, spare)))
    moving = [back_cols, by_owners(down_sum), by_owners(gate_sum)]
    if group <= 1024:
        (up_sum, output_sum), (back_cols, down_rows, gate_rows) = work(
            4, [(feed_group, up_back), (attn_grad_rows, mixed_group)], moving
        )
    else:
        (up_sum,), (back_cols, down_rows, gate_rows) = work(4, [(feed_group, up_back)], moving)
        (output_sum,), _ = work(6, [(attn_grad_rows, mixed_group)])
    back_cols = back_cols.reshape(group, back_cols.shape[2])

    sums = jnp.concatenate(
        [
            gain_one_grad.reshape(model),
            jnp.sum(attn_grad_low.astype(jnp.float32), axis=0),
            gain_two_grad.reshape(model),
            jnp.sum(grad_out, axis=0),
            gate_sums.reshape(units),
            up_sums.reshape(units),
        ]
    )
    sums = sums + across(sums, 1)
    sums = sums + across(sums, 2)
    mine = [
        lax.dynamic_index_in_dim(
            sums[i * model : (i + 1) * model].reshape(shards, contexts, owned), shard, 0, False
        )
        for i in range(4)
    ]
    wide = 4 * owned + 2 * units
    tall = -(-wide // (8 * LANES)) * LANES
    vectors = jnp.concatenate(
        mine
        + [
            jnp.broadcast_to(sums[4 * model :], (contexts, 2 * units)),
            jnp.zeros((contexts, 8 * tall - wide), jnp.float32),
        ],
        axis=1,
    ).reshape(contexts, 8, tall)
    if owned % 16 == 0:
        _, (up_rows, vectors, back_rows) = work(
            5, [(attn_group, back_cols)], [by_owners(up_sum), vectors], True
        )
    else:
        (back_sum,), (up_rows, vectors) = work(
            5, [(attn_group, back_cols)], [by_owners(up_sum), vectors]
        )
        _, (back_rows,) = work(7, [], [by_owners(back_sum)])
    vectors = vectors.reshape(contexts, 8 * tall)
    own = jnp.sum(vectors[:, : 4 * owned], axis=0).reshape(4, owned)
    unit_sums = join_units(
        vectors[:, 4 * owned : wide], 2, shards, width, per_shard
    )
    unit_owned = 2 * ff // (shards * contexts)
    gate_up_bias_grad = lax.dynamic_slice_in_dim(
        unit_sums, (shard * contexts + place) * unit_owned, unit_owned
    )
    pieces = unit_pieces(contexts, shards, width, per_shard)
    down_weight_grad = lay([down_rows], pieces, ff, True)
    gate_up_grad = lay([gate_rows, up_rows], pieces, ff)
    def by_columns(field):
        return (
            field.reshape(chips, 2, owned, field.shape[2])
            .transpose(2, 1, 0, 3)
            .reshape(owned, contexts * field.shape[2])
            .astype(jnp.float32)
        )

    query_grad = by_columns(back_rows[:, :, :head_part])
    keyval_grad = by_columns(back_rows[:, :, head_part : head_part + keyval_part])
    output_weight_grad = output_sum[:owned].astype(jnp.float32).T
    return (
        block_out,
        input_grad,
        own[0],
        query_grad,
        keyval_grad,
        output_weight_grad,
        own[1],
        own[2],
        gate_up_grad,
        gate_up_bias_grad,
        down_weight_grad,
        own[3],
    )


def solution(mesh):
    placed = (
        P(("shard", "context"), None),
        P("shard"),
        P(("shard", "context"), None),
        P("shard"),
        P("shard", None),
        P("shard", None),
        P("shard", None),
        P("shard"),
        P("shard"),
        P("shard", None),
        P("shard"),
        P("shard", None),
        P("shard"),
    )
    return jax.shard_map(
        body,
        mesh=mesh,
        in_specs=placed,
        out_specs=(
            P(("shard", "context"), None),
            P(("shard", "context"), None),
            P(("shard", "context")),
            P(("shard", "context"), None),
            P(("shard", "context"), None),
            P(None, ("shard", "context")),
            P(("shard", "context")),
            P(("shard", "context")),
            P(("shard", "context"), None),
            P(("shard", "context")),
            P(None, ("shard", "context")),
            P(("shard", "context")),
        ),
        check_vma=False,
    )
```

```python
import functools
import math

import jax
import jax.numpy as jnp
from jax import lax
from jax.experimental import pallas as pl
from jax.experimental.pallas import tpu as pltpu
from jax.sharding import PartitionSpec as P

HEADS = 10
DH = 256
FF = 7680
WINDOW = 2048


EPS = 1e-06
NEG = -1e30
ROPE_LOG = math.log(10000.0)


def frequencies(head_dim):
    quarter = head_dim // 4
    steps = jnp.arange(quarter).astype(jnp.float32)
    return jnp.exp(-ROPE_LOG * (2.0 * steps) / (head_dim // 2))


def rotate(field, cosine, sine):
    width = field.shape[-1] // 2
    quarter = width // 2
    first = field[..., :quarter]
    second = field[..., quarter:width]
    return jnp.concatenate(
        [first * cosine - second * sine, second * cosine + first * sine, field[..., width:]],
        axis=-1,
    )


def rms_norm(field, gain):
    return field * lax.rsqrt(jnp.mean(field * field, axis=-1, keepdims=True) + EPS) * gain


def geglu(gate_up):
    half = gate_up.shape[-1] // 2
    return jax.nn.gelu(gate_up[:, :half], approximate=True) * gate_up[:, half:]


def over_rows(left, right):
    return lax.dot_general(
        left, right, (((0,), (0,)), ((), ())), preferred_element_type=jnp.float32
    )


def against(left, weight):
    return lax.dot_general(
        left, weight, (((1,), (1,)), ((), ())), preferred_element_type=jnp.float32
    )


VMEM_LIMIT = 56 * 1024 * 1024
BACK_LIMIT = 60 * 1024 * 1024
LANES = 128
MESH = pl.DeviceIdType.MESH
GELU = 0.7978845608028654
CUBE = 0.044715


def gather(value, axis):
    return lax.all_gather(value, axis, axis=0, tiled=True)


def across(value, bit):
    count = lax.axis_size("shard")
    return lax.ppermute(value, "shard", [(i, i ^ bit) for i in range(count)])


def after(value, *earlier):
    return lax.optimization_barrier((value, *earlier))[0]


def sibling(value):
    count = lax.axis_size("context")
    return lax.ppermute(value, "context", [(i, i ^ 1) for i in range(count)])


def halves(value, core, axis):
    low, high = jnp.split(value, 2, axis=axis)
    return jnp.where(core == 0, low, high), jnp.where(core == 0, high, low)


def swap_rows(value, core):
    mine, theirs = halves(value, core, 0)
    other = sibling(theirs)
    return jnp.where(
        core == 0, jnp.concatenate([mine, other], axis=1), jnp.concatenate([other, mine], axis=1)
    )


def swap_columns(own, core):
    mine, theirs = halves(own, core, 1)
    other = sibling(theirs)
    return jnp.where(
        core == 0, jnp.concatenate([mine, other], axis=0), jnp.concatenate([other, mine], axis=0)
    )


def summed_half(value, core, axis):
    mine, theirs = halves(value, core, axis)
    return mine + sibling(theirs)


def unit_tiles(ff, shards, contexts):
    per_shard = ff // shards // LANES
    return -(-per_shard // contexts), per_shard


def unit_pieces(contexts, shards, width, per_shard):
    found = []
    for at in range(contexts):
        first = at * width
        if first >= per_shard:
            continue
        start, stop = min(first, per_shard - width), min(first + width, per_shard)
        for shard in range(shards):
            found.append(
                (
                    at,
                    (shard * width + first - start) * LANES,
                    (stop - first) * LANES,
                    (shard * per_shard + first) * LANES,
                )
            )
    return found


def lay_kernel(pieces, down_ref, gate_ref, up_ref, back_ref, output_ref, *outs):
    down_out, gate_up_out, query_out, keyval_out, output_out = outs
    units, owned = down_out.shape[1], down_out.shape[0]
    contexts = back_ref.shape[0]
    head_part, keyval_part = query_out.shape[1] // contexts, keyval_out.shape[1] // contexts
    for source, out, offset in (
        (down_ref, down_out, 0),
        (gate_ref, gate_up_out, 0),
        (up_ref, gate_up_out, units),
    ):
        for at, column, wide, first in pieces:
            out[:, offset + first : offset + first + wide] = source[
                at, :, column : column + wide
            ].astype(jnp.float32)
    for at in range(contexts):
        slot = (at % 2) * (contexts // 2) + at // 2
        part = back_ref[at].astype(jnp.float32)
        query_out[:, slot * head_part : (slot + 1) * head_part] = part[:, :head_part]
        keyval_out[:, slot * keyval_part : (slot + 1) * keyval_part] = part[
            :, head_part : head_part + keyval_part
        ]
    output_out[...] = output_ref[:owned].astype(jnp.float32)


def lay(pieces, owned, widths, *fields):
    return pl.pallas_call(
        functools.partial(lay_kernel, pieces),
        in_specs=[pl.BlockSpec(memory_space=pltpu.VMEM)] * len(fields),
        out_specs=[pl.BlockSpec(memory_space=pltpu.VMEM)] * len(widths),
        out_shape=[jax.ShapeDtypeStruct((owned, wide), jnp.float32) for wide in widths],
        compiler_params=pltpu.CompilerParams(vmem_limit_bytes=VMEM_LIMIT),
    )(*fields)


def shard_places():
    here = lax.axis_index("shard")
    return here, here + 1 - 2 * lax.rem(here, 2), lax.rem(here + 2, 4), 3 - here


def greet(shards, contexts=()):
    barrier = pltpu.get_barrier_semaphore()
    for axis, places in (("shard", shards), ("context", contexts)):
        for place in places:
            pl.semaphore_signal(barrier, 1, device_id={axis: place}, device_id_type=MESH)
    pl.semaphore_wait(barrier, len(shards) + len(contexts))


def to_device(axis, source, target, send, receive, place):
    return pltpu.make_async_remote_copy(
        src_ref=source,
        dst_ref=target,
        send_sem=send,
        recv_sem=receive,
        device_id={axis: place},
        device_id_type=MESH,
    )


class Gather:
    def __init__(self, rows, pieces):
        self.rows, self.pieces = rows, pieces

    def scratch(self):
        most = 2 * (len(self.pieces()) // 2) or 1
        return [
            pltpu.SemaphoreType.DMA((most, 2)),
            pltpu.SemaphoreType.DMA((most, 2)),
            pltpu.SemaphoreType.DMA((most,)),
            pltpu.SemaphoreType.DMA((2,)),
            pltpu.SemaphoreType.DMA((2,)),
        ]

    def bind(self, source, whole, send, receive, local, send_on, receive_on):
        self.source, self.whole, self.local = source, whole, local
        self.send, self.receive, self.send_on, self.receive_on = send, receive, send_on, receive_on
        self.here, along_x, along_y, self.far = shard_places()
        self.near = (along_x, along_y)
        self.kept, self.sent = [], []

    def block(self, place, start, rows):
        return pl.ds(pl.multiple_of(place * self.rows + start, 16), rows)

    def post(self):
        for j, (row, column, wide, into) in enumerate(self.pieces()):
            piece = self.source.at[pl.ds(row, self.rows), pl.ds(column, wide)]
            target = self.whole.at[self.block(self.here, 0, self.rows), pl.ds(into, wide)]
            self.kept.append(pltpu.make_async_copy(piece, target, self.local.at[j]))
            self.kept[-1].start()
            for hop, place in enumerate(self.near):
                self.push(piece, target, self.send.at[j, hop], self.receive.at[j, hop], place)

    def push(self, source, target, send, receive, place):
        self.sent.append(to_device("shard", source, target, send, receive, place))
        self.sent[-1].start()

    def pass_on(self):
        half = self.rows // 2
        for j, (_, _, wide, into) in enumerate(self.pieces()):
            for hop, place in enumerate(self.near):
                came = self.whole.at[self.block(place, 0, self.rows), pl.ds(into, wide)]
                to_device(
                    "shard", came, came, self.send.at[j, hop], self.receive.at[j, hop], place
                ).wait_recv()
        for hop in range(2):
            part = self.whole.at[self.block(self.near[1 - hop], hop * half, half)]
            self.push(part, part, self.send_on.at[hop], self.receive_on.at[hop], self.near[hop])

    def finish(self):
        half = self.rows // 2
        for hop in range(2):
            came = self.whole.at[self.block(self.far, hop * half, half)]
            to_device(
                "shard", came, came, self.send_on.at[hop], self.receive_on.at[hop], self.near[hop]
            ).wait_recv()
        for copy in self.kept:
            copy.wait()

    def close(self):
        for copy in self.sent:
            copy.wait_send()


class Spread:
    def __init__(self, chips):
        self.chips = chips

    def scratch(self):
        return [pltpu.SemaphoreType.DMA((self.chips,))] * 4 + [pltpu.SemaphoreType.DMA]

    def bind(self, own, group, send, receive, send_on, receive_on, local):
        self.own, self.group, self.local = own, group, local
        self.send, self.receive, self.send_on, self.receive_on = send, receive, send_on, receive_on
        self.me = lax.axis_index("context")
        self.chip, self.core = self.me // 2, lax.rem(self.me, 2)
        self.mate = self.me + 1 - 2 * self.core
        self.sent = []

    def push(self, source, target, send, receive, place):
        self.sent.append(to_device("context", source, target, send, receive, place))
        self.sent[-1].start()

    def came(self, k, core):
        return 2 * lax.rem(self.chip + self.chips - k, self.chips) + core

    def post(self):
        self.kept = pltpu.make_async_copy(self.own, self.group.at[self.me], self.local)
        self.kept.start()
        for k in range(1, self.chips):
            place = 2 * lax.rem(self.chip + k, self.chips) + self.core
            self.push(self.own, self.group.at[self.me], self.send.at[k], self.receive.at[k], place)
        self.push(
            self.own, self.group.at[self.me], self.send_on.at[0], self.receive_on.at[0], self.mate
        )

    def pass_on(self):
        for k in range(1, self.chips):
            block = self.group.at[self.came(k, self.core)]
            to_device(
                "context", block, block, self.send.at[k], self.receive.at[k], self.mate
            ).wait_recv()
            self.push(block, block, self.send_on.at[k], self.receive_on.at[k], self.mate)

    def finish(self):
        self.kept.wait()
        for k in range(self.chips):
            block = self.group.at[self.came(k, 1 - self.core)]
            to_device(
                "context", block, block, self.send_on.at[k], self.receive_on.at[k], self.mate
            ).wait_recv()
        for copy in self.sent:
            copy.wait_send()


def opening_kernel(gathers, spreads, *refs):
    refs = list(refs)

    def take(count):
        taken = refs[:count]
        del refs[:count]
        return taken

    sources = take(len(gathers) - 1)
    vector_refs = take(5)
    source_ref, mask_ref, cosine_ref, sine_ref = take(4)
    wholes = take(len(gathers))
    queries_ref, keyval_ref, resid_ref = take(3)
    groups = take(3)
    pair, attn, small, big, keyval, mixed, mixed_own, feed_own, out, out_came = take(10)
    vectors, vectors_own = take(2)
    swap_send, swap_receive, load, keyval_send, keyval_receive = take(5)
    for gather_of, source, whole in zip(gathers, [vectors_own] + sources, wholes):
        gather_of.bind(source, whole, *take(5))
    me, contexts = lax.axis_index("context"), lax.axis_size("context")
    chip, core = me // 2, lax.rem(me, 2)
    mate = me + 1 - 2 * core
    tok, model = source_ref.shape
    rows = 2 * tok
    attn_own = attn.at[pl.ds(pl.multiple_of(core * tok, tok), tok)]
    for spread, own, group in zip(spreads, (mixed_own, feed_own, attn_own), groups):
        spread.bind(own, group, *take(5))
    half = model // 2
    others = [lax.rem(me + k, contexts) for k in range(1, contexts)]
    vectors_own[...] = jnp.zeros_like(vectors_own)
    row, across_row = 0, vectors_own.shape[1]
    for ref in vector_refs:
        for start in range(0, ref.shape[1], across_row):
            vectors_own[row : row + 1, :] = ref[:, start : start + across_row]
            row += 1
    greet(gathers[0].near, others)
    vector_of, keyval_of, query_of, output_of, gate_up_of, down_of = gathers
    swaps = []

    def swap(step, source, target):
        swaps.append(
            to_device("context", source, target, swap_send.at[step], swap_receive.at[step], mate)
        )
        swaps[-1].start()

    def fetch(step, whole, target):
        copy = pltpu.make_async_copy(whole, target, load.at[step])
        copy.start()
        copy.wait()

    keyval_of.post()
    vector_of.post()
    query_of.post()
    pair[core] = source_ref[...]
    swap(0, source_ref, pair.at[core])

    vector_of.pass_on()
    vector_of.finish()
    fetch(0, vector_of.whole, vectors)

    def vector(row):
        tall = vector_of.rows
        return jnp.concatenate(
            [vectors[j * tall + row : j * tall + row + 1, :] for j in range(4)], axis=1
        ).astype(jnp.float32)

    swaps[0].wait_recv()
    attn[...] = rms_norm(
        pair[...].reshape(rows, model).astype(jnp.float32), vector(0)
    ).astype(jnp.bfloat16)

    keyval_of.pass_on()
    keyval_of.finish()
    fetch(1, keyval_of.whole, small)
    cosine, sine = cosine_ref[...], sine_ref[...]

    def turned(field):
        return field * cosine + pltpu.roll(field, DH // 4, 1) * sine

    raw = jnp.dot(attn[...], small[...], preferred_element_type=jnp.float32)
    at = pl.ds(pl.multiple_of(chip * rows, rows), rows)
    keyval[core, at, : DH // 2] = jnp.where(
        core == 0, turned(raw[:, : DH // 2]), raw[:, : DH // 2]
    ).astype(jnp.bfloat16)
    keyval[core, at, DH // 2 :] = raw[:, DH // 2 :].astype(jnp.bfloat16)
    keyval_sent = []
    for k in range(1, contexts):
        block = keyval.at[core, at]
        keyval_sent.append(
            to_device(
                "context", block, block, keyval_send.at[k], keyval_receive.at[k], others[k - 1]
            )
        )
        keyval_sent[-1].start()

    query_of.pass_on()
    query_of.finish()
    output_of.post()
    fetch(2, query_of.whole, big)
    heads = half // DH
    for h in range(heads):
        raw = jnp.dot(
            attn[...], big[:, h * DH : (h + 1) * DH], preferred_element_type=jnp.float32
        ) * DH ** (-0.5)
        queries_ref[:, h * DH : h * DH + DH // 2] = turned(raw[:, : DH // 2]).astype(jnp.bfloat16)
        queries_ref[:, h * DH + DH // 2 : (h + 1) * DH] = raw[:, DH // 2 :].astype(jnp.bfloat16)
    for k in range(1, contexts):
        place = lax.rem(me + contexts - k, contexts)
        block = keyval.at[
            lax.rem(place, 2), pl.ds(pl.multiple_of((place // 2) * rows, rows), rows)
        ]
        to_device(
            "context", block, block, keyval_send.at[k], keyval_receive.at[k], others[k - 1]
        ).wait_recv()
    spreads[2].post()
    for h in range(heads):
        weights = masked_weights(queries_ref[:, h * DH : (h + 1) * DH], keyval[0], mask_ref[...])
        mixed[core, :, h * DH : (h + 1) * DH] = jnp.dot(
            weights.astype(jnp.bfloat16), keyval[1], preferred_element_type=jnp.float32
        ).astype(jnp.bfloat16)
    swap(1, mixed.at[core], mixed.at[core])

    output_of.pass_on()
    output_of.finish()
    gate_up_of.post()
    down_of.post()
    fetch(3, output_of.whole, big)
    swaps[1].wait_recv()
    out[...] = jnp.dot(mixed[0], big[:half], preferred_element_type=jnp.float32) + jnp.dot(
        mixed[1], big[half:], preferred_element_type=jnp.float32
    )
    mine = pl.ds(pl.multiple_of(core * tok, tok), tok)
    theirs = pl.ds(pl.multiple_of((1 - core) * tok, tok), tok)
    swap(2, out.at[theirs], out_came)
    mixed_own[:, :half] = mixed[0, mine]
    mixed_own[:, half:] = mixed[1, mine]
    swaps[2].wait_recv()
    low = jnp.where(core == 0, out[mine], out_came[...])
    high = jnp.where(core == 0, out_came[...], out[mine])
    resid = (
        source_ref[...].astype(jnp.float32) + jnp.concatenate([low, high], axis=1) + vector(1)
    )
    resid_ref[...] = resid
    feed_own[...] = rms_norm(resid, vector(2)).astype(jnp.bfloat16)
    spreads[1].post()
    spreads[0].post()
    spreads[2].pass_on()
    keyval_ref[...] = keyval[...]
    gate_up_of.pass_on()
    down_of.pass_on()
    spreads[1].pass_on()
    spreads[0].pass_on()
    for part in spreads:
        part.finish()
    gate_up_of.finish()
    down_of.finish()
    for gather_of in gathers:
        gather_of.close()
    for copy in swaps + keyval_sent:
        copy.wait_send()


def opening(number, cuts, vectors, source, mask, cosine, sine):
    contexts = lax.axis_size("context")
    tok, model = source.shape
    slots = mask.shape[1]
    half = model // 2
    gathers = [Gather(rows, pieces) for _, rows, pieces, _ in cuts]
    spreads = [Spread(contexts // 2) for _ in range(3)]
    low, full = jnp.bfloat16, jnp.float32
    dma = pltpu.SemaphoreType.DMA
    tall, wide = cuts[0][1], cuts[0][3]
    outs = pl.pallas_call(
        functools.partial(opening_kernel, gathers, spreads),
        in_specs=[pl.BlockSpec(memory_space=pl.ANY)] * (len(cuts) - 1)
        + [pl.BlockSpec(memory_space=pltpu.VMEM)] * 9,
        out_specs=[pl.BlockSpec(memory_space=pl.ANY)] * len(cuts)
        + [pl.BlockSpec(memory_space=pltpu.VMEM)] * 3
        + [pl.BlockSpec(memory_space=pl.ANY)] * 3,
        out_shape=[jax.ShapeDtypeStruct((4 * rows, columns), low) for _, rows, _, columns in cuts]
        + [
            jax.ShapeDtypeStruct((2 * tok, half), low),
            jax.ShapeDtypeStruct((2, slots, DH), low),
            jax.ShapeDtypeStruct((tok, model), full),
        ]
        + [jax.ShapeDtypeStruct((contexts, tok, model), low)] * 3,
        scratch_shapes=[
            pltpu.VMEM((2, tok, model), low),
            pltpu.VMEM((2 * tok, model), low),
            pltpu.VMEM((model, cuts[1][3]), low),
            pltpu.VMEM((model, half), low),
            pltpu.VMEM((2, slots, DH), low),
            pltpu.VMEM((2, 2 * tok, half), low),
            pltpu.VMEM((tok, model), low),
            pltpu.VMEM((tok, model), low),
            pltpu.VMEM((2 * tok, half), full),
            pltpu.VMEM((tok, half), full),
            pltpu.VMEM((4 * tall, wide), low),
            pltpu.VMEM((tall, wide), low),
            dma((3,)),
            dma((3,)),
            dma((4,)),
            dma((contexts,)),
            dma((contexts,)),
        ]
        + [shape for part in gathers + spreads for shape in part.scratch()],
        cost_estimate=pl.CostEstimate(flops=0, transcendentals=0, bytes_accessed=700_000_000),
        compiler_params=pltpu.CompilerParams(
            collective_id=number, has_side_effects=True, vmem_limit_bytes=VMEM_LIMIT
        ),
    )(*[array for array, _, _, _ in cuts[1:]], *vectors, source, mask, cosine, sine)
    return outs[: len(cuts)], outs[len(cuts) :]


class Product:
    def __init__(self, left, right):
        self.rows, self.wide = left[1] // 4, right[1]
        half = -(-self.wide // (2 * LANES)) * LANES
        self.sides = ((0, half), (half, self.wide - half))

    def buffers(self):
        return [pltpu.VMEM((3, self.rows, wide), jnp.bfloat16) for _, wide in self.sides]

    def scratch(self):
        return self.buffers() + self.buffers() + [pltpu.SemaphoreType.DMA((6,))] * 2

    def bind(self, left, right, made_a, made_b, came_a, came_b, send, receive):
        self.left, self.right, self.send, self.receive = left, right, send, receive
        self.made, self.came = (made_a, made_b), (came_a, came_b)
        self.here, along_x, along_y, self.far = shard_places()
        self.ways = ((along_x, along_y), (along_y, along_x))
        self.columns = [pl.ds(start, wide) for start, wide in self.sides]
        self.copies = []

    def product(self, place, side):
        block = pl.ds(pl.multiple_of(place * self.rows, LANES), self.rows)
        return over_rows(self.left[:, block], self.right[:, self.columns[side]])

    def push(self, step, side, place):
        slot = 2 * step + side
        self.copies.append(
            to_device(
                "shard",
                self.made[side].at[step],
                self.came[side].at[step],
                self.send.at[slot],
                self.receive.at[slot],
                place,
            )
        )
        self.copies[-1].start()

    def begin(self):
        for side in range(2):
            self.made[side][0] = self.product(self.far, side).astype(jnp.bfloat16)
            self.push(0, side, self.ways[side][0])
        for side in range(2):
            self.made[side][1] = self.product(self.ways[side][0], side).astype(jnp.bfloat16)
            self.push(1, side, self.ways[side][0])

    def middle(self):
        for side in range(2):
            kept = self.product(self.ways[side][1], side)
            self.copies[side].wait_recv()
            self.made[side][2] = (kept + self.came[side][0].astype(jnp.float32)).astype(
                jnp.bfloat16
            )
            self.push(2, side, self.ways[side][1])

    def finish(self, out):
        for side in range(2):
            total = self.product(self.here, side)
            self.copies[2 + side].wait_recv()
            total = total + self.came[side][1].astype(jnp.float32)
            self.copies[4 + side].wait_recv()
            out[:, self.columns[side]] = (
                total + self.came[side][2].astype(jnp.float32)
            ).astype(jnp.bfloat16)

    def drain(self, first, last):
        for copy in self.copies[first:last]:
            copy.wait_send()


class Exchange:
    def __init__(self, count, stride):
        self.count, self.stride = count, stride

    def scratch(self):
        return [pltpu.SemaphoreType.DMA((self.count,))] * 2 + [pltpu.SemaphoreType.DMA]

    def peers(self):
        me = lax.axis_index("context")
        slot, rest = me // self.stride, lax.rem(me, self.stride)
        places = [lax.rem(slot + k, self.count) for k in range(self.count)]
        return places, [place * self.stride + rest for place in places]

    def start(self, blocks, out, send, receive, local):
        slots, devices = self.peers()
        kept = pltpu.make_async_copy(blocks(slots[0]), out.at[slots[0]], local)
        kept.start()
        copies = []
        for k in range(1, self.count):
            copies.append(
                to_device(
                    "context", blocks(slots[k]), out.at[slots[0]], send.at[k], receive.at[k], devices[k]
                )
            )
            copies[-1].start()

        def finish():
            kept.wait()
            for k in range(1, self.count):
                source = slots[self.count - k]
                to_device(
                    "context", out.at[source], out.at[source], send.at[k], receive.at[k], devices[k]
                ).wait_recv()
            for copy in copies:
                copy.wait_send()

        return finish


def work_kernel(products, exchanges, chained, summed, *refs):
    refs = list(refs)

    def take(count):
        taken = refs[:count]
        del refs[:count]
        return taken

    operands = [take(2) for _ in products]
    arrays = take(len(exchanges) - (1 if chained else 0))
    results = take(len(products))
    moved = take(len(exchanges))
    total_ref = take(1)[0] if summed else None
    product_scratch = [take(len(p.scratch())) for p in products]
    exchange_scratch = [take(len(e.scratch())) for e in exchanges]
    _, along_x, along_y, _ = shard_places()
    if summed:
        arrived, stage, stage_came, stage_send, stage_receive = take(5)
    everyone = max(exchanges, key=lambda e: e.count).peers()[1][1:] if exchanges else []
    greet((along_x, along_y), everyone)
    finishes, steps = [], []
    if summed:
        moved = [arrived] + moved[1:]

    def hop(step, place):
        steps.append(
            to_device(
                "shard",
                stage.at[step],
                stage_came.at[step],
                stage_send.at[step],
                stage_receive.at[step],
                place,
            )
        )
        steps[-1].start()

    for exchange, array, out, scratch in zip(exchanges, arrays, moved, exchange_scratch):
        finishes.append(exchange.start(lambda j, array=array: array.at[j], out, *scratch))
    for product, (left, right), scratch in zip(products, operands, product_scratch):
        product.bind(left, right, *scratch)
        product.begin()
    if summed:
        finishes.pop(0)()
        stage[0] = jnp.sum(arrived[...], axis=0)
        hop(0, along_x)
    for product in products:
        product.middle()
    if summed:
        steps[0].wait_recv()
        stage[1] = stage[0] + stage_came[0]
        hop(1, along_y)
    for i, product in enumerate(products):
        product.finish(results[i])
        if chained and i == 0:
            rows = product.rows // exchanges[-1].count
            finishes.append(
                exchanges[-1].start(
                    lambda j: results[0].at[pl.ds(pl.multiple_of(j * rows, 16), rows)],
                    moved[-1],
                    *exchange_scratch[-1],
                )
            )
    if summed:
        steps[1].wait_recv()
        total_ref[...] = stage[1] + stage_came[1]
    for product in products:
        product.drain(0, 6)
    for step in steps:
        step.wait_send()
    for finish in finishes:
        finish()


def work(number, products=(), exchanges=(), chained=False, summed=False):
    contexts = lax.axis_size("context")
    made = [Product(left.shape, right.shape) for left, right in products]
    swaps = [Exchange(array.shape[0], contexts // array.shape[0]) for array in exchanges]
    results = [jax.ShapeDtypeStruct((p.rows, p.wide), jnp.bfloat16) for p in made]
    moved = [jax.ShapeDtypeStruct(array.shape, array.dtype) for array in exchanges]
    if chained:
        swaps.append(Exchange(contexts, 1))
        moved.append(
            jax.ShapeDtypeStruct((contexts, made[0].rows // contexts, made[0].wide), jnp.bfloat16)
        )
    scratch = [shape for part in made + swaps for shape in part.scratch()]
    totals = []
    if summed:
        block = exchanges[0].shape[1:]
        totals = [jax.ShapeDtypeStruct(block, jnp.float32)]
        moved[0] = jax.ShapeDtypeStruct((8, LANES), jnp.float32)
        scratch += [
            pltpu.VMEM(exchanges[0].shape, jnp.float32),
            pltpu.VMEM((2, *block), jnp.float32),
            pltpu.VMEM((2, *block), jnp.float32),
            pltpu.SemaphoreType.DMA((2,)),
            pltpu.SemaphoreType.DMA((2,)),
        ]
    vmem = pl.BlockSpec(memory_space=pltpu.VMEM)
    hbm = pl.BlockSpec(memory_space=pl.ANY)
    outs = pl.pallas_call(
        functools.partial(work_kernel, made, swaps, chained, summed),
        in_specs=[vmem] * (2 * len(made)) + [hbm] * len(exchanges),
        out_specs=[vmem] * len(made) + [hbm] * len(swaps) + [vmem] * len(totals),
        out_shape=results + moved + totals,
        scratch_shapes=scratch,
        cost_estimate=pl.CostEstimate(flops=0, transcendentals=0, bytes_accessed=150_000_000),
        compiler_params=pltpu.CompilerParams(
            collective_id=number, has_side_effects=True, vmem_limit_bytes=VMEM_LIMIT
        ),
    )(*[operand for pair in products for operand in pair], *exchanges)
    others = outs[len(made) :]
    if summed:
        others = [others[-1], *others[1:-1]]
    return outs[1 if chained else 0 : len(made)], others


def norm_back(field, gain, grad):
    scale = lax.rsqrt(jnp.mean(field * field, axis=1, keepdims=True) + EPS)
    normed = field * scale
    bent = grad * gain
    back = scale * (bent - normed * jnp.mean(bent * normed, axis=1, keepdims=True))
    return back, jnp.sum(grad * normed, axis=0, keepdims=True)


def back_kernel(gate, up, swaps, *refs):
    refs = list(refs)

    def take(count):
        taken = refs[:count]
        del refs[:count]
        return taken

    output_ref, query_ref, keyval_ref, feed_ref, gate_ref, up_ref, down_ref = take(7)
    grad_ref, resid_ref, cotangent_ref, source_ref, gains_ref = take(5)
    queries_ref, keyval_of, mask_ref, cosine_ref, sine_ref = take(5)
    input_grad_ref, sums_ref, up_out, rows_out, back_out, down_out, gate_out = take(7)
    left, gate_right, up_right, big, small = take(5)
    own_grad, swapped, part, part_came, tail_came, mixed_back, query_back = take(7)
    pieces, pieces_mate, pieces_low, pieces_came = take(4)
    keyval_back, rows_blocks, back_blocks, gate_sum = take(4)
    load, mate_send, mate_receive = take(3)
    made = take(2)
    gate_scratch, up_scratch = take(4), take(4)
    rows_swap, back_swap, down_swap, gate_swap, piece_swap = swaps
    rows_sems, back_sems, down_sems, gate_sems, piece_sems = (take(3) for _ in swaps)
    me = lax.axis_index("context")
    chip, core = me // 2, lax.rem(me, 2)
    mate = me + 1 - 2 * core
    tok, model = resid_ref.shape
    half = model // 2
    rows = 2 * tok
    shards = lax.axis_size("shard")
    contexts = lax.axis_size("context")
    owned = model // (shards * contexts)
    mine = pl.ds(pl.multiple_of(core * tok, tok), tok)
    theirs = pl.ds(pl.multiple_of((1 - core) * tok, tok), tok)
    full = jnp.float32
    loads = []

    def fetch(source, target):
        loads.append(pltpu.make_async_copy(source, target, load.at[len(loads)]))
        loads[-1].start()
        return loads[-1]

    mates = []

    def to_mate(source, target):
        step = len(mates)
        mates.append(
            to_device("context", source, target, mate_send.at[step], mate_receive.at[step], mate)
        )
        mates[-1].start()
        return mates[-1]

    left_load, gate_load = fetch(feed_ref, left), fetch(gate_ref, gate_right)
    output_load, up_load = fetch(output_ref, big), fetch(up_ref, up_right)
    small_load = fetch(keyval_ref, small)
    _, along_x, along_y, _ = shard_places()
    greet((along_x, along_y), rows_swap.peers()[1][1:])
    finishes = [down_swap.start(lambda j: down_ref.at[j], down_out, *down_sems)]

    resid = resid_ref[...]
    cotangent = cotangent_ref[...].astype(full)
    resid_part, gain_two_grad = norm_back(resid, gains_ref[1:2], grad_ref[...])
    resid_grad = cotangent + resid_part
    input_grad_ref[...] = resid_grad
    attn_grad = resid_grad.astype(jnp.bfloat16)
    own_grad[...] = attn_grad
    swapped[core] = own_grad[:, pl.ds(pl.multiple_of(core * half, LANES), half)]
    first = to_mate(
        own_grad.at[:, pl.ds(pl.multiple_of((1 - core) * half, LANES), half)], swapped.at[core]
    )
    left_load.wait()
    gate_load.wait()
    gate.bind(left, gate_right, *made, *gate_scratch)
    gate.begin()
    sums_ref[...] = jnp.zeros_like(sums_ref)
    sums_ref[1:2] = jnp.sum(attn_grad.astype(full), axis=0, keepdims=True)
    sums_ref[2:3] = gain_two_grad
    sums_ref[3:4] = jnp.sum(cotangent, axis=0, keepdims=True)
    wide = rows_blocks.shape[2] // shards
    rows_blocks[...] = jnp.zeros_like(rows_blocks)
    for j in range(contexts):
        for shard in range(shards):
            start = (shard * contexts + j) * owned
            rows_blocks[j, :, shard * wide : shard * wide + owned] = attn_grad[
                :, start : start + owned
            ]
    finishes.append(rows_swap.start(lambda j: rows_blocks.at[j], rows_out, *rows_sems))

    first.wait_recv()
    output_load.wait()
    pair_grad = swapped[...].reshape(rows, half)
    for side in range(2):
        part[side] = against(pair_grad, big[side * half : (side + 1) * half])
    second = to_mate(part.at[1 - core], part_came)
    query_load = fetch(query_ref, big)
    second.wait_recv()
    mixed_back[...] = (part[core] + part_came[...]).astype(jnp.bfloat16)
    cosine, sine = cosine_ref[...], sine_ref[...]

    def unturned(field):
        return field * cosine - pltpu.roll(field, DH // 4, 1) * sine

    keys, values = keyval_of[0], keyval_of[1]
    for h in range(half // DH):
        at = slice(h * DH, (h + 1) * DH)
        queries, grad = queries_ref[:, at], mixed_back[:, at]
        weights = masked_weights(queries, keys, mask_ref[...])
        value_score = against(grad, values)
        delta = jnp.sum(weights * value_score, axis=1, keepdims=True)
        score_back = (weights * (value_score - delta)).astype(jnp.bfloat16)
        back = jnp.dot(score_back, keys, preferred_element_type=full) * DH ** (-0.5)
        query_back[:, h * DH : h * DH + DH // 2] = unturned(back[:, : DH // 2]).astype(jnp.bfloat16)
        query_back[:, h * DH + DH // 2 : (h + 1) * DH] = back[:, DH // 2 :].astype(jnp.bfloat16)
        key_piece = over_rows(score_back, queries)
        value_piece = over_rows(weights.astype(jnp.bfloat16), grad)
        if h == 0:
            pieces[0], pieces[1] = key_piece, value_piece
        else:
            pieces[0] += key_piece
            pieces[1] += value_piece
    fourth = to_mate(pieces.at[1 - core], pieces_mate)
    gate.middle()
    fourth.wait_recv()
    pieces_low[...] = (pieces[core] + pieces_mate[...]).astype(jnp.bfloat16)
    pieces_done = piece_swap.start(
        lambda j: pieces_low.at[pl.ds(pl.multiple_of(j * rows, rows), rows)],
        pieces_came,
        *piece_sems,
    )

    gate.drain(0, 4)
    up_load.wait()
    up.bind(left, up_right, *made, *up_scratch)
    up.begin()
    gate.finish(gate_sum)
    tall = gate.rows // contexts
    finishes.append(
        gate_swap.start(
            lambda j: gate_sum.at[pl.ds(pl.multiple_of(j * tall, 16), tall)], gate_out, *gate_sems
        )
    )

    pieces_done()
    total = jnp.sum(pieces_came[...].astype(full), axis=0)
    keyval_back[:, : DH // 2] = jnp.where(
        core == 0, unturned(total[:, : DH // 2]), total[:, : DH // 2]
    ).astype(jnp.bfloat16)
    keyval_back[:, DH // 2 :] = total[:, DH // 2 :].astype(jnp.bfloat16)
    chips = contexts // 2
    head_part, keyval_part = half // chips, DH // chips
    back_blocks[...] = jnp.zeros_like(back_blocks)
    for j in range(chips):
        back_blocks[j, :, :head_part] = query_back[:, j * head_part : (j + 1) * head_part]
        back_blocks[j, :, head_part : head_part + keyval_part] = keyval_back[
            :, j * keyval_part : (j + 1) * keyval_part
        ]
    finishes.append(back_swap.start(lambda j: back_blocks.at[j], back_out, *back_sems))
    query_load.wait()
    small_load.wait()
    second.wait_send()
    for side in range(2):
        at = slice(side * half, (side + 1) * half)
        part[side] = against(query_back[...], big[at]) + against(keyval_back[...], small[at])
    third = [to_mate(part.at[side, theirs], tail_came.at[side]) for side in range(2)]
    gate.drain(4, 6)
    up.middle()
    for copy in third:
        copy.wait_recv()
    attn_in_grad = jnp.concatenate([part[side, mine] + tail_came[side] for side in range(2)], axis=1)
    input_part, gain_one_grad = norm_back(
        source_ref[...].astype(full), gains_ref[0:1], attn_in_grad
    )
    input_grad_ref[...] += input_part
    sums_ref[0:1] = gain_one_grad
    up.finish(up_out)
    up.drain(0, 6)
    for copy in [first, fourth] + third:
        copy.wait_send()
    for finish in finishes:
        finish()


def back(number, weights, feed_group, gate_back, up_back, down_rows, tokens, attention):
    contexts, shards = lax.axis_size("context"), lax.axis_size("shard")
    tok, model = tokens[1].shape
    slots = attention[2].shape[1]
    half, rows, chips = model // 2, 2 * tok, contexts // 2
    owned = model // (shards * contexts)
    wide = -(-owned // LANES) * LANES
    gate = Product(feed_group.shape, gate_back.shape)
    up = Product(feed_group.shape, up_back.shape)
    cols = max(half // chips + DH // chips, 2 * LANES)
    low, full = jnp.bfloat16, jnp.float32
    shape = jax.ShapeDtypeStruct
    swaps = [Exchange(n, contexts // n) for n in (contexts, chips, contexts, contexts, chips)]
    tall = gate.rows // contexts
    vmem, hbm = pl.BlockSpec(memory_space=pltpu.VMEM), pl.BlockSpec(memory_space=pl.ANY)
    dma = pltpu.SemaphoreType.DMA
    return pl.pallas_call(
        functools.partial(back_kernel, gate, up, swaps),
        in_specs=[hbm] * 7 + [vmem] * 10,
        out_specs=[vmem] * 3 + [hbm] * 4,
        out_shape=[
            shape((tok, model), full),
            shape((8, model), full),
            shape((up.rows, up.wide), low),
            shape((contexts, tok, shards * wide), low),
            shape((chips, rows, cols), low),
            shape(down_rows.shape, low),
            shape((contexts, tall, gate.wide), low),
        ],
        scratch_shapes=[
            pltpu.VMEM(feed_group.shape, low),
            pltpu.VMEM(gate_back.shape, low),
            pltpu.VMEM(up_back.shape, low),
            pltpu.VMEM((model, half), low),
            pltpu.VMEM((model, DH), low),
            pltpu.VMEM((tok, model), low),
            pltpu.VMEM((2, tok, half), low),
            pltpu.VMEM((2, rows, half), full),
            pltpu.VMEM((rows, half), full),
            pltpu.VMEM((2, tok, half), full),
            pltpu.VMEM((rows, half), low),
            pltpu.VMEM((rows, half), low),
            pltpu.VMEM((2, slots, DH), full),
            pltpu.VMEM((slots, DH), full),
            pltpu.VMEM((slots, DH), low),
            pltpu.VMEM((chips, rows, DH), low),
            pltpu.VMEM((rows, DH), low),
            pltpu.VMEM((contexts, tok, shards * wide), low),
            pltpu.VMEM((chips, rows, cols), low),
            pltpu.VMEM((gate.rows, gate.wide), low),
            dma((6,)),
            dma((5,)),
            dma((5,)),
        ]
        + gate.buffers()
        + (gate.buffers() + [dma((6,))] * 2)
        + (up.buffers() + [dma((6,))] * 2)
        + [each for swap in swaps for each in swap.scratch()],
        cost_estimate=pl.CostEstimate(flops=0, transcendentals=0, bytes_accessed=400_000_000),
        compiler_params=pltpu.CompilerParams(
            collective_id=number, has_side_effects=True, vmem_limit_bytes=BACK_LIMIT
        ),
    )(*weights, feed_group, gate_back, up_back, down_rows, *tokens, *attention)


def masked_weights(q, k, mask):
    scores = lax.dot_general(q, k, (((1,), (1,)), ((), ())), preferred_element_type=jnp.float32)
    scores = jnp.where(mask > 0.0, scores, NEG)
    raised = jnp.exp(scores - jnp.max(scores, axis=1, keepdims=True))
    return raised / jnp.sum(raised, axis=1, keepdims=True)


def mix_back_kernel(mask_ref, q_ref, k_ref, v_ref, g_ref, dq_ref, dk_ref, dv_ref):
    q, k, g = q_ref[...], k_ref[...], g_ref[...]
    weights = masked_weights(q, k, mask_ref[...])
    value_score = against(g, v_ref[...])
    delta = jnp.sum(weights * value_score, axis=1, keepdims=True)
    score_back = (weights * (value_score - delta)).astype(jnp.bfloat16)
    dq_ref[...] = jnp.dot(score_back, k, preferred_element_type=jnp.float32)
    key_piece = over_rows(score_back, q)
    value_piece = over_rows(weights.astype(jnp.bfloat16), g)

    @pl.when(pl.program_id(0) == 0)
    def _():
        dk_ref[...] = key_piece
        dv_ref[...] = value_piece

    @pl.when(pl.program_id(0) > 0)
    def _():
        dk_ref[...] += key_piece
        dv_ref[...] += value_piece


def mix_back(mask, queries, keys, values, grad):
    rows, width = queries.shape
    slots = keys.shape[0]
    whole = lambda h: (0, 0)
    part = lambda h: (0, h)
    return pl.pallas_call(
        mix_back_kernel,
        grid=(width // DH,),
        in_specs=[
            pl.BlockSpec((rows, slots), whole),
            pl.BlockSpec((rows, DH), part),
            pl.BlockSpec((slots, DH), whole),
            pl.BlockSpec((slots, DH), whole),
            pl.BlockSpec((rows, DH), part),
        ],
        out_specs=[
            pl.BlockSpec((rows, DH), part),
            pl.BlockSpec((slots, DH), whole),
            pl.BlockSpec((slots, DH), whole),
        ],
        out_shape=[
            jax.ShapeDtypeStruct((rows, width), jnp.float32),
            jax.ShapeDtypeStruct((slots, DH), jnp.float32),
            jax.ShapeDtypeStruct((slots, DH), jnp.float32),
        ],
        compiler_params=pltpu.CompilerParams(vmem_limit_bytes=VMEM_LIMIT),
    )(mask, queries, keys, values, grad)


def feed_kernel(feed_ref, grad_ref, gate_ref, up_ref, down_ref, bias_gate_ref, bias_up_ref, live_ref,
                hidden_ref, gate_back_ref, up_back_ref, gate_sum_ref, up_sum_ref):
    rows = feed_ref.shape[0]
    step = min(rows, 256)

    @pl.when(pl.program_id(1) == 0)
    def _():
        gate_sum_ref[...] = jnp.zeros_like(gate_sum_ref)
        up_sum_ref[...] = jnp.zeros_like(up_sum_ref)

    def part(i, carry):
        at = pl.ds(pl.multiple_of(i * step, step), step)
        feed = feed_ref[at, :]
        gate = jnp.dot(feed, gate_ref[...], preferred_element_type=jnp.float32) + bias_gate_ref[...]
        up = jnp.dot(feed, up_ref[...], preferred_element_type=jnp.float32) + bias_up_ref[...]
        back = against(grad_ref[at, :], down_ref[...])
        live = live_ref[...]
        square = gate * gate
        bend = jnp.tanh(GELU * gate * (1.0 + CUBE * square))
        half = 0.5 * (1.0 + bend)
        gelu = gate * half * live
        slope = half + 0.5 * gate * (1.0 - bend * bend) * (GELU * (1.0 + 3.0 * CUBE * square))
        hidden_ref[at, :] = (gelu * up).astype(jnp.bfloat16)
        gate_back = (back * up * slope * live).astype(jnp.bfloat16)
        up_back = (back * gelu).astype(jnp.bfloat16)
        gate_back_ref[at, :] = gate_back
        up_back_ref[at, :] = up_back
        gate_sum_ref[...] += jnp.sum(gate_back.astype(jnp.float32), axis=0, keepdims=True)
        up_sum_ref[...] += jnp.sum(up_back.astype(jnp.float32), axis=0, keepdims=True)
        return carry

    lax.fori_loop(0, rows // step, part, 0)


def feed(feed_group, grad_group, gate_up, down, bias, live):
    rows, model = feed_group.shape
    units = down.shape[0]
    wide = min(units, 256)
    blocks = units // wide
    tall = min(rows, 1024)
    buffers = {"pipeline_mode": pl.Buffered(1)} if tall == rows else {}
    tokens = lambda j, i: (i, 0)
    column = lambda j, i: (0, j)
    later = lambda j, i: (0, j + blocks)
    made = lambda j, i: (i, j)
    return pl.pallas_call(
        feed_kernel,
        grid=(blocks, rows // tall),
        in_specs=[
            pl.BlockSpec((tall, model), tokens, **buffers),
            pl.BlockSpec((tall, model), tokens, **buffers),
            pl.BlockSpec((model, wide), column),
            pl.BlockSpec((model, wide), later),
            pl.BlockSpec((wide, model), lambda j, i: (j, 0)),
            pl.BlockSpec((1, wide), column),
            pl.BlockSpec((1, wide), later),
            pl.BlockSpec((1, wide), column),
        ],
        out_specs=[
            pl.BlockSpec((tall, wide), made),
            pl.BlockSpec((tall, wide), made),
            pl.BlockSpec((tall, wide), made),
            pl.BlockSpec((1, wide), column),
            pl.BlockSpec((1, wide), column),
        ],
        out_shape=[
            jax.ShapeDtypeStruct((rows, units), jnp.bfloat16),
            jax.ShapeDtypeStruct((rows, units), jnp.bfloat16),
            jax.ShapeDtypeStruct((rows, units), jnp.bfloat16),
            jax.ShapeDtypeStruct((1, units), jnp.float32),
            jax.ShapeDtypeStruct((1, units), jnp.float32),
        ],
        compiler_params=pltpu.CompilerParams(vmem_limit_bytes=VMEM_LIMIT),
    )(feed_group, grad_group, gate_up, gate_up, down, bias, bias, live)


def middle_kernel(*refs):
    refs = list(refs)

    def take(count):
        taken = refs[:count]
        del refs[:count]
        return taken

    feed_ref, grad_ref, weight_ref, down_ref, bias_ref, live_ref = take(6)
    hidden_ref, gate_back_ref, up_back_ref, sums_ref, down_out_ref, feed_grad_ref = take(6)
    gate_weight, up_weight, down_weight, feed_rows, grad_rows = take(5)
    own_part, mate_out, mate_in, sent_out, came, swap_in = take(6)
    weight_load, row_load, mate_send, mate_receive, send, receive = take(6)
    me = lax.axis_index("context")
    chips = lax.axis_size("context") // 2
    chip, core = me // 2, lax.rem(me, 2)
    mate = me + 1 - 2 * core
    units, model = down_weight.shape
    rows, half, wide = feed_rows.shape[1], model // 2, 256
    blocks = units // wide
    full, low = jnp.float32, jnp.bfloat16
    mine = pl.ds(pl.multiple_of(core * half, LANES), half)
    theirs = pl.ds(pl.multiple_of((1 - core) * half, LANES), half)
    targets = [lax.rem(chip + 1 + i, chips) for i in range(chips)]

    def token_rows(i):
        return pl.ds(pl.multiple_of(targets[i] * rows, rows), rows)

    def weight_loads(j):
        at = pl.ds(pl.multiple_of(j * wide, wide), wide)
        later = pl.ds(pl.multiple_of(units + j * wide, wide), wide)
        return [
            pltpu.make_async_copy(weight_ref.at[:, at], gate_weight.at[:, at], weight_load.at[j, 0]),
            pltpu.make_async_copy(weight_ref.at[:, later], up_weight.at[:, at], weight_load.at[j, 1]),
            pltpu.make_async_copy(down_ref.at[at], down_weight.at[at], weight_load.at[j, 2]),
        ]

    def row_loads(i):
        at = token_rows(i)
        return [
            pltpu.make_async_copy(feed_ref.at[at], feed_rows.at[i % 2], row_load.at[i, 0]),
            pltpu.make_async_copy(grad_ref.at[at], grad_rows.at[i % 2], row_load.at[i, 1]),
        ]

    for copy in row_loads(0):
        copy.start()
    for j in range(blocks):
        for copy in weight_loads(j):
            copy.start()
    greet((), [mate] + [2 * targets[i] + core for i in range(chips - 1)])
    sums_ref[...] = jnp.zeros_like(sums_ref)
    to_mate, to_chips = [], []
    for i in range(chips):
        for copy in row_loads(i):
            copy.wait()
        if i + 1 < chips:
            for copy in row_loads(i + 1):
                copy.start()
        at = token_rows(i)

        def block(j, carry, i=i, at=at):
            if i == 0:
                for copy in weight_loads(j):
                    copy.wait()
            cut = pl.ds(pl.multiple_of(j * wide, wide), wide)
            later = pl.ds(pl.multiple_of(units + j * wide, wide), wide)
            feed = feed_rows[i % 2]
            gate = jnp.dot(feed, gate_weight[:, cut], preferred_element_type=full) + bias_ref[:, cut]
            up = jnp.dot(feed, up_weight[:, cut], preferred_element_type=full) + bias_ref[:, later]
            back = against(grad_rows[i % 2], down_weight[cut])
            live = live_ref[:, cut]
            square = gate * gate
            bend = jnp.tanh(GELU * gate * (1.0 + CUBE * square))
            share = 0.5 * (1.0 + bend)
            gelu = gate * share * live
            slope = share + 0.5 * gate * (1.0 - bend * bend) * (GELU * (1.0 + 3.0 * CUBE * square))
            hidden_ref[at, cut] = (gelu * up).astype(low)
            gate_back = (back * up * slope * live).astype(low)
            up_back = (back * gelu).astype(low)
            gate_back_ref[at, cut] = gate_back
            up_back_ref[at, cut] = up_back
            sums_ref[0:1, cut] += jnp.sum(gate_back.astype(full), axis=0, keepdims=True)
            sums_ref[1:2, cut] += jnp.sum(up_back.astype(full), axis=0, keepdims=True)
            return carry

        lax.fori_loop(0, blocks, block, 0)

        def feed_part(columns):
            return against(gate_back_ref[at, :], gate_weight[columns, :]) + against(
                up_back_ref[at, :], up_weight[columns, :]
            )

        mate_out[i] = feed_part(theirs).astype(low)
        to_mate.append(
            to_device(
                "context", mate_out.at[i], mate_in.at[i], mate_send.at[i], mate_receive.at[i], mate
            )
        )
        to_mate[-1].start()
        own_part[...] = feed_part(mine)
        to_mate[-1].wait_recv()
        if i + 1 < chips:
            sent_out[i] = (own_part[...] + mate_in[i].astype(full)).astype(low)
            to_chips.append(
                to_device(
                    "context",
                    sent_out.at[i],
                    came.at[i],
                    send.at[i],
                    receive.at[i],
                    2 * targets[i] + core,
                )
            )
            to_chips[-1].start()
        else:
            own_part[...] += mate_in[i].astype(full)
        down_out_ref[at, :] = jnp.dot(
            hidden_ref[at, :], down_weight[...], preferred_element_type=full
        ).astype(low)
    for i, copy in enumerate(to_chips):
        copy.wait_recv()
        own_part[...] += came[i].astype(full)
    tok = rows // 2
    own_rows = pl.ds(pl.multiple_of(core * tok, tok), tok)
    mate_rows = pl.ds(pl.multiple_of((1 - core) * tok, tok), tok)
    last = to_device(
        "context",
        own_part.at[mate_rows],
        swap_in,
        mate_send.at[chips],
        mate_receive.at[chips],
        mate,
    )
    last.start()
    feed_grad_ref[:, mine] = own_part[own_rows, :]
    last.wait_recv()
    feed_grad_ref[:, theirs] = swap_in[...]
    for copy in to_mate + to_chips + [last]:
        copy.wait_send()


def middle(number, feed_group, grad_group, gate_up, down, bias, live):
    group, model = feed_group.shape
    units, contexts = down.shape[0], lax.axis_size("context")
    chips, half = contexts // 2, model // 2
    rows = group // chips
    low, full = jnp.bfloat16, jnp.float32
    shape, dma = jax.ShapeDtypeStruct, pltpu.SemaphoreType.DMA
    vmem, hbm = pl.BlockSpec(memory_space=pltpu.VMEM), pl.BlockSpec(memory_space=pl.ANY)
    return pl.pallas_call(
        middle_kernel,
        in_specs=[hbm] * 4 + [vmem] * 2,
        out_specs=[vmem] * 6,
        out_shape=[shape((group, units), low)] * 3
        + [shape((8, units), full), shape((group, model), low), shape((rows // 2, model), full)],
        scratch_shapes=[
            pltpu.VMEM((model, units), low),
            pltpu.VMEM((model, units), low),
            pltpu.VMEM((units, model), low),
            pltpu.VMEM((2, rows, model), low),
            pltpu.VMEM((2, rows, model), low),
            pltpu.VMEM((rows, half), full),
            pltpu.VMEM((chips, rows, half), low),
            pltpu.VMEM((chips, rows, half), low),
            pltpu.VMEM((chips, rows, half), low),
            pltpu.VMEM((chips, rows, half), low),
            pltpu.VMEM((rows // 2, half), full),
            dma((units // 256, 3)),
            dma((chips, 2)),
            dma((chips + 1,)),
            dma((chips + 1,)),
            dma((chips,)),
            dma((chips,)),
        ],
        cost_estimate=pl.CostEstimate(flops=0, transcendentals=0, bytes_accessed=200_000_000),
        compiler_params=pltpu.CompilerParams(
            collective_id=number, has_side_effects=True, vmem_limit_bytes=BACK_LIMIT
        ),
    )(feed_group, grad_group, gate_up, down, bias, live)


def body(
    inputs,
    doc_ids,
    cotangent,
    attn_gain,
    query_weight,
    keyval_weight,
    output_weight,
    output_bias,
    feed_gain,
    gate_up_weight,
    gate_up_bias,
    down_weight,
    down_bias,
):
    tok, model = inputs.shape
    shards, contexts = lax.axis_size("shard"), lax.axis_size("context")
    shard, place = lax.axis_index("shard"), lax.axis_index("context")
    core, chip = place % 2, place // 2
    group = tok * contexts
    owned = model // (shards * contexts)
    ff = gate_up_weight.shape[1] // 2
    width, per_shard = unit_tiles(ff, shards, contexts)
    unit_start = jnp.minimum(place * width, per_shard - width)
    units = shards * width * LANES

    shard_rows = model // shards
    block = width * LANES

    def half_of(wide):
        def pieces():
            column = lax.rem(lax.axis_index("context"), 2) * wide
            return [(0, pl.multiple_of(column, LANES), wide, 0)]

        return pieces

    def first_unit():
        return jnp.minimum(lax.axis_index("context") * width, per_shard - width) * LANES

    def gate_up_pieces():
        return [
            (0, pl.multiple_of(j * per_shard * LANES + first_unit(), LANES), block, j * block)
            for j in range(2 * shards)
        ]

    def down_pieces():
        return [(pl.multiple_of(first_unit(), LANES), 0, model, 0)]

    unit_at = unit_start * LANES + jnp.arange(block, dtype=jnp.int32)
    unit_live = jnp.tile(unit_at >= place * block, shards)[None, :].astype(jnp.float32)
    slots = jnp.arange(group, dtype=jnp.int32)
    pair_slots = chip * (2 * tok) + jnp.arange(2 * tok, dtype=jnp.int32)
    pair_docs = lax.dynamic_slice_in_dim(doc_ids, chip * (2 * tok), 2 * tok)
    distance = pair_slots[:, None] - slots[None, :]
    mask = (
        (pair_docs[:, None] == doc_ids[None, :]) & (distance >= 0) & (distance < WINDOW)
    ).astype(jnp.float32)
    angles = pair_slots.astype(jnp.float32)[:, None] * frequencies(DH)[None, :]
    cosine, sine = jnp.cos(angles), jnp.sin(angles)
    turns = (jnp.concatenate([cosine, cosine], axis=1), jnp.concatenate([-sine, sine], axis=1))
    vectors = [
        each.reshape(1, each.shape[0])
        for each in (attn_gain, output_bias, feed_gain, down_bias, gate_up_bias)
    ]
    vector_rows = 4 + gate_up_bias.shape[0] // shard_rows
    vector_tall = -(-vector_rows // 32) * 32
    core_cols, core_heads = keyval_weight.shape[1] // 2, query_weight.shape[1] // 2
    (vectors, keyval_half, query_half, output_half, gate_up_part, down_part), (
        queries, keyval, resid, mixed_group, feed_group, attn_group
    ) = opening(
        0,
        (
            (None, vector_tall, lambda: [(0, 0, shard_rows, 0)], shard_rows),
            (keyval_weight, shard_rows, half_of(core_cols), core_cols),
            (query_weight, shard_rows, half_of(core_heads), core_heads),
            (output_weight, shard_rows, half_of(model // 2), model // 2),
            (gate_up_weight, shard_rows, gate_up_pieces, 2 * units),
            (down_weight, block, down_pieces, model),
        ),
        vectors,
        inputs,
        mask,
        *turns,
    )
    grad_group = gather(cotangent, "context")
    vectors = vectors.reshape(shards, vector_tall, shard_rows).astype(jnp.float32)
    gain_one, gain_two, bias_down = (vectors[:, i].reshape(1, model) for i in (0, 2, 3))
    bias_gate_up = vectors[:, 4:vector_rows].reshape(2 * shards, per_shard * LANES)
    bias_gate_up = lax.dynamic_slice_in_dim(
        bias_gate_up, unit_start * LANES, block, 1
    ).reshape(1, 2 * units)
    source = inputs.astype(jnp.float32)
    keys, values = keyval[0], keyval[1]
    heads = core_heads // DH
    mixed_group, feed_group, attn_group = (
        field.reshape(group, model) for field in (mixed_group, feed_group, attn_group)
    )

    if group <= 1024:
        hidden, gate_back, up_back, unit_sums, down_part_out, feed_in_grad = middle(
            8,
            feed_group,
            grad_group,
            gate_up_part,
            down_part,
            bias_gate_up,
            unit_live,
        )
        gate_sums, up_sums = unit_sums[0], unit_sums[1]
    else:
        hidden, gate_back, up_back, gate_sums, up_sums = feed(
            feed_group, grad_group, gate_up_part, down_part, bias_gate_up, unit_live
        )
        feed_part = against(
            jnp.concatenate([gate_back, up_back], axis=1), gate_up_part
        ).astype(jnp.bfloat16)
        feed_in_grad = lax.psum_scatter(feed_part, "context", scatter_dimension=0, tiled=True)
        feed_in_grad = feed_in_grad.astype(jnp.float32)
        down_part_out = jnp.dot(hidden, down_part, preferred_element_type=jnp.float32).astype(
            jnp.bfloat16
        )
    down_out = lax.psum_scatter(
        down_part_out, "context", scatter_dimension=0, tiled=True
    ).astype(jnp.float32)
    block_out = (resid + down_out + bias_down).astype(jnp.bfloat16)
    (down_sum,), _ = work(2, [(grad_group, after(hidden, feed_in_grad))])

    chips = contexts // 2
    rows_wide = -(-owned // LANES) * LANES
    head_part, keyval_part = HEADS * DH // contexts, DH // chips

    def by_owners(field):
        return field.reshape(contexts, owned, field.shape[1])

    if group <= 1024:
        gains = jnp.concatenate([gain_one, gain_two, jnp.zeros((6, model), jnp.float32)], axis=0)
        input_grad, sums, up_sum, attn_grad_rows, back_cols, down_rows, gate_rows = back(
            3,
            (output_half, query_half, keyval_half),
            feed_group,
            gate_back,
            up_back,
            by_owners(down_sum),
            (feed_in_grad, resid, cotangent, inputs, gains),
            (queries, keyval, mask, *turns),
        )
        sums = sums[:4].reshape(4 * model)
        attn_grad_rows = attn_grad_rows.reshape(group, shards * rows_wide)
        back_cols = back_cols.reshape(group, back_cols.shape[2])
    else:
        grad_out = cotangent.astype(jnp.float32)
        resid_part, gain_two_grad = jax.vjp(rms_norm, resid, gain_two)[1](feed_in_grad)
        resid_grad = grad_out + resid_part
        attn_grad_low = resid_grad.astype(jnp.bfloat16)
        mixed_back = summed_half(
            against(swap_columns(attn_grad_low, core), output_half), core, 1
        ).astype(jnp.bfloat16)
        query_acc, key_acc, value_acc = mix_back(mask, queries, keys, values, mixed_back)
        keyval_acc = jnp.stack(
            [key_acc.reshape(contexts // 2, 2 * tok, DH), value_acc.reshape(contexts // 2, 2 * tok, DH)],
            axis=1,
        ).reshape(contexts, 2 * tok, DH).astype(jnp.bfloat16)
        attn_grad_rows = jnp.pad(
            attn_grad_low.reshape(tok, shards, contexts, owned).transpose(2, 0, 1, 3),
            ((0, 0), (0, 0), (0, 0), (0, rows_wide - owned)),
        ).reshape(contexts, tok, shards * rows_wide)
        (gate_sum,), (keyval_acc, attn_grad_rows) = work(
            3, [(feed_group, gate_back)], [keyval_acc, attn_grad_rows]
        )
        attn_grad_rows = attn_grad_rows.reshape(group, shards * rows_wide)
        keyval_acc = jnp.sum(keyval_acc.astype(jnp.float32), axis=0)
        keyval_back = jnp.where(core == 0, rotate(keyval_acc, cosine, -sine), keyval_acc).astype(
            jnp.bfloat16
        )
        query_back = (
            rotate(query_acc.reshape(2 * tok, heads, DH), cosine[:, None, :], -sine[:, None, :])
            * DH ** (-0.5)
        ).reshape(2 * tok, heads * DH).astype(jnp.bfloat16)
        attn_in_grad = summed_half(
            against(query_back, query_half) + against(keyval_back, keyval_half), core, 0
        )
        input_part, gain_one_grad = jax.vjp(rms_norm, source, gain_one)[1](attn_in_grad)
        input_grad = resid_grad + input_part

        def by_chips(field):
            return field.reshape(2 * tok, chips, field.shape[1] // chips).transpose(1, 0, 2)

        spare = max(2 * LANES - head_part - keyval_part, 0)
        back_cols = jnp.concatenate([by_chips(query_back), by_chips(keyval_back)], axis=2)
        back_cols = jnp.pad(back_cols, ((0, 0), (0, 0), (0, spare)))
        moving = [back_cols, by_owners(down_sum), by_owners(gate_sum)]
        (up_sum,), (back_cols, down_rows, gate_rows) = work(4, [(feed_group, up_back)], moving)
        back_cols = back_cols.reshape(group, back_cols.shape[2])

        sums = jnp.concatenate(
            [
                gain_one_grad.reshape(model),
                jnp.sum(attn_grad_low.astype(jnp.float32), axis=0),
                gain_two_grad.reshape(model),
                jnp.sum(grad_out, axis=0),
            ]
        )

    sums = jnp.concatenate([sums, gate_sums.reshape(units), up_sums.reshape(units)])
    unit_owned = 2 * ff // (shards * contexts)
    mine = sums[: 4 * model].reshape(4, shards, contexts, owned).transpose(2, 0, 1, 3)
    unit_sums = lax.dynamic_update_slice_in_dim(
        jnp.zeros((2 * shards, per_shard * LANES), jnp.float32),
        sums[4 * model :].reshape(2 * shards, block),
        unit_start * LANES,
        1,
    )
    unit_sums = unit_sums.reshape(shards, contexts, unit_owned).transpose(1, 0, 2)
    at = 4 * shards * owned
    wide = at + shards * unit_owned
    tall = -(-wide // (8 * LANES)) * LANES
    vectors = jnp.concatenate(
        [
            mine.reshape(contexts, at),
            unit_sums.reshape(contexts, wide - at),
            jnp.zeros((contexts, 8 * tall - wide), jnp.float32),
        ],
        axis=1,
    ).reshape(contexts, 8, tall)
    if owned % 16 == 0:
        (output_sum,), (vectors, up_rows, back_rows) = work(
            5,
            [(attn_group, back_cols), (attn_grad_rows, mixed_group)],
            [vectors, by_owners(up_sum)],
            True,
            True,
        )
    else:
        (back_sum,), (vectors, up_rows) = work(
            5, [(attn_group, back_cols)], [vectors, by_owners(up_sum)], False, True
        )
        _, (back_rows,) = work(7, [], [by_owners(back_sum)])
        (output_sum,), _ = work(6, [(attn_grad_rows, mixed_group)])
    vectors = vectors.reshape(8 * tall)
    own = vectors[:at].reshape(4, shards, owned)
    own = lax.dynamic_index_in_dim(own, shard, 1, False)
    gate_up_bias_grad = lax.dynamic_index_in_dim(
        vectors[at:wide].reshape(shards, unit_owned), shard, 0, False
    )
    pieces = unit_pieces(contexts, shards, width, per_shard)
    down_grad, gate_up_grad, query_grad, keyval_grad, output_grad = lay(
        pieces,
        owned,
        (ff, 2 * ff, HEADS * DH, 2 * DH, model),
        down_rows,
        gate_rows,
        up_rows,
        back_rows,
        output_sum,
    )
    output_weight_grad, down_weight_grad = output_grad.T, down_grad.T
    return (
        block_out,
        input_grad,
        own[0],
        query_grad,
        keyval_grad,
        output_weight_grad,
        own[1],
        own[2],
        gate_up_grad,
        gate_up_bias_grad,
        down_weight_grad,
        own[3],
    )


def solution(mesh):
    placed = (
        P(("shard", "context"), None),
        P("shard"),
        P(("shard", "context"), None),
        P("shard"),
        P("shard", None),
        P("shard", None),
        P("shard", None),
        P("shard"),
        P("shard"),
        P("shard", None),
        P("shard"),
        P("shard", None),
        P("shard"),
    )
    return jax.shard_map(
        body,
        mesh=mesh,
        in_specs=placed,
        out_specs=(
            P(("shard", "context"), None),
            P(("shard", "context"), None),
            P(("shard", "context")),
            P(("shard", "context"), None),
            P(("shard", "context"), None),
            P(None, ("shard", "context")),
            P(("shard", "context")),
            P(("shard", "context")),
            P(("shard", "context"), None),
            P(("shard", "context")),
            P(None, ("shard", "context")),
            P(("shard", "context")),
        ),
        check_vma=False,
    )
```

```python
import functools
import math

import jax
import jax.numpy as jnp
from jax import lax
from jax.experimental import pallas as pl
from jax.experimental.pallas import tpu as pltpu
from jax.sharding import PartitionSpec as P

HEADS = 10
DH = 256
FF = 7680
WINDOW = 2048


EPS = 1e-06
NEG = -1e30
ROPE_LOG = math.log(10000.0)


def frequencies(head_dim):
    quarter = head_dim // 4
    steps = jnp.arange(quarter).astype(jnp.float32)
    return jnp.exp(-ROPE_LOG * (2.0 * steps) / (head_dim // 2))


def rotate(field, cosine, sine):
    width = field.shape[-1] // 2
    quarter = width // 2
    first = field[..., :quarter]
    second = field[..., quarter:width]
    return jnp.concatenate(
        [first * cosine - second * sine, second * cosine + first * sine, field[..., width:]],
        axis=-1,
    )


def rms_norm(field, gain):
    return field * lax.rsqrt(jnp.mean(field * field, axis=-1, keepdims=True) + EPS) * gain


def geglu(gate_up):
    half = gate_up.shape[-1] // 2
    return jax.nn.gelu(gate_up[:, :half], approximate=True) * gate_up[:, half:]


def over_rows(left, right):
    return lax.dot_general(
        left, right, (((0,), (0,)), ((), ())), preferred_element_type=jnp.float32
    )


def against(left, weight):
    return lax.dot_general(
        left, weight, (((1,), (1,)), ((), ())), preferred_element_type=jnp.float32
    )


VMEM_LIMIT = 56 * 1024 * 1024
BACK_LIMIT = 61 * 1024 * 1024
LANES = 128
MESH = pl.DeviceIdType.MESH
LINE = (
    ((1, 0), (1, 2), (1, 3)),
    ((2, 1), (0, 4), (2, 3)),
    ((1, 1), (3, 3), (1, 4)),
    ((2, 0), (2, 2), (2, 4)),
)
GELU = 0.7978845608028654
CUBE = 0.044715


def gather(value, axis):
    return lax.all_gather(value, axis, axis=0, tiled=True)


def across(value, bit):
    count = lax.axis_size("shard")
    return lax.ppermute(value, "shard", [(i, i ^ bit) for i in range(count)])


def after(value, *earlier):
    return lax.optimization_barrier((value, *earlier))[0]


def sibling(value):
    count = lax.axis_size("context")
    return lax.ppermute(value, "context", [(i, i ^ 1) for i in range(count)])


def halves(value, core, axis):
    low, high = jnp.split(value, 2, axis=axis)
    return jnp.where(core == 0, low, high), jnp.where(core == 0, high, low)


def swap_rows(value, core):
    mine, theirs = halves(value, core, 0)
    other = sibling(theirs)
    return jnp.where(
        core == 0, jnp.concatenate([mine, other], axis=1), jnp.concatenate([other, mine], axis=1)
    )


def swap_columns(own, core):
    mine, theirs = halves(own, core, 1)
    other = sibling(theirs)
    return jnp.where(
        core == 0, jnp.concatenate([mine, other], axis=0), jnp.concatenate([other, mine], axis=0)
    )


def summed_half(value, core, axis):
    mine, theirs = halves(value, core, axis)
    return mine + sibling(theirs)


def unit_tiles(ff, shards, contexts):
    per_shard = ff // shards // LANES
    return -(-per_shard // contexts), per_shard


def unit_pieces(contexts, shards, width, per_shard):
    found = []
    for at in range(contexts):
        first = at * width
        if first >= per_shard:
            continue
        start, stop = min(first, per_shard - width), min(first + width, per_shard)
        for shard in range(shards):
            found.append(
                (
                    at,
                    (shard * width + first - start) * LANES,
                    (stop - first) * LANES,
                    (shard * per_shard + first) * LANES,
                )
            )
    return found


def lay_kernel(pieces, down_ref, gate_ref, up_ref, back_ref, output_ref, *outs):
    down_leaves, gate_up_leaves, query_out, keyval_out, output_out, down_out, gate_up_out, leave = outs
    units, owned = down_out.shape[1], down_out.shape[0]
    contexts = back_ref.shape[0]
    head_part, keyval_part = query_out.shape[1] // contexts, keyval_out.shape[1] // contexts
    copies = []
    for i, (source, out, leaves, offset) in enumerate(
        (
            (down_ref, down_out, down_leaves, 0),
            (gate_ref, gate_up_out, gate_up_leaves, 0),
            (up_ref, gate_up_out, gate_up_leaves, units),
        )
    ):
        for at, column, wide, first in pieces:
            out[:, offset + first : offset + first + wide] = source[
                at, :, column : column + wide
            ].astype(jnp.float32)
        whole = pl.ds(offset, units)
        copies.append(pltpu.make_async_copy(out.at[:, whole], leaves.at[:, whole], leave.at[i]))
        copies[-1].start()
    for at in range(contexts):
        slot = (at % 2) * (contexts // 2) + at // 2
        part = back_ref[at].astype(jnp.float32)
        query_out[:, slot * head_part : (slot + 1) * head_part] = part[:, :head_part]
        keyval_out[:, slot * keyval_part : (slot + 1) * keyval_part] = part[
            :, head_part : head_part + keyval_part
        ]
    output_out[...] = output_ref[:owned].astype(jnp.float32)
    for copy in copies:
        copy.wait()


def lay(pieces, owned, widths, *fields):
    return pl.pallas_call(
        functools.partial(lay_kernel, pieces),
        in_specs=[pl.BlockSpec(memory_space=pltpu.VMEM)] * len(fields),
        out_specs=[pl.BlockSpec(memory_space=pl.ANY)] * 2
        + [pl.BlockSpec(memory_space=pltpu.VMEM)] * (len(widths) - 2),
        out_shape=[jax.ShapeDtypeStruct((owned, wide), jnp.float32) for wide in widths],
        scratch_shapes=[pltpu.VMEM((owned, wide), jnp.float32) for wide in widths[:2]]
        + [pltpu.SemaphoreType.DMA((3,))],
        compiler_params=pltpu.CompilerParams(vmem_limit_bytes=VMEM_LIMIT),
    )(*fields)


def shard_places():
    here = lax.axis_index("shard")
    return here, here + 1 - 2 * lax.rem(here, 2), lax.rem(here + 2, 4), 3 - here


def greet(shards, contexts=()):
    barrier = pltpu.get_barrier_semaphore()
    for axis, places in (("shard", shards), ("context", contexts)):
        for place in places:
            pl.semaphore_signal(barrier, 1, device_id={axis: place}, device_id_type=MESH)
    pl.semaphore_wait(barrier, len(shards) + len(contexts))


def to_device(axis, source, target, send, receive, place):
    return pltpu.make_async_remote_copy(
        src_ref=source,
        dst_ref=target,
        send_sem=send,
        recv_sem=receive,
        device_id={axis: place},
        device_id_type=MESH,
    )


class Gather:
    def __init__(self, rows, pieces):
        self.rows, self.pieces = rows, pieces

    def scratch(self):
        most = 2 * (len(self.pieces()) // 2) or 1
        return [
            pltpu.SemaphoreType.DMA((most, 2)),
            pltpu.SemaphoreType.DMA((most, 2)),
            pltpu.SemaphoreType.DMA((most,)),
            pltpu.SemaphoreType.DMA((2,)),
            pltpu.SemaphoreType.DMA((2,)),
        ]

    def bind(self, source, whole, send, receive, local, send_on, receive_on):
        self.source, self.whole, self.local = source, whole, local
        self.send, self.receive, self.send_on, self.receive_on = send, receive, send_on, receive_on
        self.here, along_x, along_y, self.far = shard_places()
        self.near = (along_x, along_y)
        self.kept, self.sent = [], []

    def block(self, place, start, rows):
        return pl.ds(pl.multiple_of(place * self.rows + start, 16), rows)

    def post(self):
        for j, (row, column, wide, into) in enumerate(self.pieces()):
            piece = self.source.at[pl.ds(row, self.rows), pl.ds(column, wide)]
            target = self.whole.at[self.block(self.here, 0, self.rows), pl.ds(into, wide)]
            self.kept.append(pltpu.make_async_copy(piece, target, self.local.at[j]))
            self.kept[-1].start()
            for hop, place in enumerate(self.near):
                self.push(piece, target, self.send.at[j, hop], self.receive.at[j, hop], place)

    def push(self, source, target, send, receive, place):
        self.sent.append(to_device("shard", source, target, send, receive, place))
        self.sent[-1].start()

    def pass_on(self):
        half = self.rows // 2
        for j, (_, _, wide, into) in enumerate(self.pieces()):
            for hop, place in enumerate(self.near):
                came = self.whole.at[self.block(place, 0, self.rows), pl.ds(into, wide)]
                to_device(
                    "shard", came, came, self.send.at[j, hop], self.receive.at[j, hop], place
                ).wait_recv()
        for hop in range(2):
            part = self.whole.at[self.block(self.near[1 - hop], hop * half, half)]
            self.push(part, part, self.send_on.at[hop], self.receive_on.at[hop], self.near[hop])

    def finish(self):
        half = self.rows // 2
        for hop in range(2):
            came = self.whole.at[self.block(self.far, hop * half, half)]
            to_device(
                "shard", came, came, self.send_on.at[hop], self.receive_on.at[hop], self.near[hop]
            ).wait_recv()
        for copy in self.kept:
            copy.wait()

    def close(self):
        for copy in self.sent:
            copy.wait_send()


class Spread:
    def __init__(self, chips):
        self.chips = chips

    def scratch(self):
        return [pltpu.SemaphoreType.DMA((self.chips,))] * 4 + [pltpu.SemaphoreType.DMA]

    def bind(self, own, group, send, receive, send_on, receive_on, local):
        self.own, self.group, self.local = own, group, local
        self.send, self.receive, self.send_on, self.receive_on = send, receive, send_on, receive_on
        self.me = lax.axis_index("context")
        self.chip, self.core = self.me // 2, lax.rem(self.me, 2)
        self.mate = self.me + 1 - 2 * self.core
        self.sent = []

    def push(self, source, target, send, receive, place):
        self.sent.append(to_device("context", source, target, send, receive, place))
        self.sent[-1].start()

    def other(self, k):
        if self.chips == 4:
            beside = self.chip + 1 - 2 * lax.rem(self.chip, 2)
            return (self.chip, beside, lax.rem(self.chip + 2, 4), 3 - self.chip)[k]
        return lax.rem(self.chip + self.chips - k, self.chips)

    def to_chip(self, block, k, place):
        self.push(block, block, self.send.at[k], self.receive.at[k], 2 * place + self.core)

    def post(self):
        mine = self.group.at[self.me]
        self.kept = pltpu.make_async_copy(self.own, mine, self.local)
        self.kept.start()
        first = len(self.sent)
        for k in range(1, 3 if self.chips == 4 else self.chips):
            place = self.other(k) if self.chips == 4 else lax.rem(self.chip + k, self.chips)
            self.sent.append(
                to_device(
                    "context",
                    self.own,
                    mine,
                    self.send.at[k],
                    self.receive.at[k],
                    2 * place + self.core,
                )
            )
        posted = self.sent[first:]
        for core, order in enumerate((posted, posted[::-1])):

            @pl.when(self.core == core)
            def _(order=order):
                for copy in order:
                    copy.start()

        self.push(self.own, mine, self.send_on.at[0], self.receive_on.at[0], self.mate)

    def arrived(self, k):
        block = self.group.at[2 * self.other(k) + self.core]
        to_device(
            "context", block, block, self.send.at[k], self.receive.at[k], self.mate
        ).wait_recv()
        self.push(block, block, self.send_on.at[k], self.receive_on.at[k], self.mate)

    def relay(self):
        if self.chips == 4:
            self.arrived(2)
            self.to_chip(self.group.at[2 * self.other(2) + self.core], 3, self.other(1))

    def pass_on(self):
        for k in (1, 3) if self.chips == 4 else range(1, self.chips):
            self.arrived(k)

    def finish(self):
        self.kept.wait()
        for k in range(self.chips):
            block = self.group.at[2 * (self.other(k) if k else self.chip) + 1 - self.core]
            to_device(
                "context", block, block, self.send_on.at[k], self.receive_on.at[k], self.mate
            ).wait_recv()
        for copy in self.sent:
            copy.wait_send()


def opening_kernel(gathers, spreads, *refs):
    refs = list(refs)

    def take(count):
        taken = refs[:count]
        del refs[:count]
        return taken

    sources = take(len(gathers) - 1)
    vector_refs = take(5)
    source_ref, mask_ref, cosine_ref, sine_ref = take(4)
    wholes = take(len(gathers))
    queries_ref, keyval_ref, resid_ref = take(3)
    groups = take(3)
    pair, attn, small, big, keyval, mixed, mixed_own, feed_own, out, out_came = take(10)
    vectors, vectors_own = take(2)
    swap_send, swap_receive, load, keyval_send, keyval_receive = take(5)
    for gather_of, source, whole in zip(gathers, [vectors_own] + sources, wholes):
        gather_of.bind(source, whole, *take(5))
    me, contexts = lax.axis_index("context"), lax.axis_size("context")
    chip, core = me // 2, lax.rem(me, 2)
    mate = me + 1 - 2 * core
    tok, model = source_ref.shape
    rows = 2 * tok
    attn_own = attn.at[pl.ds(pl.multiple_of(core * tok, tok), tok)]
    for spread, own, group in zip(spreads, (mixed_own, feed_own, attn_own), groups):
        spread.bind(own, group, *take(5))
    half = model // 2
    others = [lax.rem(me + k, contexts) for k in range(1, contexts)]
    vectors_own[...] = jnp.zeros_like(vectors_own)
    row, across_row = 0, vectors_own.shape[1]
    for ref in vector_refs:
        for start in range(0, ref.shape[1], across_row):
            vectors_own[row : row + 1, :] = ref[:, start : start + across_row]
            row += 1
    greet(gathers[0].near, others)
    vector_of, keyval_of, query_of, output_of, gate_up_of, down_of = gathers
    swaps = []

    def swap(step, source, target):
        swaps.append(
            to_device("context", source, target, swap_send.at[step], swap_receive.at[step], mate)
        )
        swaps[-1].start()

    def fetch(step, whole, target):
        copy = pltpu.make_async_copy(whole, target, load.at[step])
        copy.start()
        copy.wait()

    keyval_of.post()
    vector_of.post()
    query_of.post()
    pair[core] = source_ref[...]
    swap(0, source_ref, pair.at[core])

    vector_of.pass_on()
    vector_of.finish()
    fetch(0, vector_of.whole, vectors)

    def vector(row):
        tall = vector_of.rows
        return jnp.concatenate(
            [vectors[j * tall + row : j * tall + row + 1, :] for j in range(4)], axis=1
        ).astype(jnp.float32)

    swaps[0].wait_recv()
    attn[...] = rms_norm(
        pair[...].reshape(rows, model).astype(jnp.float32), vector(0)
    ).astype(jnp.bfloat16)

    keyval_of.pass_on()
    keyval_of.finish()
    fetch(1, keyval_of.whole, small)
    cosine, sine = cosine_ref[...], sine_ref[...]

    def turned(field):
        return field * cosine + pltpu.roll(field, DH // 4, 1) * sine

    raw = jnp.dot(attn[...], small[...], preferred_element_type=jnp.float32)
    at = pl.ds(pl.multiple_of(chip * rows, rows), rows)
    keyval[core, at, : DH // 2] = jnp.where(
        core == 0, turned(raw[:, : DH // 2]), raw[:, : DH // 2]
    ).astype(jnp.bfloat16)
    keyval[core, at, DH // 2 :] = raw[:, DH // 2 :].astype(jnp.bfloat16)
    keyval_sent = []
    for k in range(1, contexts):
        block = keyval.at[core, at]
        keyval_sent.append(
            to_device(
                "context", block, block, keyval_send.at[k], keyval_receive.at[k], others[k - 1]
            )
        )
        keyval_sent[-1].start()

    query_of.pass_on()
    query_of.finish()
    output_of.post()
    fetch(2, query_of.whole, big)
    heads = half // DH
    for h in range(heads):
        raw = jnp.dot(
            attn[...], big[:, h * DH : (h + 1) * DH], preferred_element_type=jnp.float32
        ) * DH ** (-0.5)
        queries_ref[:, h * DH : h * DH + DH // 2] = turned(raw[:, : DH // 2]).astype(jnp.bfloat16)
        queries_ref[:, h * DH + DH // 2 : (h + 1) * DH] = raw[:, DH // 2 :].astype(jnp.bfloat16)
    for k in range(1, contexts):
        place = lax.rem(me + contexts - k, contexts)
        block = keyval.at[
            lax.rem(place, 2), pl.ds(pl.multiple_of((place // 2) * rows, rows), rows)
        ]
        to_device(
            "context", block, block, keyval_send.at[k], keyval_receive.at[k], others[k - 1]
        ).wait_recv()
    spreads[2].post()
    for h in range(heads):
        weights = masked_weights(queries_ref[:, h * DH : (h + 1) * DH], keyval[0], mask_ref[...])
        mixed[core, :, h * DH : (h + 1) * DH] = jnp.dot(
            weights.astype(jnp.bfloat16), keyval[1], preferred_element_type=jnp.float32
        ).astype(jnp.bfloat16)
    swap(1, mixed.at[core], mixed.at[core])

    output_of.pass_on()
    gate_up_of.post()
    output_of.finish()
    down_of.post()
    fetch(3, output_of.whole, big)
    swaps[1].wait_recv()
    out[...] = jnp.dot(mixed[0], big[:half], preferred_element_type=jnp.float32) + jnp.dot(
        mixed[1], big[half:], preferred_element_type=jnp.float32
    )
    mine = pl.ds(pl.multiple_of(core * tok, tok), tok)
    theirs = pl.ds(pl.multiple_of((1 - core) * tok, tok), tok)
    swap(2, out.at[theirs], out_came)
    mixed_own[:, :half] = mixed[0, mine]
    mixed_own[:, half:] = mixed[1, mine]
    swaps[2].wait_recv()
    low = jnp.where(core == 0, out[mine], out_came[...])
    high = jnp.where(core == 0, out_came[...], out[mine])
    resid = (
        source_ref[...].astype(jnp.float32) + jnp.concatenate([low, high], axis=1) + vector(1)
    )
    resid_ref[...] = resid
    feed_own[...] = rms_norm(resid, vector(2)).astype(jnp.bfloat16)
    spreads[1].post()
    spreads[0].post()
    spreads[2].relay()
    spreads[2].pass_on()
    keyval_ref[...] = keyval[...]
    gate_up_of.pass_on()
    spreads[1].relay()
    down_of.pass_on()
    spreads[0].relay()
    spreads[1].pass_on()
    spreads[0].pass_on()
    for part in spreads:
        part.finish()
    gate_up_of.finish()
    down_of.finish()
    for gather_of in gathers:
        gather_of.close()
    for copy in swaps + keyval_sent:
        copy.wait_send()


def opening(number, cuts, vectors, source, mask, cosine, sine):
    contexts = lax.axis_size("context")
    tok, model = source.shape
    slots = mask.shape[1]
    half = model // 2
    gathers = [Gather(rows, pieces) for _, rows, pieces, _ in cuts]
    spreads = [Spread(contexts // 2) for _ in range(3)]
    low, full = jnp.bfloat16, jnp.float32
    dma = pltpu.SemaphoreType.DMA
    tall, wide = cuts[0][1], cuts[0][3]
    outs = pl.pallas_call(
        functools.partial(opening_kernel, gathers, spreads),
        in_specs=[pl.BlockSpec(memory_space=pl.ANY)] * (len(cuts) - 1)
        + [pl.BlockSpec(memory_space=pltpu.VMEM)] * 9,
        out_specs=[pl.BlockSpec(memory_space=pl.ANY)] * len(cuts)
        + [pl.BlockSpec(memory_space=pltpu.VMEM)] * 3
        + [pl.BlockSpec(memory_space=pl.ANY)] * 3,
        out_shape=[jax.ShapeDtypeStruct((4 * rows, columns), low) for _, rows, _, columns in cuts]
        + [
            jax.ShapeDtypeStruct((2 * tok, half), low),
            jax.ShapeDtypeStruct((2, slots, DH), low),
            jax.ShapeDtypeStruct((tok, model), full),
        ]
        + [jax.ShapeDtypeStruct((contexts, tok, model), low)] * 3,
        scratch_shapes=[
            pltpu.VMEM((2, tok, model), low),
            pltpu.VMEM((2 * tok, model), low),
            pltpu.VMEM((model, cuts[1][3]), low),
            pltpu.VMEM((model, half), low),
            pltpu.VMEM((2, slots, DH), low),
            pltpu.VMEM((2, 2 * tok, half), low),
            pltpu.VMEM((tok, model), low),
            pltpu.VMEM((tok, model), low),
            pltpu.VMEM((2 * tok, half), full),
            pltpu.VMEM((tok, half), full),
            pltpu.VMEM((4 * tall, wide), low),
            pltpu.VMEM((tall, wide), low),
            dma((3,)),
            dma((3,)),
            dma((4,)),
            dma((contexts,)),
            dma((contexts,)),
        ]
        + [shape for part in gathers + spreads for shape in part.scratch()],
        cost_estimate=pl.CostEstimate(flops=0, transcendentals=0, bytes_accessed=700_000_000),
        compiler_params=pltpu.CompilerParams(
            collective_id=number, has_side_effects=True, vmem_limit_bytes=VMEM_LIMIT
        ),
    )(*[array for array, _, _, _ in cuts[1:]], *vectors, source, mask, cosine, sine)
    return outs[: len(cuts)], outs[len(cuts) :]


class Product:
    def __init__(self, left, right):
        self.rows, self.wide = left[1] // 4, right[1]
        half = -(-self.wide // (2 * LANES)) * LANES
        self.sides = ((0, half), (half, self.wide - half))

    def buffers(self):
        return [pltpu.VMEM((3, self.rows, wide), jnp.bfloat16) for _, wide in self.sides]

    def scratch(self):
        return self.buffers() + self.buffers() + [pltpu.SemaphoreType.DMA((6,))] * 2

    def bind(self, left, right, made_a, made_b, came_a, came_b, send, receive):
        self.left, self.right, self.send, self.receive = left, right, send, receive
        self.made, self.came = (made_a, made_b), (came_a, came_b)
        self.here, along_x, along_y, self.far = shard_places()
        self.ways = ((along_x, along_y), (along_y, along_x))
        self.columns = [pl.ds(start, wide) for start, wide in self.sides]
        self.copies = []

    def product(self, place, side):
        block = pl.ds(pl.multiple_of(place * self.rows, LANES), self.rows)
        return over_rows(self.left[:, block], self.right[:, self.columns[side]])

    def push(self, step, side, place):
        slot = 2 * step + side
        self.copies.append(
            to_device(
                "shard",
                self.made[side].at[step],
                self.came[side].at[step],
                self.send.at[slot],
                self.receive.at[slot],
                place,
            )
        )
        self.copies[-1].start()

    def begin(self):
        for side in range(2):
            self.made[side][0] = self.product(self.far, side).astype(jnp.bfloat16)
            self.push(0, side, self.ways[side][0])
        for side in range(2):
            self.made[side][1] = self.product(self.ways[side][0], side).astype(jnp.bfloat16)
            self.push(1, side, self.ways[side][0])

    def middle(self):
        for side in range(2):
            kept = self.product(self.ways[side][1], side)
            self.copies[side].wait_recv()
            self.made[side][2] = (kept + self.came[side][0].astype(jnp.float32)).astype(
                jnp.bfloat16
            )
            self.push(2, side, self.ways[side][1])

    def finish(self, out):
        for side in range(2):
            total = self.product(self.here, side)
            self.copies[2 + side].wait_recv()
            total = total + self.came[side][1].astype(jnp.float32)
            self.copies[4 + side].wait_recv()
            out[:, self.columns[side]] = (
                total + self.came[side][2].astype(jnp.float32)
            ).astype(jnp.bfloat16)

    def drain(self, first, last):
        for copy in self.copies[first:last]:
            copy.wait_send()


class Exchange:
    def __init__(self, count, stride):
        self.count, self.stride = count, stride

    def scratch(self):
        return [pltpu.SemaphoreType.DMA((self.count,))] * 2 + [pltpu.SemaphoreType.DMA]

    def peers(self):
        me = lax.axis_index("context")
        slot, rest = me // self.stride, lax.rem(me, self.stride)
        places = [lax.rem(slot + k, self.count) for k in range(self.count)]
        return places, [place * self.stride + rest for place in places]

    def start(self, blocks, out, send, receive, local):
        slots, devices = self.peers()
        kept = pltpu.make_async_copy(blocks(slots[0]), out.at[slots[0]], local)
        kept.start()
        copies = []
        for k in range(1, self.count):
            copies.append(
                to_device(
                    "context", blocks(slots[k]), out.at[slots[0]], send.at[k], receive.at[k], devices[k]
                )
            )
            copies[-1].start()

        def finish():
            kept.wait()
            for k in range(1, self.count):
                source = slots[self.count - k]
                to_device(
                    "context", out.at[source], out.at[source], send.at[k], receive.at[k], devices[k]
                ).wait_recv()
            for copy in copies:
                copy.wait_send()

        return finish


def work_kernel(products, exchanges, chained, summed, packed, *refs):
    refs = list(refs)

    def take(count):
        taken = refs[:count]
        del refs[:count]
        return taken

    operands = [take(2) for _ in products]
    arrays = take(len(exchanges) - (1 if chained else 0))
    results = take(len(products))
    moved = take(len(exchanges))
    total_ref = take(1)[0] if summed else None
    held = [take(2) for _ in products]
    loads = take(1)[0] if products else None
    copies = []
    for i, (pair, targets) in enumerate(zip(operands, held)):
        for j in range(2):
            copies.append(pltpu.make_async_copy(pair[j], targets[j], loads.at[i, j]))
            copies[-1].start()
    if packed:
        apart = take(1)[0]
    product_scratch = [take(len(p.scratch())) for p in products]
    exchange_scratch = [take(len(e.scratch())) for e in exchanges]
    _, along_x, along_y, _ = shard_places()
    if summed:
        arrived, stage, stage_came, stage_send, stage_receive = take(5)
    everyone = max(exchanges, key=lambda e: e.count).peers()[1][1:] if exchanges else []
    greet((along_x, along_y), everyone)
    finishes, steps = [], []
    if summed:
        moved = [arrived] + moved[1:]

    def hop(step, place):
        steps.append(
            to_device(
                "shard",
                stage.at[step],
                stage_came.at[step],
                stage_send.at[step],
                stage_receive.at[step],
                place,
            )
        )
        steps[-1].start()

    for exchange, array, out, scratch in zip(exchanges, arrays, moved, exchange_scratch):
        finishes.append(exchange.start(lambda j, array=array: array.at[j], out, *scratch))
    for i, (product, (left, right), scratch) in enumerate(zip(products, held, product_scratch)):
        product.bind(left, right, *scratch)
        copies[2 * i].wait()
        copies[2 * i + 1].wait()
        if i == 1:
            if packed:
                wide = apart.shape[1] // 4
                apart[...] = jnp.zeros_like(apart)
                for j in range(4):
                    apart[:, j * wide : j * wide + packed] = left[:, j * packed : (j + 1) * packed]
                product.left = apart
            products[0].middle()
        product.begin()
    if summed:
        finishes.pop(0)()
        stage[0] = jnp.sum(arrived[...], axis=0)
        hop(0, along_x)
    if len(products) == 1:
        products[0].middle()
    for i, product in enumerate(products):
        if i == 1:
            product.middle()
        product.finish(results[i])
        if i == 0 and summed:
            steps[0].wait_recv()
            stage[1] = stage[0] + stage_came[0]
            hop(1, along_y)
        if chained and i == 0:
            rows = product.rows // exchanges[-1].count
            finishes.append(
                exchanges[-1].start(
                    lambda j: results[0].at[pl.ds(pl.multiple_of(j * rows, 16), rows)],
                    moved[-1],
                    *exchange_scratch[-1],
                )
            )
    if summed:
        steps[1].wait_recv()
        total_ref[...] = stage[1] + stage_came[1]
    for product in products:
        product.drain(0, 6)
    for step in steps:
        step.wait_send()
    for finish in finishes:
        finish()


def work(number, products=(), exchanges=(), chained=False, summed=False, packed=0):
    contexts = lax.axis_size("context")
    made = [Product(left.shape, right.shape) for left, right in products]
    apart = []
    if packed:
        rows, right = products[1][0].shape[0], products[1][1]
        apart = [(rows, 4 * -(-packed // LANES) * LANES)]
        made[1] = Product(apart[0], right.shape)
    swaps = [Exchange(array.shape[0], contexts // array.shape[0]) for array in exchanges]
    results = [jax.ShapeDtypeStruct((p.rows, p.wide), jnp.bfloat16) for p in made]
    moved = [jax.ShapeDtypeStruct(array.shape, array.dtype) for array in exchanges]
    if chained:
        swaps.append(Exchange(contexts, 1))
        moved.append(
            jax.ShapeDtypeStruct((contexts, made[0].rows // contexts, made[0].wide), jnp.bfloat16)
        )
    scratch = [pltpu.VMEM(operand.shape, operand.dtype) for pair in products for operand in pair]
    if made:
        scratch.append(pltpu.SemaphoreType.DMA((len(made), 2)))
    scratch += [pltpu.VMEM(each, jnp.bfloat16) for each in apart]
    scratch += [shape for part in made + swaps for shape in part.scratch()]
    totals = []
    if summed:
        block = exchanges[0].shape[1:]
        totals = [jax.ShapeDtypeStruct(block, jnp.float32)]
        moved[0] = jax.ShapeDtypeStruct((8, LANES), jnp.float32)
        scratch += [
            pltpu.VMEM(exchanges[0].shape, jnp.float32),
            pltpu.VMEM((2, *block), jnp.float32),
            pltpu.VMEM((2, *block), jnp.float32),
            pltpu.SemaphoreType.DMA((2,)),
            pltpu.SemaphoreType.DMA((2,)),
        ]
    vmem = pl.BlockSpec(memory_space=pltpu.VMEM)
    hbm = pl.BlockSpec(memory_space=pl.ANY)
    outs = pl.pallas_call(
        functools.partial(work_kernel, made, swaps, chained, summed, packed),
        in_specs=[hbm] * (2 * len(made) + len(exchanges)),
        out_specs=[vmem] * len(made) + [hbm] * len(swaps) + [vmem] * len(totals),
        out_shape=results + moved + totals,
        scratch_shapes=scratch,
        cost_estimate=pl.CostEstimate(flops=0, transcendentals=0, bytes_accessed=150_000_000),
        compiler_params=pltpu.CompilerParams(
            collective_id=number, has_side_effects=True, vmem_limit_bytes=VMEM_LIMIT
        ),
    )(*[operand for pair in products for operand in pair], *exchanges)
    others = outs[len(made) :]
    if summed:
        others = [others[-1], *others[1:-1]]
    return outs[1 if chained else 0 : len(made)], others


def norm_back(field, gain, grad):
    scale = lax.rsqrt(jnp.mean(field * field, axis=1, keepdims=True) + EPS)
    normed = field * scale
    bent = grad * gain
    back = scale * (bent - normed * jnp.mean(bent * normed, axis=1, keepdims=True))
    return back, jnp.sum(grad * normed, axis=0, keepdims=True)


def back_kernel(gate, up, swaps, *refs):
    refs = list(refs)

    def take(count):
        taken = refs[:count]
        del refs[:count]
        return taken

    output_ref, query_ref, keyval_ref, feed_ref, gate_ref, up_ref, down_ref = take(7)
    grad_ref, resid_ref, cotangent_ref, source_ref, gains_ref = take(5)
    queries_ref, keyval_of, mask_ref, cosine_ref, sine_ref = take(5)
    input_grad_ref, sums_ref, up_out, rows_out, back_out, down_out, gate_out = take(7)
    left, gate_right, up_right, big, small = take(5)
    own_grad, swapped, part, part_came, tail_came, mixed_back, query_back = take(7)
    pieces, pieces_mate, pieces_low, pieces_came = take(4)
    keyval_back, rows_blocks, back_blocks, gate_sum = take(4)
    load, mate_send, mate_receive = take(3)
    made = take(2)
    gate_scratch, up_scratch = take(4), take(4)
    rows_swap, back_swap, down_swap, gate_swap, piece_swap = swaps
    rows_sems, back_sems, down_sems, gate_sems, piece_sems = (take(3) for _ in swaps)
    me = lax.axis_index("context")
    chip, core = me // 2, lax.rem(me, 2)
    mate = me + 1 - 2 * core
    tok, model = resid_ref.shape
    half = model // 2
    rows = 2 * tok
    shards = lax.axis_size("shard")
    contexts = lax.axis_size("context")
    owned = model // (shards * contexts)
    mine = pl.ds(pl.multiple_of(core * tok, tok), tok)
    theirs = pl.ds(pl.multiple_of((1 - core) * tok, tok), tok)
    full = jnp.float32
    loads = []

    def fetch(source, target):
        loads.append(pltpu.make_async_copy(source, target, load.at[len(loads)]))
        loads[-1].start()
        return loads[-1]

    mates = []

    def to_mate(source, target):
        step = len(mates)
        mates.append(
            to_device("context", source, target, mate_send.at[step], mate_receive.at[step], mate)
        )
        mates[-1].start()
        return mates[-1]

    left_load, gate_load = fetch(feed_ref, left), fetch(gate_ref, gate_right)
    output_load, up_load = fetch(output_ref, big), fetch(up_ref, up_right)
    small_load = fetch(keyval_ref, small)
    _, along_x, along_y, _ = shard_places()
    greet((along_x, along_y), rows_swap.peers()[1][1:])
    finishes = [down_swap.start(lambda j: down_ref.at[j], down_out, *down_sems)]

    resid = resid_ref[...]
    cotangent = cotangent_ref[...].astype(full)
    resid_part, gain_two_grad = norm_back(resid, gains_ref[1:2], grad_ref[...])
    resid_grad = cotangent + resid_part
    input_grad_ref[...] = resid_grad
    attn_grad = resid_grad.astype(jnp.bfloat16)
    own_grad[...] = attn_grad
    swapped[core] = own_grad[:, pl.ds(pl.multiple_of(core * half, LANES), half)]
    first = to_mate(
        own_grad.at[:, pl.ds(pl.multiple_of((1 - core) * half, LANES), half)], swapped.at[core]
    )
    left_load.wait()
    gate_load.wait()
    gate.bind(left, gate_right, *made, *gate_scratch)
    gate.begin()
    sums_ref[...] = jnp.zeros_like(sums_ref)
    sums_ref[1:2] = jnp.sum(attn_grad.astype(full), axis=0, keepdims=True)
    sums_ref[2:3] = gain_two_grad
    sums_ref[3:4] = jnp.sum(cotangent, axis=0, keepdims=True)
    rows_blocks[...] = jnp.zeros_like(rows_blocks)
    for j in range(contexts):
        for shard in range(shards):
            start = (shard * contexts + j) * owned
            rows_blocks[j, :, shard * owned : (shard + 1) * owned] = attn_grad[
                :, start : start + owned
            ]
    finishes.append(rows_swap.start(lambda j: rows_blocks.at[j], rows_out, *rows_sems))

    first.wait_recv()
    output_load.wait()
    pair_grad = swapped[...].reshape(rows, half)
    for side in range(2):
        part[side] = against(pair_grad, big[side * half : (side + 1) * half])
    second = to_mate(part.at[1 - core], part_came)
    query_load = fetch(query_ref, big)
    second.wait_recv()
    mixed_back[...] = (part[core] + part_came[...]).astype(jnp.bfloat16)
    cosine, sine = cosine_ref[...], sine_ref[...]

    def unturned(field):
        return field * cosine - pltpu.roll(field, DH // 4, 1) * sine

    keys, values = keyval_of[0], keyval_of[1]
    for h in range(half // DH):
        at = slice(h * DH, (h + 1) * DH)
        queries, grad = queries_ref[:, at], mixed_back[:, at]
        weights = masked_weights(queries, keys, mask_ref[...])
        value_score = against(grad, values)
        delta = jnp.sum(weights * value_score, axis=1, keepdims=True)
        score_back = (weights * (value_score - delta)).astype(jnp.bfloat16)
        back = jnp.dot(score_back, keys, preferred_element_type=full) * DH ** (-0.5)
        query_back[:, h * DH : h * DH + DH // 2] = unturned(back[:, : DH // 2]).astype(jnp.bfloat16)
        query_back[:, h * DH + DH // 2 : (h + 1) * DH] = back[:, DH // 2 :].astype(jnp.bfloat16)
        key_piece = over_rows(score_back, queries)
        value_piece = over_rows(weights.astype(jnp.bfloat16), grad)
        if h == 0:
            pieces[0], pieces[1] = key_piece, value_piece
        else:
            pieces[0] += key_piece
            pieces[1] += value_piece
    fourth = to_mate(pieces.at[1 - core], pieces_mate)
    gate.middle()
    fourth.wait_recv()
    pieces_low[...] = (pieces[core] + pieces_mate[...]).astype(jnp.bfloat16)
    pieces_done = piece_swap.start(
        lambda j: pieces_low.at[pl.ds(pl.multiple_of(j * rows, rows), rows)],
        pieces_came,
        *piece_sems,
    )

    gate.drain(0, 4)
    up_load.wait()
    up.bind(left, up_right, *made, *up_scratch)
    up.begin()
    gate.finish(gate_sum)
    tall = gate.rows // contexts
    finishes.append(
        gate_swap.start(
            lambda j: gate_sum.at[pl.ds(pl.multiple_of(j * tall, 16), tall)], gate_out, *gate_sems
        )
    )

    pieces_done()
    total = jnp.sum(pieces_came[...].astype(full), axis=0)
    keyval_back[:, : DH // 2] = jnp.where(
        core == 0, unturned(total[:, : DH // 2]), total[:, : DH // 2]
    ).astype(jnp.bfloat16)
    keyval_back[:, DH // 2 :] = total[:, DH // 2 :].astype(jnp.bfloat16)
    chips = contexts // 2
    head_part, keyval_part = half // chips, DH // chips
    back_blocks[...] = jnp.zeros_like(back_blocks)
    for j in range(chips):
        back_blocks[j, :, :head_part] = query_back[:, j * head_part : (j + 1) * head_part]
        back_blocks[j, :, head_part : head_part + keyval_part] = keyval_back[
            :, j * keyval_part : (j + 1) * keyval_part
        ]
    finishes.append(back_swap.start(lambda j: back_blocks.at[j], back_out, *back_sems))
    query_load.wait()
    small_load.wait()
    second.wait_send()
    for side in range(2):
        at = slice(side * half, (side + 1) * half)
        part[side] = against(query_back[...], big[at]) + against(keyval_back[...], small[at])
    third = [to_mate(part.at[side, theirs], tail_came.at[side]) for side in range(2)]
    gate.drain(4, 6)
    up.middle()
    for copy in third:
        copy.wait_recv()
    attn_in_grad = jnp.concatenate([part[side, mine] + tail_came[side] for side in range(2)], axis=1)
    input_part, gain_one_grad = norm_back(
        source_ref[...].astype(full), gains_ref[0:1], attn_in_grad
    )
    input_grad_ref[...] += input_part
    sums_ref[0:1] = gain_one_grad
    up.finish(up_out)
    up.drain(0, 6)
    for copy in [first, fourth] + third:
        copy.wait_send()
    for finish in finishes:
        finish()


def back(number, weights, feed_group, gate_back, up_back, down_rows, tokens, attention):
    contexts, shards = lax.axis_size("context"), lax.axis_size("shard")
    tok, model = tokens[1].shape
    slots = attention[2].shape[1]
    half, rows, chips = model // 2, 2 * tok, contexts // 2
    owned = model // (shards * contexts)
    wide = -(-shards * owned // LANES) * LANES
    gate = Product(feed_group.shape, gate_back.shape)
    up = Product(feed_group.shape, up_back.shape)
    cols = max(half // chips + DH // chips, 2 * LANES)
    low, full = jnp.bfloat16, jnp.float32
    shape = jax.ShapeDtypeStruct
    swaps = [Exchange(n, contexts // n) for n in (contexts, chips, contexts, contexts, chips)]
    tall = gate.rows // contexts
    vmem, hbm = pl.BlockSpec(memory_space=pltpu.VMEM), pl.BlockSpec(memory_space=pl.ANY)
    dma = pltpu.SemaphoreType.DMA
    return pl.pallas_call(
        functools.partial(back_kernel, gate, up, swaps),
        in_specs=[hbm] * 7 + [vmem] * 10,
        out_specs=[vmem] * 3 + [hbm] * 4,
        out_shape=[
            shape((tok, model), full),
            shape((8, model), full),
            shape((up.rows, up.wide), low),
            shape((contexts, tok, wide), low),
            shape((chips, rows, cols), low),
            shape(down_rows.shape, low),
            shape((contexts, tall, gate.wide), low),
        ],
        scratch_shapes=[
            pltpu.VMEM(feed_group.shape, low),
            pltpu.VMEM(gate_back.shape, low),
            pltpu.VMEM(up_back.shape, low),
            pltpu.VMEM((model, half), low),
            pltpu.VMEM((model, DH), low),
            pltpu.VMEM((tok, model), low),
            pltpu.VMEM((2, tok, half), low),
            pltpu.VMEM((2, rows, half), full),
            pltpu.VMEM((rows, half), full),
            pltpu.VMEM((2, tok, half), full),
            pltpu.VMEM((rows, half), low),
            pltpu.VMEM((rows, half), low),
            pltpu.VMEM((2, slots, DH), full),
            pltpu.VMEM((slots, DH), full),
            pltpu.VMEM((slots, DH), low),
            pltpu.VMEM((chips, rows, DH), low),
            pltpu.VMEM((rows, DH), low),
            pltpu.VMEM((contexts, tok, wide), low),
            pltpu.VMEM((chips, rows, cols), low),
            pltpu.VMEM((gate.rows, gate.wide), low),
            dma((6,)),
            dma((5,)),
            dma((5,)),
        ]
        + gate.buffers()
        + (gate.buffers() + [dma((6,))] * 2)
        + (up.buffers() + [dma((6,))] * 2)
        + [each for swap in swaps for each in swap.scratch()],
        cost_estimate=pl.CostEstimate(flops=0, transcendentals=0, bytes_accessed=400_000_000),
        compiler_params=pltpu.CompilerParams(
            collective_id=number, has_side_effects=True, vmem_limit_bytes=BACK_LIMIT
        ),
    )(*weights, feed_group, gate_back, up_back, down_rows, *tokens, *attention)


def masked_weights(q, k, mask):
    scores = lax.dot_general(q, k, (((1,), (1,)), ((), ())), preferred_element_type=jnp.float32)
    scores = jnp.where(mask > 0.0, scores, NEG)
    raised = jnp.exp(scores - jnp.max(scores, axis=1, keepdims=True))
    return raised / jnp.sum(raised, axis=1, keepdims=True)


def mix_back_kernel(mask_ref, q_ref, k_ref, v_ref, g_ref, dq_ref, dk_ref, dv_ref):
    q, k, g = q_ref[...], k_ref[...], g_ref[...]
    weights = masked_weights(q, k, mask_ref[...])
    value_score = against(g, v_ref[...])
    delta = jnp.sum(weights * value_score, axis=1, keepdims=True)
    score_back = (weights * (value_score - delta)).astype(jnp.bfloat16)
    dq_ref[...] = jnp.dot(score_back, k, preferred_element_type=jnp.float32)
    key_piece = over_rows(score_back, q)
    value_piece = over_rows(weights.astype(jnp.bfloat16), g)

    @pl.when(pl.program_id(0) == 0)
    def _():
        dk_ref[...] = key_piece
        dv_ref[...] = value_piece

    @pl.when(pl.program_id(0) > 0)
    def _():
        dk_ref[...] += key_piece
        dv_ref[...] += value_piece


def mix_back(mask, queries, keys, values, grad):
    rows, width = queries.shape
    slots = keys.shape[0]
    whole = lambda h: (0, 0)
    part = lambda h: (0, h)
    return pl.pallas_call(
        mix_back_kernel,
        grid=(width // DH,),
        in_specs=[
            pl.BlockSpec((rows, slots), whole),
            pl.BlockSpec((rows, DH), part),
            pl.BlockSpec((slots, DH), whole),
            pl.BlockSpec((slots, DH), whole),
            pl.BlockSpec((rows, DH), part),
        ],
        out_specs=[
            pl.BlockSpec((rows, DH), part),
            pl.BlockSpec((slots, DH), whole),
            pl.BlockSpec((slots, DH), whole),
        ],
        out_shape=[
            jax.ShapeDtypeStruct((rows, width), jnp.float32),
            jax.ShapeDtypeStruct((slots, DH), jnp.float32),
            jax.ShapeDtypeStruct((slots, DH), jnp.float32),
        ],
        compiler_params=pltpu.CompilerParams(vmem_limit_bytes=VMEM_LIMIT),
    )(mask, queries, keys, values, grad)


def feed_kernel(feed_ref, grad_ref, gate_ref, up_ref, down_ref, bias_gate_ref, bias_up_ref, live_ref,
                hidden_ref, gate_back_ref, up_back_ref, gate_sum_ref, up_sum_ref):
    rows = feed_ref.shape[0]
    step = min(rows, 256)

    @pl.when(pl.program_id(1) == 0)
    def _():
        gate_sum_ref[...] = jnp.zeros_like(gate_sum_ref)
        up_sum_ref[...] = jnp.zeros_like(up_sum_ref)

    def part(i, carry):
        at = pl.ds(pl.multiple_of(i * step, step), step)
        feed = feed_ref[at, :]
        gate = jnp.dot(feed, gate_ref[...], preferred_element_type=jnp.float32) + bias_gate_ref[...]
        up = jnp.dot(feed, up_ref[...], preferred_element_type=jnp.float32) + bias_up_ref[...]
        back = against(grad_ref[at, :], down_ref[...])
        live = live_ref[...]
        square = gate * gate
        bend = jnp.tanh(GELU * gate * (1.0 + CUBE * square))
        half = 0.5 * (1.0 + bend)
        gelu = gate * half * live
        slope = half + 0.5 * gate * (1.0 - bend * bend) * (GELU * (1.0 + 3.0 * CUBE * square))
        hidden_ref[at, :] = (gelu * up).astype(jnp.bfloat16)
        gate_back = (back * up * slope * live).astype(jnp.bfloat16)
        up_back = (back * gelu).astype(jnp.bfloat16)
        gate_back_ref[at, :] = gate_back
        up_back_ref[at, :] = up_back
        gate_sum_ref[...] += jnp.sum(gate_back.astype(jnp.float32), axis=0, keepdims=True)
        up_sum_ref[...] += jnp.sum(up_back.astype(jnp.float32), axis=0, keepdims=True)
        return carry

    lax.fori_loop(0, rows // step, part, 0)


def feed(feed_group, grad_group, gate_up, down, bias, live):
    rows, model = feed_group.shape
    units = down.shape[0]
    wide = min(units, 256)
    blocks = units // wide
    tall = min(rows, 1024)
    buffers = {"pipeline_mode": pl.Buffered(1)} if tall == rows else {}
    tokens = lambda j, i: (i, 0)
    column = lambda j, i: (0, j)
    later = lambda j, i: (0, j + blocks)
    made = lambda j, i: (i, j)
    return pl.pallas_call(
        feed_kernel,
        grid=(blocks, rows // tall),
        in_specs=[
            pl.BlockSpec((tall, model), tokens, **buffers),
            pl.BlockSpec((tall, model), tokens, **buffers),
            pl.BlockSpec((model, wide), column),
            pl.BlockSpec((model, wide), later),
            pl.BlockSpec((wide, model), lambda j, i: (j, 0)),
            pl.BlockSpec((1, wide), column),
            pl.BlockSpec((1, wide), later),
            pl.BlockSpec((1, wide), column),
        ],
        out_specs=[
            pl.BlockSpec((tall, wide), made),
            pl.BlockSpec((tall, wide), made),
            pl.BlockSpec((tall, wide), made),
            pl.BlockSpec((1, wide), column),
            pl.BlockSpec((1, wide), column),
        ],
        out_shape=[
            jax.ShapeDtypeStruct((rows, units), jnp.bfloat16),
            jax.ShapeDtypeStruct((rows, units), jnp.bfloat16),
            jax.ShapeDtypeStruct((rows, units), jnp.bfloat16),
            jax.ShapeDtypeStruct((1, units), jnp.float32),
            jax.ShapeDtypeStruct((1, units), jnp.float32),
        ],
        compiler_params=pltpu.CompilerParams(vmem_limit_bytes=VMEM_LIMIT),
    )(feed_group, grad_group, gate_up, gate_up, down, bias, bias, live)


def middle_kernel(*refs):
    refs = list(refs)

    def take(count):
        taken = refs[:count]
        del refs[:count]
        return taken

    feed_ref, grad_ref, weight_ref, down_ref, bias_ref, live_ref = take(6)
    *leaving, down_out_ref, sums_ref, feed_grad_ref = take(6)
    hidden_ref, gate_back_ref, up_back_ref, down_rows, leave, down_leave = take(6)
    gate_weight, up_weight, down_weight, feed_rows, grad_rows = take(5)
    own_part, mate_out, mate_in, sent_out, came, swap_in = take(6)
    weight_load, row_load, mate_send, mate_receive, send, receive = take(6)
    me = lax.axis_index("context")
    chips = lax.axis_size("context") // 2
    chip, core = me // 2, lax.rem(me, 2)
    mate = me + 1 - 2 * core
    units, model = down_weight.shape
    rows, half, wide = feed_rows.shape[0], model // 2, 256
    blocks = units // wide
    full, low = jnp.float32, jnp.bfloat16
    mine = pl.ds(pl.multiple_of(core * half, LANES), half)
    theirs = pl.ds(pl.multiple_of((1 - core) * half, LANES), half)
    targets = [3 * (1 - chip // 2), lax.rem(2 + 3 * chip, 5), 1 + lax.rem(chip, 2), chip]
    inner = lax.rem(chip + 1, 4) // 2

    def token_rows(i):
        return pl.ds(pl.multiple_of(targets[i] * rows, rows), rows)

    def weight_loads(j):
        at = pl.ds(pl.multiple_of(j * wide, wide), wide)
        later = pl.ds(pl.multiple_of(units + j * wide, wide), wide)
        return [
            pltpu.make_async_copy(weight_ref.at[:, at], gate_weight.at[:, at], weight_load.at[j, 0]),
            pltpu.make_async_copy(weight_ref.at[:, later], up_weight.at[:, at], weight_load.at[j, 1]),
            pltpu.make_async_copy(down_ref.at[at], down_weight.at[at], weight_load.at[j, 2]),
        ]

    def row_loads(i):
        at = token_rows(i)
        return [
            pltpu.make_async_copy(feed_ref.at[at], feed_rows, row_load.at[i, 0]),
            pltpu.make_async_copy(grad_ref.at[at], grad_rows.at[at], row_load.at[i, 1]),
        ]

    for copy in row_loads(0):
        copy.start()
    for j in range(blocks):
        for copy in weight_loads(j):
            copy.start()
    greet((), [lax.rem(me + k, 2 * chips) for k in range(1, 2 * chips)])
    sums_ref[...] = jnp.zeros_like(sums_ref)
    to_mate, left = [], []

    def passed(which, i, chip_at):
        receiver, slot = LINE[chip_at][i]
        return to_device(
            "context",
            sent_out.at[which, i],
            came.at[which, slot],
            send.at[which, i],
            receive.at[which, slot],
            2 * receiver + core,
        )

    def arrived(which, slot):
        part = came.at[which, slot]
        to_device(
            "context", part, part, send.at[which, 0], receive.at[which, slot], mate
        ).wait_recv()
        own_part[which] += part[...].astype(full)

    def reduce(i, which, part):
        step = i
        if step >= 1:
            to_mate[step - 1].wait_send()
        mate_out[which] = part(theirs).astype(low)
        to_mate.append(
            to_device(
                "context",
                mate_out.at[which],
                mate_in.at[i % 2],
                mate_send.at[step],
                mate_receive.at[step],
                mate,
            )
        )
        to_mate[-1].start()
        own_part[which] = part(mine)
        to_mate[-1].wait_recv()
        own_part[which] += mate_in[i % 2].astype(full)
        if i + 1 == chips:
            return

        @pl.when(inner == 1)
        def _():
            arrived(which, i)

        sent_out[which, i] = own_part[which].astype(low)
        for chip_at in range(chips):

            @pl.when(chip == chip_at)
            def _(chip_at=chip_at):
                passed(which, i, chip_at).start()

    for i in range(chips):
        for copy in row_loads(i):
            copy.wait()
        at = token_rows(i)

        def block(j, carry, i=i, at=at):
            if i == 0:
                for copy in weight_loads(j):
                    copy.wait()
            cut = pl.ds(pl.multiple_of(j * wide, wide), wide)
            later = pl.ds(pl.multiple_of(units + j * wide, wide), wide)
            feed = feed_rows[...]
            gate = jnp.dot(feed, gate_weight[:, cut], preferred_element_type=full) + bias_ref[:, cut]
            up = jnp.dot(feed, up_weight[:, cut], preferred_element_type=full) + bias_ref[:, later]
            back = against(grad_rows[at, :], down_weight[cut])
            live = live_ref[:, cut]
            square = gate * gate
            bend = jnp.tanh(GELU * gate * (1.0 + CUBE * square))
            share = 0.5 * (1.0 + bend)
            gelu = gate * share * live
            slope = share + 0.5 * gate * (1.0 - bend * bend) * (GELU * (1.0 + 3.0 * CUBE * square))
            hidden_ref[at, cut] = (gelu * up).astype(low)
            gate_back = (back * up * slope * live).astype(low)
            up_back = (back * gelu).astype(low)
            gate_back_ref[at, cut] = gate_back
            up_back_ref[at, cut] = up_back
            sums_ref[0:1, cut] += jnp.sum(gate_back.astype(full), axis=0, keepdims=True)
            sums_ref[1:2, cut] += jnp.sum(up_back.astype(full), axis=0, keepdims=True)
            return carry

        lax.fori_loop(0, blocks, block, 0)
        if i + 1 < chips:
            for copy in row_loads(i + 1):
                copy.start()
        for j, made in enumerate((hidden_ref, gate_back_ref, up_back_ref)):
            left.append(pltpu.make_async_copy(made.at[at], leaving[j].at[at], leave.at[i, j]))
            left[-1].start()

        def feed_part(columns, at=at):
            return against(gate_back_ref[at, :], gate_weight[columns, :]) + against(
                up_back_ref[at, :], up_weight[columns, :]
            )

        reduce(i, 0, feed_part)
    for i in range(chips):
        at = token_rows(i)
        if i >= 2:
            left[-2].wait()
        down_rows[i % 2] = jnp.dot(
            hidden_ref[at, :], down_weight[...], preferred_element_type=full
        ).astype(low)
        left.append(pltpu.make_async_copy(down_rows.at[i % 2], down_out_ref.at[at], down_leave.at[i]))
        left[-1].start()
    tok = rows // 2
    own_rows = pl.ds(pl.multiple_of(core * tok, tok), tok)
    mate_rows = pl.ds(pl.multiple_of((1 - core) * tok, tok), tok)
    lasts = []

    def complete(which, out):
        for slot, missing in ((3, 0), (4, chips - 1)):

            @pl.when(chip != missing)
            def _(slot=slot):
                arrived(which, slot)

        lasts.append(
            to_device(
                "context",
                own_part.at[which, mate_rows],
                swap_in.at[which],
                mate_send.at[chips + which],
                mate_receive.at[chips + which],
                mate,
            )
        )
        lasts[-1].start()
        out[:, mine] = own_part[which, own_rows]

    complete(0, feed_grad_ref)
    lasts[0].wait_recv()
    feed_grad_ref[:, theirs] = swap_in[0]
    for copy in left[: 3 * chips] + left[-2:]:
        copy.wait()
    for i in range(chips - 1):
        passed(0, i, 0).wait_send()
    for copy in to_mate[-1:] + lasts:
        copy.wait_send()


def middle(number, feed_group, grad_group, gate_up, down, bias, live):
    group, model = feed_group.shape
    units, contexts = down.shape[0], lax.axis_size("context")
    chips, half = contexts // 2, model // 2
    rows = group // chips
    low, full = jnp.bfloat16, jnp.float32
    shape, dma = jax.ShapeDtypeStruct, pltpu.SemaphoreType.DMA
    vmem, hbm = pl.BlockSpec(memory_space=pltpu.VMEM), pl.BlockSpec(memory_space=pl.ANY)
    return pl.pallas_call(
        middle_kernel,
        in_specs=[hbm] * 4 + [vmem] * 2,
        out_specs=[hbm] * 4 + [vmem] * 2,
        out_shape=[shape((group, units), low)] * 3
        + [shape((group, model), low), shape((8, units), full), shape((rows // 2, model), full)],
        scratch_shapes=[pltpu.VMEM((group, units), low)] * 3
        + [pltpu.VMEM((2, rows, model), low), dma((chips, 3)), dma((chips,))]
        + [
            pltpu.VMEM((model, units), low),
            pltpu.VMEM((model, units), low),
            pltpu.VMEM((units, model), low),
            pltpu.VMEM((rows, model), low),
            pltpu.VMEM((group, model), low),
            pltpu.VMEM((1, rows, half), full),
            pltpu.VMEM((1, rows, half), low),
            pltpu.VMEM((2, rows, half), low),
            pltpu.VMEM((1, chips - 1, rows, half), low),
            pltpu.VMEM((1, chips + 1, rows, half), low),
            pltpu.VMEM((1, rows // 2, half), full),
            dma((units // 256, 3)),
            dma((chips, 2)),
            dma((chips + 1,)),
            dma((chips + 1,)),
            dma((1, chips)),
            dma((1, chips + 1)),
        ],
        cost_estimate=pl.CostEstimate(flops=0, transcendentals=0, bytes_accessed=200_000_000),
        compiler_params=pltpu.CompilerParams(
            collective_id=number, has_side_effects=True, vmem_limit_bytes=BACK_LIMIT
        ),
    )(feed_group, grad_group, gate_up, down, bias, live)


def body(
    inputs,
    doc_ids,
    cotangent,
    attn_gain,
    query_weight,
    keyval_weight,
    output_weight,
    output_bias,
    feed_gain,
    gate_up_weight,
    gate_up_bias,
    down_weight,
    down_bias,
):
    tok, model = inputs.shape
    shards, contexts = lax.axis_size("shard"), lax.axis_size("context")
    shard, place = lax.axis_index("shard"), lax.axis_index("context")
    core, chip = place % 2, place // 2
    group = tok * contexts
    owned = model // (shards * contexts)
    ff = gate_up_weight.shape[1] // 2
    width, per_shard = unit_tiles(ff, shards, contexts)
    unit_start = jnp.minimum(place * width, per_shard - width)
    units = shards * width * LANES

    shard_rows = model // shards
    block = width * LANES

    def half_of(wide):
        def pieces():
            column = lax.rem(lax.axis_index("context"), 2) * wide
            return [(0, pl.multiple_of(column, LANES), wide, 0)]

        return pieces

    def first_unit():
        return jnp.minimum(lax.axis_index("context") * width, per_shard - width) * LANES

    def gate_up_pieces():
        return [
            (0, pl.multiple_of(j * per_shard * LANES + first_unit(), LANES), block, j * block)
            for j in range(2 * shards)
        ]

    def down_pieces():
        return [(pl.multiple_of(first_unit(), LANES), 0, model, 0)]

    unit_at = unit_start * LANES + jnp.arange(block, dtype=jnp.int32)
    unit_live = jnp.tile(unit_at >= place * block, shards)[None, :].astype(jnp.float32)
    slots = jnp.arange(group, dtype=jnp.int32)
    pair_slots = chip * (2 * tok) + jnp.arange(2 * tok, dtype=jnp.int32)
    pair_docs = lax.dynamic_slice_in_dim(doc_ids, chip * (2 * tok), 2 * tok)
    distance = pair_slots[:, None] - slots[None, :]
    mask = (
        (pair_docs[:, None] == doc_ids[None, :]) & (distance >= 0) & (distance < WINDOW)
    ).astype(jnp.float32)
    angles = pair_slots.astype(jnp.float32)[:, None] * frequencies(DH)[None, :]
    cosine, sine = jnp.cos(angles), jnp.sin(angles)
    turns = (jnp.concatenate([cosine, cosine], axis=1), jnp.concatenate([-sine, sine], axis=1))
    vectors = [
        each.reshape(1, each.shape[0])
        for each in (attn_gain, output_bias, feed_gain, down_bias, gate_up_bias)
    ]
    vector_rows = 4 + gate_up_bias.shape[0] // shard_rows
    vector_tall = -(-vector_rows // 32) * 32
    core_cols, core_heads = keyval_weight.shape[1] // 2, query_weight.shape[1] // 2
    (vectors, keyval_half, query_half, output_half, gate_up_part, down_part), (
        queries, keyval, resid, mixed_group, feed_group, attn_group
    ) = opening(
        0,
        (
            (None, vector_tall, lambda: [(0, 0, shard_rows, 0)], shard_rows),
            (keyval_weight, shard_rows, half_of(core_cols), core_cols),
            (query_weight, shard_rows, half_of(core_heads), core_heads),
            (output_weight, shard_rows, half_of(model // 2), model // 2),
            (gate_up_weight, shard_rows, gate_up_pieces, 2 * units),
            (down_weight, block, down_pieces, model),
        ),
        vectors,
        inputs,
        mask,
        *turns,
    )
    grad_group = gather(cotangent, "context")
    vectors = vectors.reshape(shards, vector_tall, shard_rows).astype(jnp.float32)
    gain_one, gain_two, bias_down = (vectors[:, i].reshape(1, model) for i in (0, 2, 3))
    bias_gate_up = vectors[:, 4:vector_rows].reshape(2 * shards, per_shard * LANES)
    bias_gate_up = lax.dynamic_slice_in_dim(
        bias_gate_up, unit_start * LANES, block, 1
    ).reshape(1, 2 * units)
    source = inputs.astype(jnp.float32)
    keys, values = keyval[0], keyval[1]
    heads = core_heads // DH
    mixed_group, feed_group, attn_group = (
        field.reshape(group, model) for field in (mixed_group, feed_group, attn_group)
    )

    if group <= 1024 and contexts == 8:
        hidden, gate_back, up_back, down_part_out, unit_sums, feed_in_grad = middle(
            8, feed_group, grad_group, gate_up_part, down_part, bias_gate_up, unit_live
        )
        gate_sums, up_sums = unit_sums[0], unit_sums[1]
    else:
        hidden, gate_back, up_back, gate_sums, up_sums = feed(
            feed_group, grad_group, gate_up_part, down_part, bias_gate_up, unit_live
        )
        feed_part = against(
            jnp.concatenate([gate_back, up_back], axis=1), gate_up_part
        ).astype(jnp.bfloat16)
        feed_in_grad = lax.psum_scatter(feed_part, "context", scatter_dimension=0, tiled=True)
        feed_in_grad = feed_in_grad.astype(jnp.float32)
        down_part_out = jnp.dot(hidden, down_part, preferred_element_type=jnp.float32).astype(
            jnp.bfloat16
        )
    down_out = lax.psum_scatter(
        down_part_out, "context", scatter_dimension=0, tiled=True
    ).astype(jnp.float32)
    (down_sum,), _ = work(2, [(grad_group, after(hidden, feed_in_grad))])
    block_out = (resid + down_out + bias_down).astype(jnp.bfloat16)

    chips = contexts // 2
    rows_wide = -(-owned // LANES) * LANES
    head_part, keyval_part = HEADS * DH // contexts, DH // chips

    def by_owners(field):
        return field.reshape(contexts, owned, field.shape[1])

    if group <= 1024 and contexts == 8:
        gains = jnp.concatenate([gain_one, gain_two, jnp.zeros((6, model), jnp.float32)], axis=0)
        input_grad, sums, up_sum, attn_grad_rows, back_cols, down_rows, gate_rows = back(
            3,
            (output_half, query_half, keyval_half),
            feed_group,
            gate_back,
            up_back,
            by_owners(down_sum),
            (feed_in_grad, resid, cotangent, inputs, gains),
            (queries, keyval, mask, *turns),
        )
        sums = sums[:4].reshape(4 * model)
        attn_grad_rows = attn_grad_rows.reshape(group, attn_grad_rows.shape[2])
        back_cols = back_cols.reshape(group, back_cols.shape[2])
    else:
        grad_out = cotangent.astype(jnp.float32)
        resid_part, gain_two_grad = jax.vjp(rms_norm, resid, gain_two)[1](feed_in_grad)
        resid_grad = grad_out + resid_part
        attn_grad_low = resid_grad.astype(jnp.bfloat16)
        mixed_back = summed_half(
            against(swap_columns(attn_grad_low, core), output_half), core, 1
        ).astype(jnp.bfloat16)
        query_acc, key_acc, value_acc = mix_back(mask, queries, keys, values, mixed_back)
        keyval_acc = jnp.stack(
            [key_acc.reshape(contexts // 2, 2 * tok, DH), value_acc.reshape(contexts // 2, 2 * tok, DH)],
            axis=1,
        ).reshape(contexts, 2 * tok, DH).astype(jnp.bfloat16)
        attn_grad_rows = jnp.pad(
            attn_grad_low.reshape(tok, shards, contexts, owned).transpose(2, 0, 1, 3),
            ((0, 0), (0, 0), (0, 0), (0, rows_wide - owned)),
        ).reshape(contexts, tok, shards * rows_wide)
        (gate_sum,), (keyval_acc, attn_grad_rows) = work(
            3, [(feed_group, gate_back)], [keyval_acc, attn_grad_rows]
        )
        attn_grad_rows = attn_grad_rows.reshape(group, shards * rows_wide)
        keyval_acc = jnp.sum(keyval_acc.astype(jnp.float32), axis=0)
        keyval_back = jnp.where(core == 0, rotate(keyval_acc, cosine, -sine), keyval_acc).astype(
            jnp.bfloat16
        )
        query_back = (
            rotate(query_acc.reshape(2 * tok, heads, DH), cosine[:, None, :], -sine[:, None, :])
            * DH ** (-0.5)
        ).reshape(2 * tok, heads * DH).astype(jnp.bfloat16)
        attn_in_grad = summed_half(
            against(query_back, query_half) + against(keyval_back, keyval_half), core, 0
        )
        input_part, gain_one_grad = jax.vjp(rms_norm, source, gain_one)[1](attn_in_grad)
        input_grad = resid_grad + input_part

        def by_chips(field):
            return field.reshape(2 * tok, chips, field.shape[1] // chips).transpose(1, 0, 2)

        spare = max(2 * LANES - head_part - keyval_part, 0)
        back_cols = jnp.concatenate([by_chips(query_back), by_chips(keyval_back)], axis=2)
        back_cols = jnp.pad(back_cols, ((0, 0), (0, 0), (0, spare)))
        moving = [back_cols, by_owners(down_sum), by_owners(gate_sum)]
        (up_sum,), (back_cols, down_rows, gate_rows) = work(4, [(feed_group, up_back)], moving)
        back_cols = back_cols.reshape(group, back_cols.shape[2])

        sums = jnp.concatenate(
            [
                gain_one_grad.reshape(model),
                jnp.sum(attn_grad_low.astype(jnp.float32), axis=0),
                gain_two_grad.reshape(model),
                jnp.sum(grad_out, axis=0),
            ]
        )

    sums = jnp.concatenate([sums, gate_sums.reshape(units), up_sums.reshape(units)])
    unit_owned = 2 * ff // (shards * contexts)
    mine = sums[: 4 * model].reshape(4, shards, contexts, owned).transpose(2, 0, 1, 3)
    unit_sums = lax.dynamic_update_slice_in_dim(
        jnp.zeros((2 * shards, per_shard * LANES), jnp.float32),
        sums[4 * model :].reshape(2 * shards, block),
        unit_start * LANES,
        1,
    )
    unit_sums = unit_sums.reshape(shards, contexts, unit_owned).transpose(1, 0, 2)
    at = 4 * shards * owned
    wide = at + shards * unit_owned
    tall = -(-wide // (8 * LANES)) * LANES
    vectors = jnp.concatenate(
        [
            mine.reshape(contexts, at),
            unit_sums.reshape(contexts, wide - at),
            jnp.zeros((contexts, 8 * tall - wide), jnp.float32),
        ],
        axis=1,
    ).reshape(contexts, 8, tall)
    if owned % 16 == 0:
        (output_sum,), (vectors, up_rows, back_rows) = work(
            5,
            [(attn_group, back_cols), (attn_grad_rows, mixed_group)],
            [vectors, by_owners(up_sum)],
            True,
            True,
            owned,
        )
    else:
        (back_sum,), (vectors, up_rows) = work(
            5, [(attn_group, back_cols)], [vectors, by_owners(up_sum)], False, True
        )
        _, (back_rows,) = work(7, [], [by_owners(back_sum)])
        (output_sum,), _ = work(6, [(attn_grad_rows, mixed_group)])
    vectors = vectors.reshape(8 * tall)
    own = vectors[:at].reshape(4, shards, owned)
    own = lax.dynamic_index_in_dim(own, shard, 1, False)
    gate_up_bias_grad = lax.dynamic_index_in_dim(
        vectors[at:wide].reshape(shards, unit_owned), shard, 0, False
    )
    pieces = unit_pieces(contexts, shards, width, per_shard)
    down_grad, gate_up_grad, query_grad, keyval_grad, output_grad = lay(
        pieces,
        owned,
        (ff, 2 * ff, HEADS * DH, 2 * DH, model),
        down_rows,
        gate_rows,
        up_rows,
        back_rows,
        output_sum,
    )
    output_weight_grad, down_weight_grad = output_grad.T, down_grad.T
    return (
        block_out,
        input_grad,
        own[0],
        query_grad,
        keyval_grad,
        output_weight_grad,
        own[1],
        own[2],
        gate_up_grad,
        gate_up_bias_grad,
        down_weight_grad,
        own[3],
    )


def solution(mesh):
    placed = (
        P(("shard", "context"), None),
        P("shard"),
        P(("shard", "context"), None),
        P("shard"),
        P("shard", None),
        P("shard", None),
        P("shard", None),
        P("shard"),
        P("shard"),
        P("shard", None),
        P("shard"),
        P("shard", None),
        P("shard"),
    )
    return jax.shard_map(
        body,
        mesh=mesh,
        in_specs=placed,
        out_specs=(
            P(("shard", "context"), None),
            P(("shard", "context"), None),
            P(("shard", "context")),
            P(("shard", "context"), None),
            P(("shard", "context"), None),
            P(None, ("shard", "context")),
            P(("shard", "context")),
            P(("shard", "context")),
            P(("shard", "context"), None),
            P(("shard", "context")),
            P(None, ("shard", "context")),
            P(("shard", "context")),
        ),
        check_vma=False,
    )
```

```python
import functools
import math

import jax
import jax.numpy as jnp
from jax import lax
from jax.experimental import pallas as pl
from jax.experimental.pallas import tpu as pltpu
from jax.sharding import PartitionSpec as P

HEADS = 10
DH = 256
FF = 7680
WINDOW = 2048


EPS = 1e-06
NEG = -1e30
ROPE_LOG = math.log(10000.0)


def frequencies(head_dim):
    quarter = head_dim // 4
    steps = jnp.arange(quarter).astype(jnp.float32)
    return jnp.exp(-ROPE_LOG * (2.0 * steps) / (head_dim // 2))


def rotate(field, cosine, sine):
    width = field.shape[-1] // 2
    quarter = width // 2
    first = field[..., :quarter]
    second = field[..., quarter:width]
    return jnp.concatenate(
        [first * cosine - second * sine, second * cosine + first * sine, field[..., width:]],
        axis=-1,
    )


def rms_norm(field, gain):
    return field * lax.rsqrt(jnp.mean(field * field, axis=-1, keepdims=True) + EPS) * gain


def geglu(gate_up):
    half = gate_up.shape[-1] // 2
    return jax.nn.gelu(gate_up[:, :half], approximate=True) * gate_up[:, half:]


def over_rows(left, right):
    return lax.dot_general(
        left, right, (((0,), (0,)), ((), ())), preferred_element_type=jnp.float32
    )


def against(left, weight):
    return lax.dot_general(
        left, weight, (((1,), (1,)), ((), ())), preferred_element_type=jnp.float32
    )


VMEM_LIMIT = 56 * 1024 * 1024
BACK_LIMIT = 61 * 1024 * 1024
LANES = 128
MESH = pl.DeviceIdType.MESH
LINE = (
    ((1, 0), (1, 2), (1, 3)),
    ((2, 1), (0, 4), (2, 3)),
    ((1, 1), (3, 3), (1, 4)),
    ((2, 0), (2, 2), (2, 4)),
)
GELU = 0.7978845608028654
CUBE = 0.044715


def gather(value, axis):
    return lax.all_gather(value, axis, axis=0, tiled=True)


def across(value, bit):
    count = lax.axis_size("shard")
    return lax.ppermute(value, "shard", [(i, i ^ bit) for i in range(count)])


def after(value, *earlier):
    return lax.optimization_barrier((value, *earlier))[0]


def sibling(value):
    count = lax.axis_size("context")
    return lax.ppermute(value, "context", [(i, i ^ 1) for i in range(count)])


def halves(value, core, axis):
    low, high = jnp.split(value, 2, axis=axis)
    return jnp.where(core == 0, low, high), jnp.where(core == 0, high, low)


def swap_rows(value, core):
    mine, theirs = halves(value, core, 0)
    other = sibling(theirs)
    return jnp.where(
        core == 0, jnp.concatenate([mine, other], axis=1), jnp.concatenate([other, mine], axis=1)
    )


def swap_columns(own, core):
    mine, theirs = halves(own, core, 1)
    other = sibling(theirs)
    return jnp.where(
        core == 0, jnp.concatenate([mine, other], axis=0), jnp.concatenate([other, mine], axis=0)
    )


def summed_half(value, core, axis):
    mine, theirs = halves(value, core, axis)
    return mine + sibling(theirs)


def unit_tiles(ff, shards, contexts):
    per_shard = ff // shards // LANES
    return -(-per_shard // contexts), per_shard


def unit_pieces(contexts, shards, width, per_shard):
    found = []
    for at in range(contexts):
        first = at * width
        if first >= per_shard:
            continue
        start, stop = min(first, per_shard - width), min(first + width, per_shard)
        for shard in range(shards):
            found.append(
                (
                    at,
                    (shard * width + first - start) * LANES,
                    (stop - first) * LANES,
                    (shard * per_shard + first) * LANES,
                )
            )
    return found


def lay_kernel(pieces, down_ref, gate_ref, up_ref, back_ref, output_ref, *outs):
    down_leaves, gate_up_leaves, query_out, keyval_out, output_out, down_out, gate_up_out, leave = outs
    units, owned = down_out.shape[1], down_out.shape[0]
    contexts = back_ref.shape[0]
    head_part, keyval_part = query_out.shape[1] // contexts, keyval_out.shape[1] // contexts
    copies = []
    for i, (source, out, leaves, offset) in enumerate(
        (
            (down_ref, down_out, down_leaves, 0),
            (gate_ref, gate_up_out, gate_up_leaves, 0),
            (up_ref, gate_up_out, gate_up_leaves, units),
        )
    ):
        for at, column, wide, first in pieces:
            out[:, offset + first : offset + first + wide] = source[
                at, :, column : column + wide
            ].astype(jnp.float32)
        whole = pl.ds(offset, units)
        copies.append(pltpu.make_async_copy(out.at[:, whole], leaves.at[:, whole], leave.at[i]))
        copies[-1].start()
    for at in range(contexts):
        slot = (at % 2) * (contexts // 2) + at // 2
        part = back_ref[at].astype(jnp.float32)
        query_out[:, slot * head_part : (slot + 1) * head_part] = part[:, :head_part]
        keyval_out[:, slot * keyval_part : (slot + 1) * keyval_part] = part[
            :, head_part : head_part + keyval_part
        ]
    output_out[...] = output_ref[:owned].astype(jnp.float32)
    for copy in copies:
        copy.wait()


def lay(pieces, owned, widths, *fields):
    return pl.pallas_call(
        functools.partial(lay_kernel, pieces),
        in_specs=[pl.BlockSpec(memory_space=pltpu.VMEM)] * len(fields),
        out_specs=[pl.BlockSpec(memory_space=pl.ANY)] * 2
        + [pl.BlockSpec(memory_space=pltpu.VMEM)] * (len(widths) - 2),
        out_shape=[jax.ShapeDtypeStruct((owned, wide), jnp.float32) for wide in widths],
        scratch_shapes=[pltpu.VMEM((owned, wide), jnp.float32) for wide in widths[:2]]
        + [pltpu.SemaphoreType.DMA((3,))],
        compiler_params=pltpu.CompilerParams(vmem_limit_bytes=VMEM_LIMIT),
    )(*fields)


def shard_places():
    here = lax.axis_index("shard")
    return here, here + 1 - 2 * lax.rem(here, 2), lax.rem(here + 2, 4), 3 - here


def greet(shards, contexts=()):
    barrier = pltpu.get_barrier_semaphore()
    for axis, places in (("shard", shards), ("context", contexts)):
        for place in places:
            pl.semaphore_signal(barrier, 1, device_id={axis: place}, device_id_type=MESH)
    pl.semaphore_wait(barrier, len(shards) + len(contexts))


def to_device(axis, source, target, send, receive, place):
    return pltpu.make_async_remote_copy(
        src_ref=source,
        dst_ref=target,
        send_sem=send,
        recv_sem=receive,
        device_id={axis: place},
        device_id_type=MESH,
    )


class Gather:
    def __init__(self, rows, pieces):
        self.rows, self.pieces = rows, pieces

    def scratch(self):
        most = 2 * (len(self.pieces()) // 2) or 1
        return [
            pltpu.SemaphoreType.DMA((most, 2)),
            pltpu.SemaphoreType.DMA((most, 2)),
            pltpu.SemaphoreType.DMA((most,)),
            pltpu.SemaphoreType.DMA((2,)),
            pltpu.SemaphoreType.DMA((2,)),
        ]

    def bind(self, source, whole, send, receive, local, send_on, receive_on):
        self.source, self.whole, self.local = source, whole, local
        self.send, self.receive, self.send_on, self.receive_on = send, receive, send_on, receive_on
        self.here, along_x, along_y, self.far = shard_places()
        self.near = (along_x, along_y)
        self.kept, self.sent = [], []

    def block(self, place, start, rows):
        return pl.ds(pl.multiple_of(place * self.rows + start, 16), rows)

    def post(self):
        for j, (row, column, wide, into) in enumerate(self.pieces()):
            piece = self.source.at[pl.ds(row, self.rows), pl.ds(column, wide)]
            target = self.whole.at[self.block(self.here, 0, self.rows), pl.ds(into, wide)]
            self.kept.append(pltpu.make_async_copy(piece, target, self.local.at[j]))
            self.kept[-1].start()
            for hop, place in enumerate(self.near):
                self.push(piece, target, self.send.at[j, hop], self.receive.at[j, hop], place)

    def push(self, source, target, send, receive, place):
        self.sent.append(to_device("shard", source, target, send, receive, place))
        self.sent[-1].start()

    def pass_on(self):
        half = self.rows // 2
        for j, (_, _, wide, into) in enumerate(self.pieces()):
            for hop, place in enumerate(self.near):
                came = self.whole.at[self.block(place, 0, self.rows), pl.ds(into, wide)]
                to_device(
                    "shard", came, came, self.send.at[j, hop], self.receive.at[j, hop], place
                ).wait_recv()
        for hop in range(2):
            part = self.whole.at[self.block(self.near[1 - hop], hop * half, half)]
            self.push(part, part, self.send_on.at[hop], self.receive_on.at[hop], self.near[hop])

    def finish(self):
        half = self.rows // 2
        for hop in range(2):
            came = self.whole.at[self.block(self.far, hop * half, half)]
            to_device(
                "shard", came, came, self.send_on.at[hop], self.receive_on.at[hop], self.near[hop]
            ).wait_recv()
        for copy in self.kept:
            copy.wait()

    def close(self):
        for copy in self.sent:
            copy.wait_send()


class Spread:
    def __init__(self, chips):
        self.chips = chips

    def scratch(self):
        return [pltpu.SemaphoreType.DMA((self.chips,))] * 4 + [pltpu.SemaphoreType.DMA]

    def bind(self, own, group, send, receive, send_on, receive_on, local):
        self.own, self.group, self.local = own, group, local
        self.send, self.receive, self.send_on, self.receive_on = send, receive, send_on, receive_on
        self.me = lax.axis_index("context")
        self.chip, self.core = self.me // 2, lax.rem(self.me, 2)
        self.mate = self.me + 1 - 2 * self.core
        self.sent = []

    def push(self, source, target, send, receive, place):
        self.sent.append(to_device("context", source, target, send, receive, place))
        self.sent[-1].start()

    def other(self, k):
        if self.chips == 4:
            beside = self.chip + 1 - 2 * lax.rem(self.chip, 2)
            return (self.chip, beside, lax.rem(self.chip + 2, 4), 3 - self.chip)[k]
        return lax.rem(self.chip + self.chips - k, self.chips)

    def to_chip(self, block, k, place):
        self.push(block, block, self.send.at[k], self.receive.at[k], 2 * place + self.core)

    def post(self):
        mine = self.group.at[self.me]
        self.kept = pltpu.make_async_copy(self.own, mine, self.local)
        self.kept.start()
        first = len(self.sent)
        for k in range(1, 3 if self.chips == 4 else self.chips):
            place = self.other(k) if self.chips == 4 else lax.rem(self.chip + k, self.chips)
            self.sent.append(
                to_device(
                    "context",
                    self.own,
                    mine,
                    self.send.at[k],
                    self.receive.at[k],
                    2 * place + self.core,
                )
            )
        posted = self.sent[first:]
        for core, order in enumerate((posted, posted[::-1])):

            @pl.when(self.core == core)
            def _(order=order):
                for copy in order:
                    copy.start()

        self.push(self.own, mine, self.send_on.at[0], self.receive_on.at[0], self.mate)

    def arrived(self, k):
        block = self.group.at[2 * self.other(k) + self.core]
        to_device(
            "context", block, block, self.send.at[k], self.receive.at[k], self.mate
        ).wait_recv()
        self.push(block, block, self.send_on.at[k], self.receive_on.at[k], self.mate)

    def relay(self):
        if self.chips == 4:
            self.arrived(2)
            self.to_chip(self.group.at[2 * self.other(2) + self.core], 3, self.other(1))

    def pass_on(self):
        for k in (1, 3) if self.chips == 4 else range(1, self.chips):
            self.arrived(k)

    def finish(self):
        self.kept.wait()
        for k in range(self.chips):
            block = self.group.at[2 * (self.other(k) if k else self.chip) + 1 - self.core]
            to_device(
                "context", block, block, self.send_on.at[k], self.receive_on.at[k], self.mate
            ).wait_recv()
        for copy in self.sent:
            copy.wait_send()


def opening_kernel(gathers, spreads, *refs):
    refs = list(refs)

    def take(count):
        taken = refs[:count]
        del refs[:count]
        return taken

    sources = take(len(gathers) - 1)
    vector_refs = take(2)
    source_ref, mask_ref, cosine_ref, sine_ref = take(4)
    wholes = take(len(gathers))
    queries_ref, keyval_ref, resid_ref = take(3)
    groups = take(3)
    pair, attn, small, big, keyval, mixed, mixed_own, feed_own, out, out_came = take(10)
    vectors, vectors_own = take(2)
    swap_send, swap_receive, load, keyval_send, keyval_receive = take(5)
    for gather_of, source, whole in zip(gathers, [vectors_own] + sources, wholes):
        gather_of.bind(source, whole, *take(5))
    me, contexts = lax.axis_index("context"), lax.axis_size("context")
    chip, core = me // 2, lax.rem(me, 2)
    mate = me + 1 - 2 * core
    tok, model = source_ref.shape
    rows = 2 * tok
    attn_own = attn.at[pl.ds(pl.multiple_of(core * tok, tok), tok)]
    for spread, own, group in zip(spreads, (mixed_own, feed_own, attn_own), groups):
        spread.bind(own, group, *take(5))
    half = model // 2
    others = [lax.rem(me + k, contexts) for k in range(1, contexts)]
    vectors_own[...] = jnp.zeros_like(vectors_own)
    row = 0
    for ref in vector_refs:
        vectors_own[row : row + ref.shape[0], :] = ref[...]
        row += ref.shape[0]
    greet(gathers[0].near, others)
    vector_of, keyval_of, query_of, output_of, gate_up_of, down_of = gathers
    swaps = []

    def swap(step, source, target):
        swaps.append(
            to_device("context", source, target, swap_send.at[step], swap_receive.at[step], mate)
        )
        swaps[-1].start()

    def fetch(step, whole, target):
        copy = pltpu.make_async_copy(whole, target, load.at[step])
        copy.start()
        copy.wait()

    keyval_of.post()
    vector_of.post()
    query_of.post()
    pair[core] = source_ref[...]
    swap(0, source_ref, pair.at[core])

    vector_of.pass_on()
    vector_of.finish()
    fetch(0, vector_of.whole, vectors)

    def vector(row):
        tall = vector_of.rows
        return jnp.concatenate(
            [vectors[j * tall + row : j * tall + row + 1, :] for j in range(4)], axis=1
        ).astype(jnp.float32)

    swaps[0].wait_recv()
    attn[...] = rms_norm(
        pair[...].reshape(rows, model).astype(jnp.float32), vector(0)
    ).astype(jnp.bfloat16)

    keyval_of.pass_on()
    keyval_of.finish()
    fetch(1, keyval_of.whole, small)
    cosine, sine = cosine_ref[...], sine_ref[...]

    def turned(field):
        return field * cosine + pltpu.roll(field, DH // 4, 1) * sine

    raw = jnp.dot(attn[...], small[...], preferred_element_type=jnp.float32)
    at = pl.ds(pl.multiple_of(chip * rows, rows), rows)
    keyval[core, at, : DH // 2] = jnp.where(
        core == 0, turned(raw[:, : DH // 2]), raw[:, : DH // 2]
    ).astype(jnp.bfloat16)
    keyval[core, at, DH // 2 :] = raw[:, DH // 2 :].astype(jnp.bfloat16)
    keyval_sent = []
    for k in range(1, contexts):
        block = keyval.at[core, at]
        keyval_sent.append(
            to_device(
                "context", block, block, keyval_send.at[k], keyval_receive.at[k], others[k - 1]
            )
        )
        keyval_sent[-1].start()

    query_of.pass_on()
    query_of.finish()
    output_of.post()
    fetch(2, query_of.whole, big)
    heads = half // DH
    for h in range(heads):
        raw = jnp.dot(
            attn[...], big[:, h * DH : (h + 1) * DH], preferred_element_type=jnp.float32
        ) * DH ** (-0.5)
        queries_ref[:, h * DH : h * DH + DH // 2] = turned(raw[:, : DH // 2]).astype(jnp.bfloat16)
        queries_ref[:, h * DH + DH // 2 : (h + 1) * DH] = raw[:, DH // 2 :].astype(jnp.bfloat16)
    for k in range(1, contexts):
        place = lax.rem(me + contexts - k, contexts)
        block = keyval.at[
            lax.rem(place, 2), pl.ds(pl.multiple_of((place // 2) * rows, rows), rows)
        ]
        to_device(
            "context", block, block, keyval_send.at[k], keyval_receive.at[k], others[k - 1]
        ).wait_recv()
    spreads[2].post()
    for h in range(heads):
        weights = masked_weights(queries_ref[:, h * DH : (h + 1) * DH], keyval[0], mask_ref[...])
        mixed[core, :, h * DH : (h + 1) * DH] = jnp.dot(
            weights.astype(jnp.bfloat16), keyval[1], preferred_element_type=jnp.float32
        ).astype(jnp.bfloat16)
    swap(1, mixed.at[core], mixed.at[core])

    output_of.pass_on()
    gate_up_of.post()
    output_of.finish()
    down_of.post()
    fetch(3, output_of.whole, big)
    swaps[1].wait_recv()
    out[...] = jnp.dot(mixed[0], big[:half], preferred_element_type=jnp.float32) + jnp.dot(
        mixed[1], big[half:], preferred_element_type=jnp.float32
    )
    mine = pl.ds(pl.multiple_of(core * tok, tok), tok)
    theirs = pl.ds(pl.multiple_of((1 - core) * tok, tok), tok)
    swap(2, out.at[theirs], out_came)
    mixed_own[:, :half] = mixed[0, mine]
    mixed_own[:, half:] = mixed[1, mine]
    swaps[2].wait_recv()
    low = jnp.where(core == 0, out[mine], out_came[...])
    high = jnp.where(core == 0, out_came[...], out[mine])
    resid = (
        source_ref[...].astype(jnp.float32) + jnp.concatenate([low, high], axis=1) + vector(1)
    )
    resid_ref[...] = resid
    feed_own[...] = rms_norm(resid, vector(2)).astype(jnp.bfloat16)
    spreads[1].post()
    spreads[0].post()
    spreads[2].relay()
    spreads[2].pass_on()
    keyval_ref[...] = keyval[...]
    gate_up_of.pass_on()
    spreads[1].relay()
    down_of.pass_on()
    spreads[0].relay()
    spreads[1].pass_on()
    spreads[0].pass_on()
    for part in spreads:
        part.finish()
    gate_up_of.finish()
    down_of.finish()
    for gather_of in gathers:
        gather_of.close()
    for copy in swaps + keyval_sent:
        copy.wait_send()


def opening(number, cuts, vectors, source, mask, cosine, sine):
    contexts = lax.axis_size("context")
    tok, model = source.shape
    slots = mask.shape[1]
    half = model // 2
    gathers = [Gather(rows, pieces) for _, rows, pieces, _ in cuts]
    spreads = [Spread(contexts // 2) for _ in range(3)]
    low, full = jnp.bfloat16, jnp.float32
    dma = pltpu.SemaphoreType.DMA
    tall, wide = cuts[0][1], cuts[0][3]
    outs = pl.pallas_call(
        functools.partial(opening_kernel, gathers, spreads),
        in_specs=[pl.BlockSpec(memory_space=pl.ANY)] * (len(cuts) - 1)
        + [pl.BlockSpec(memory_space=pltpu.VMEM)] * 6,
        out_specs=[pl.BlockSpec(memory_space=pl.ANY)] * len(cuts)
        + [pl.BlockSpec(memory_space=pltpu.VMEM)] * 3
        + [pl.BlockSpec(memory_space=pl.ANY)] * 3,
        out_shape=[jax.ShapeDtypeStruct((4 * rows, columns), low) for _, rows, _, columns in cuts]
        + [
            jax.ShapeDtypeStruct((2 * tok, half), low),
            jax.ShapeDtypeStruct((2, slots, DH), low),
            jax.ShapeDtypeStruct((tok, model), full),
        ]
        + [jax.ShapeDtypeStruct((contexts, tok, model), low)] * 3,
        scratch_shapes=[
            pltpu.VMEM((2, tok, model), low),
            pltpu.VMEM((2 * tok, model), low),
            pltpu.VMEM((model, cuts[1][3]), low),
            pltpu.VMEM((model, half), low),
            pltpu.VMEM((2, slots, DH), low),
            pltpu.VMEM((2, 2 * tok, half), low),
            pltpu.VMEM((tok, model), low),
            pltpu.VMEM((tok, model), low),
            pltpu.VMEM((2 * tok, half), full),
            pltpu.VMEM((tok, half), full),
            pltpu.VMEM((4 * tall, wide), low),
            pltpu.VMEM((tall, wide), low),
            dma((3,)),
            dma((3,)),
            dma((4,)),
            dma((contexts,)),
            dma((contexts,)),
        ]
        + [shape for part in gathers + spreads for shape in part.scratch()],
        cost_estimate=pl.CostEstimate(flops=0, transcendentals=0, bytes_accessed=700_000_000),
        compiler_params=pltpu.CompilerParams(
            collective_id=number, has_side_effects=True, vmem_limit_bytes=VMEM_LIMIT
        ),
    )(*[array for array, _, _, _ in cuts[1:]], *vectors, source, mask, cosine, sine)
    return outs[: len(cuts)], outs[len(cuts) :]


class Product:
    def __init__(self, left, right):
        self.rows, self.wide = left[1] // 4, right[1]
        half = -(-self.wide // (2 * LANES)) * LANES
        self.sides = ((0, half), (half, self.wide - half))

    def buffers(self):
        return [pltpu.VMEM((3, self.rows, wide), jnp.bfloat16) for _, wide in self.sides]

    def scratch(self):
        return self.buffers() + self.buffers() + [pltpu.SemaphoreType.DMA((6,))] * 2

    def bind(self, left, right, made_a, made_b, came_a, came_b, send, receive):
        self.left, self.right, self.send, self.receive = left, right, send, receive
        self.made, self.came = (made_a, made_b), (came_a, came_b)
        self.here, along_x, along_y, self.far = shard_places()
        self.ways = ((along_x, along_y), (along_y, along_x))
        self.columns = [pl.ds(start, wide) for start, wide in self.sides]
        self.copies = []

    def product(self, place, side):
        block = pl.ds(pl.multiple_of(place * self.rows, LANES), self.rows)
        return over_rows(self.left[:, block], self.right[:, self.columns[side]])

    def push(self, step, side, place):
        slot = 2 * step + side
        self.copies.append(
            to_device(
                "shard",
                self.made[side].at[step],
                self.came[side].at[step],
                self.send.at[slot],
                self.receive.at[slot],
                place,
            )
        )
        self.copies[-1].start()

    def begin(self):
        for side in range(2):
            self.made[side][0] = self.product(self.far, side).astype(jnp.bfloat16)
            self.push(0, side, self.ways[side][0])
        for side in range(2):
            self.made[side][1] = self.product(self.ways[side][0], side).astype(jnp.bfloat16)
            self.push(1, side, self.ways[side][0])

    def middle(self):
        for side in range(2):
            kept = self.product(self.ways[side][1], side)
            self.copies[side].wait_recv()
            self.made[side][2] = (kept + self.came[side][0].astype(jnp.float32)).astype(
                jnp.bfloat16
            )
            self.push(2, side, self.ways[side][1])

    def finish(self, out):
        for side in range(2):
            total = self.product(self.here, side)
            self.copies[2 + side].wait_recv()
            total = total + self.came[side][1].astype(jnp.float32)
            self.copies[4 + side].wait_recv()
            out[:, self.columns[side]] = (
                total + self.came[side][2].astype(jnp.float32)
            ).astype(jnp.bfloat16)

    def drain(self, first, last):
        for copy in self.copies[first:last]:
            copy.wait_send()


class Exchange:
    def __init__(self, count, stride):
        self.count, self.stride = count, stride

    def scratch(self):
        return [pltpu.SemaphoreType.DMA((self.count,))] * 2 + [pltpu.SemaphoreType.DMA]

    def peers(self):
        me = lax.axis_index("context")
        slot, rest = me // self.stride, lax.rem(me, self.stride)
        places = [lax.rem(slot + k, self.count) for k in range(self.count)]
        return places, [place * self.stride + rest for place in places]

    def start(self, blocks, out, send, receive, local):
        slots, devices = self.peers()
        kept = pltpu.make_async_copy(blocks(slots[0]), out.at[slots[0]], local)
        kept.start()
        copies = []
        for k in range(1, self.count):
            copies.append(
                to_device(
                    "context", blocks(slots[k]), out.at[slots[0]], send.at[k], receive.at[k], devices[k]
                )
            )
            copies[-1].start()

        def finish():
            kept.wait()
            for k in range(1, self.count):
                source = slots[self.count - k]
                to_device(
                    "context", out.at[source], out.at[source], send.at[k], receive.at[k], devices[k]
                ).wait_recv()
            for copy in copies:
                copy.wait_send()

        return finish


def work_kernel(products, exchanges, chained, summed, packed, *refs):
    refs = list(refs)

    def take(count):
        taken = refs[:count]
        del refs[:count]
        return taken

    operands = [take(2) for _ in products]
    arrays = take(len(exchanges) - (1 if chained else 0))
    results = take(len(products))
    moved = take(len(exchanges))
    total_ref = take(1)[0] if summed else None
    held = [take(2) for _ in products]
    loads = take(1)[0] if products else None
    copies = []
    for i, (pair, targets) in enumerate(zip(operands, held)):
        for j in range(2):
            copies.append(pltpu.make_async_copy(pair[j], targets[j], loads.at[i, j]))
            copies[-1].start()
    if packed:
        apart = take(1)[0]
    product_scratch = [take(len(p.scratch())) for p in products]
    exchange_scratch = [take(len(e.scratch())) for e in exchanges]
    _, along_x, along_y, _ = shard_places()
    if summed:
        arrived, stage, stage_came, stage_send, stage_receive = take(5)
    everyone = max(exchanges, key=lambda e: e.count).peers()[1][1:] if exchanges else []
    greet((along_x, along_y), everyone)
    finishes, steps = [], []
    if summed:
        moved = [arrived] + moved[1:]

    def hop(step, place):
        steps.append(
            to_device(
                "shard",
                stage.at[step],
                stage_came.at[step],
                stage_send.at[step],
                stage_receive.at[step],
                place,
            )
        )
        steps[-1].start()

    for exchange, array, out, scratch in zip(exchanges, arrays, moved, exchange_scratch):
        finishes.append(exchange.start(lambda j, array=array: array.at[j], out, *scratch))
    for i, (product, (left, right), scratch) in enumerate(zip(products, held, product_scratch)):
        product.bind(left, right, *scratch)
        copies[2 * i].wait()
        copies[2 * i + 1].wait()
        if i == 1:
            if packed:
                wide = apart.shape[1] // 4
                apart[...] = jnp.zeros_like(apart)
                for j in range(4):
                    apart[:, j * wide : j * wide + packed] = left[:, j * packed : (j + 1) * packed]
                product.left = apart
            products[0].middle()
        product.begin()
    if summed:
        finishes.pop(0)()
        stage[0] = jnp.sum(arrived[...], axis=0)
        hop(0, along_x)
    if len(products) == 1:
        products[0].middle()
    for i, product in enumerate(products):
        if i == 1:
            product.middle()
        product.finish(results[i])
        if i == 0 and summed:
            steps[0].wait_recv()
            stage[1] = stage[0] + stage_came[0]
            hop(1, along_y)
        if chained and i == 0:
            rows = product.rows // exchanges[-1].count
            finishes.append(
                exchanges[-1].start(
                    lambda j: results[0].at[pl.ds(pl.multiple_of(j * rows, 16), rows)],
                    moved[-1],
                    *exchange_scratch[-1],
                )
            )
    if summed:
        steps[1].wait_recv()
        total_ref[...] = stage[1] + stage_came[1]
    for product in products:
        product.drain(0, 6)
    for step in steps:
        step.wait_send()
    for finish in finishes:
        finish()


def work(number, products=(), exchanges=(), chained=False, summed=False, packed=0):
    contexts = lax.axis_size("context")
    made = [Product(left.shape, right.shape) for left, right in products]
    apart = []
    if packed:
        rows, right = products[1][0].shape[0], products[1][1]
        apart = [(rows, 4 * -(-packed // LANES) * LANES)]
        made[1] = Product(apart[0], right.shape)
    swaps = [Exchange(array.shape[0], contexts // array.shape[0]) for array in exchanges]
    results = [jax.ShapeDtypeStruct((p.rows, p.wide), jnp.bfloat16) for p in made]
    moved = [jax.ShapeDtypeStruct(array.shape, array.dtype) for array in exchanges]
    if chained:
        swaps.append(Exchange(contexts, 1))
        moved.append(
            jax.ShapeDtypeStruct((contexts, made[0].rows // contexts, made[0].wide), jnp.bfloat16)
        )
    scratch = [pltpu.VMEM(operand.shape, operand.dtype) for pair in products for operand in pair]
    if made:
        scratch.append(pltpu.SemaphoreType.DMA((len(made), 2)))
    scratch += [pltpu.VMEM(each, jnp.bfloat16) for each in apart]
    scratch += [shape for part in made + swaps for shape in part.scratch()]
    totals = []
    if summed:
        block = exchanges[0].shape[1:]
        totals = [jax.ShapeDtypeStruct(block, jnp.float32)]
        moved[0] = jax.ShapeDtypeStruct((8, LANES), jnp.float32)
        scratch += [
            pltpu.VMEM(exchanges[0].shape, jnp.float32),
            pltpu.VMEM((2, *block), jnp.float32),
            pltpu.VMEM((2, *block), jnp.float32),
            pltpu.SemaphoreType.DMA((2,)),
            pltpu.SemaphoreType.DMA((2,)),
        ]
    vmem = pl.BlockSpec(memory_space=pltpu.VMEM)
    hbm = pl.BlockSpec(memory_space=pl.ANY)
    outs = pl.pallas_call(
        functools.partial(work_kernel, made, swaps, chained, summed, packed),
        in_specs=[hbm] * (2 * len(made) + len(exchanges)),
        out_specs=[vmem] * len(made) + [hbm] * len(swaps) + [vmem] * len(totals),
        out_shape=results + moved + totals,
        scratch_shapes=scratch,
        cost_estimate=pl.CostEstimate(flops=0, transcendentals=0, bytes_accessed=150_000_000),
        compiler_params=pltpu.CompilerParams(
            collective_id=number, has_side_effects=True, vmem_limit_bytes=VMEM_LIMIT
        ),
    )(*[operand for pair in products for operand in pair], *exchanges)
    others = outs[len(made) :]
    if summed:
        others = [others[-1], *others[1:-1]]
    return outs[1 if chained else 0 : len(made)], others


def norm_back(field, gain, grad):
    scale = lax.rsqrt(jnp.mean(field * field, axis=1, keepdims=True) + EPS)
    normed = field * scale
    bent = grad * gain
    back = scale * (bent - normed * jnp.mean(bent * normed, axis=1, keepdims=True))
    return back, jnp.sum(grad * normed, axis=0, keepdims=True)


def back_kernel(gate, up, swaps, *refs):
    refs = list(refs)

    def take(count):
        taken = refs[:count]
        del refs[:count]
        return taken

    output_ref, query_ref, keyval_ref, feed_ref, gate_ref, up_ref, down_ref = take(7)
    grad_ref, resid_ref, cotangent_ref, source_ref, gains_ref = take(5)
    queries_ref, keyval_of, mask_ref, cosine_ref, sine_ref = take(5)
    input_grad_ref, sums_ref, up_out, rows_out, back_out, down_out, gate_out = take(7)
    left, gate_right, up_right, big, small = take(5)
    own_grad, swapped, part, part_came, tail_came, mixed_back, query_back = take(7)
    pieces, pieces_mate, pieces_low, pieces_came = take(4)
    keyval_back, rows_blocks, back_blocks, gate_sum = take(4)
    load, mate_send, mate_receive = take(3)
    made = take(2)
    gate_scratch, up_scratch = take(4), take(4)
    rows_swap, back_swap, down_swap, gate_swap, piece_swap = swaps
    rows_sems, back_sems, down_sems, gate_sems, piece_sems = (take(3) for _ in swaps)
    me = lax.axis_index("context")
    chip, core = me // 2, lax.rem(me, 2)
    mate = me + 1 - 2 * core
    tok, model = resid_ref.shape
    half = model // 2
    rows = 2 * tok
    shards = lax.axis_size("shard")
    contexts = lax.axis_size("context")
    owned = model // (shards * contexts)
    mine = pl.ds(pl.multiple_of(core * tok, tok), tok)
    theirs = pl.ds(pl.multiple_of((1 - core) * tok, tok), tok)
    full = jnp.float32
    loads = []

    def fetch(source, target):
        loads.append(pltpu.make_async_copy(source, target, load.at[len(loads)]))
        loads[-1].start()
        return loads[-1]

    mates = []

    def to_mate(source, target):
        step = len(mates)
        mates.append(
            to_device("context", source, target, mate_send.at[step], mate_receive.at[step], mate)
        )
        mates[-1].start()
        return mates[-1]

    left_load, gate_load = fetch(feed_ref, left), fetch(gate_ref, gate_right)
    output_load, up_load = fetch(output_ref, big), fetch(up_ref, up_right)
    small_load = fetch(keyval_ref, small)
    _, along_x, along_y, _ = shard_places()
    greet((along_x, along_y), rows_swap.peers()[1][1:])
    finishes = [down_swap.start(lambda j: down_ref.at[j], down_out, *down_sems)]

    resid = resid_ref[...]
    cotangent = cotangent_ref[...].astype(full)
    resid_part, gain_two_grad = norm_back(resid, gains_ref[1:2], grad_ref[...])
    resid_grad = cotangent + resid_part
    input_grad_ref[...] = resid_grad
    attn_grad = resid_grad.astype(jnp.bfloat16)
    own_grad[...] = attn_grad
    swapped[core] = own_grad[:, pl.ds(pl.multiple_of(core * half, LANES), half)]
    first = to_mate(
        own_grad.at[:, pl.ds(pl.multiple_of((1 - core) * half, LANES), half)], swapped.at[core]
    )
    left_load.wait()
    gate_load.wait()
    gate.bind(left, gate_right, *made, *gate_scratch)
    gate.begin()
    sums_ref[...] = jnp.zeros_like(sums_ref)
    sums_ref[1:2] = jnp.sum(attn_grad.astype(full), axis=0, keepdims=True)
    sums_ref[2:3] = gain_two_grad
    sums_ref[3:4] = jnp.sum(cotangent, axis=0, keepdims=True)
    rows_blocks[...] = jnp.zeros_like(rows_blocks)
    for j in range(contexts):
        for shard in range(shards):
            start = (shard * contexts + j) * owned
            rows_blocks[j, :, shard * owned : (shard + 1) * owned] = attn_grad[
                :, start : start + owned
            ]
    finishes.append(rows_swap.start(lambda j: rows_blocks.at[j], rows_out, *rows_sems))

    first.wait_recv()
    output_load.wait()
    pair_grad = swapped[...].reshape(rows, half)
    for side in range(2):
        part[side] = against(pair_grad, big[side * half : (side + 1) * half])
    second = to_mate(part.at[1 - core], part_came)
    query_load = fetch(query_ref, big)
    second.wait_recv()
    mixed_back[...] = (part[core] + part_came[...]).astype(jnp.bfloat16)
    cosine, sine = cosine_ref[...], sine_ref[...]

    def unturned(field):
        return field * cosine - pltpu.roll(field, DH // 4, 1) * sine

    keys, values = keyval_of[0], keyval_of[1]
    for h in range(half // DH):
        at = slice(h * DH, (h + 1) * DH)
        queries, grad = queries_ref[:, at], mixed_back[:, at]
        weights = masked_weights(queries, keys, mask_ref[...])
        value_score = against(grad, values)
        delta = jnp.sum(weights * value_score, axis=1, keepdims=True)
        score_back = (weights * (value_score - delta)).astype(jnp.bfloat16)
        back = jnp.dot(score_back, keys, preferred_element_type=full) * DH ** (-0.5)
        query_back[:, h * DH : h * DH + DH // 2] = unturned(back[:, : DH // 2]).astype(jnp.bfloat16)
        query_back[:, h * DH + DH // 2 : (h + 1) * DH] = back[:, DH // 2 :].astype(jnp.bfloat16)
        key_piece = over_rows(score_back, queries)
        value_piece = over_rows(weights.astype(jnp.bfloat16), grad)
        if h == 0:
            pieces[0], pieces[1] = key_piece, value_piece
        else:
            pieces[0] += key_piece
            pieces[1] += value_piece
    fourth = to_mate(pieces.at[1 - core], pieces_mate)
    gate.middle()
    fourth.wait_recv()
    pieces_low[...] = (pieces[core] + pieces_mate[...]).astype(jnp.bfloat16)
    pieces_done = piece_swap.start(
        lambda j: pieces_low.at[pl.ds(pl.multiple_of(j * rows, rows), rows)],
        pieces_came,
        *piece_sems,
    )

    gate.drain(0, 4)
    up_load.wait()
    up.bind(left, up_right, *made, *up_scratch)
    up.begin()
    gate.finish(gate_sum)
    tall = gate.rows // contexts
    finishes.append(
        gate_swap.start(
            lambda j: gate_sum.at[pl.ds(pl.multiple_of(j * tall, 16), tall)], gate_out, *gate_sems
        )
    )

    pieces_done()
    total = jnp.sum(pieces_came[...].astype(full), axis=0)
    keyval_back[:, : DH // 2] = jnp.where(
        core == 0, unturned(total[:, : DH // 2]), total[:, : DH // 2]
    ).astype(jnp.bfloat16)
    keyval_back[:, DH // 2 :] = total[:, DH // 2 :].astype(jnp.bfloat16)
    chips = contexts // 2
    head_part, keyval_part = half // chips, DH // chips
    back_blocks[...] = jnp.zeros_like(back_blocks)
    for j in range(chips):
        back_blocks[j, :, :head_part] = query_back[:, j * head_part : (j + 1) * head_part]
        back_blocks[j, :, head_part : head_part + keyval_part] = keyval_back[
            :, j * keyval_part : (j + 1) * keyval_part
        ]
    finishes.append(back_swap.start(lambda j: back_blocks.at[j], back_out, *back_sems))
    query_load.wait()
    small_load.wait()
    second.wait_send()
    for side in range(2):
        at = slice(side * half, (side + 1) * half)
        part[side] = against(query_back[...], big[at]) + against(keyval_back[...], small[at])
    third = [to_mate(part.at[side, theirs], tail_came.at[side]) for side in range(2)]
    gate.drain(4, 6)
    up.middle()
    for copy in third:
        copy.wait_recv()
    attn_in_grad = jnp.concatenate([part[side, mine] + tail_came[side] for side in range(2)], axis=1)
    input_part, gain_one_grad = norm_back(
        source_ref[...].astype(full), gains_ref[0:1], attn_in_grad
    )
    input_grad_ref[...] += input_part
    sums_ref[0:1] = gain_one_grad
    up.finish(up_out)
    up.drain(0, 6)
    for copy in [first, fourth] + third:
        copy.wait_send()
    for finish in finishes:
        finish()


def back(number, weights, feed_group, gate_back, up_back, down_rows, tokens, attention):
    contexts, shards = lax.axis_size("context"), lax.axis_size("shard")
    tok, model = tokens[1].shape
    slots = attention[2].shape[1]
    half, rows, chips = model // 2, 2 * tok, contexts // 2
    owned = model // (shards * contexts)
    wide = -(-shards * owned // LANES) * LANES
    gate = Product(feed_group.shape, gate_back.shape)
    up = Product(feed_group.shape, up_back.shape)
    cols = max(half // chips + DH // chips, 2 * LANES)
    low, full = jnp.bfloat16, jnp.float32
    shape = jax.ShapeDtypeStruct
    swaps = [Exchange(n, contexts // n) for n in (contexts, chips, contexts, contexts, chips)]
    tall = gate.rows // contexts
    vmem, hbm = pl.BlockSpec(memory_space=pltpu.VMEM), pl.BlockSpec(memory_space=pl.ANY)
    dma = pltpu.SemaphoreType.DMA
    return pl.pallas_call(
        functools.partial(back_kernel, gate, up, swaps),
        in_specs=[hbm] * 7 + [vmem] * 10,
        out_specs=[vmem] * 3 + [hbm] * 4,
        out_shape=[
            shape((tok, model), full),
            shape((8, model), full),
            shape((up.rows, up.wide), low),
            shape((contexts, tok, wide), low),
            shape((chips, rows, cols), low),
            shape(down_rows.shape, low),
            shape((contexts, tall, gate.wide), low),
        ],
        scratch_shapes=[
            pltpu.VMEM(feed_group.shape, low),
            pltpu.VMEM(gate_back.shape, low),
            pltpu.VMEM(up_back.shape, low),
            pltpu.VMEM((model, half), low),
            pltpu.VMEM((model, DH), low),
            pltpu.VMEM((tok, model), low),
            pltpu.VMEM((2, tok, half), low),
            pltpu.VMEM((2, rows, half), full),
            pltpu.VMEM((rows, half), full),
            pltpu.VMEM((2, tok, half), full),
            pltpu.VMEM((rows, half), low),
            pltpu.VMEM((rows, half), low),
            pltpu.VMEM((2, slots, DH), full),
            pltpu.VMEM((slots, DH), full),
            pltpu.VMEM((slots, DH), low),
            pltpu.VMEM((chips, rows, DH), low),
            pltpu.VMEM((rows, DH), low),
            pltpu.VMEM((contexts, tok, wide), low),
            pltpu.VMEM((chips, rows, cols), low),
            pltpu.VMEM((gate.rows, gate.wide), low),
            dma((6,)),
            dma((5,)),
            dma((5,)),
        ]
        + gate.buffers()
        + (gate.buffers() + [dma((6,))] * 2)
        + (up.buffers() + [dma((6,))] * 2)
        + [each for swap in swaps for each in swap.scratch()],
        cost_estimate=pl.CostEstimate(flops=0, transcendentals=0, bytes_accessed=400_000_000),
        compiler_params=pltpu.CompilerParams(
            collective_id=number, has_side_effects=True, vmem_limit_bytes=BACK_LIMIT
        ),
    )(*weights, feed_group, gate_back, up_back, down_rows, *tokens, *attention)


def masked_weights(q, k, mask):
    scores = lax.dot_general(q, k, (((1,), (1,)), ((), ())), preferred_element_type=jnp.float32)
    scores = jnp.where(mask > 0.0, scores, NEG)
    raised = jnp.exp(scores - jnp.max(scores, axis=1, keepdims=True))
    return raised / jnp.sum(raised, axis=1, keepdims=True)


def mix_back_kernel(mask_ref, q_ref, k_ref, v_ref, g_ref, dq_ref, dk_ref, dv_ref):
    q, k, g = q_ref[...], k_ref[...], g_ref[...]
    weights = masked_weights(q, k, mask_ref[...])
    value_score = against(g, v_ref[...])
    delta = jnp.sum(weights * value_score, axis=1, keepdims=True)
    score_back = (weights * (value_score - delta)).astype(jnp.bfloat16)
    dq_ref[...] = jnp.dot(score_back, k, preferred_element_type=jnp.float32)
    key_piece = over_rows(score_back, q)
    value_piece = over_rows(weights.astype(jnp.bfloat16), g)

    @pl.when(pl.program_id(0) == 0)
    def _():
        dk_ref[...] = key_piece
        dv_ref[...] = value_piece

    @pl.when(pl.program_id(0) > 0)
    def _():
        dk_ref[...] += key_piece
        dv_ref[...] += value_piece


def mix_back(mask, queries, keys, values, grad):
    rows, width = queries.shape
    slots = keys.shape[0]
    whole = lambda h: (0, 0)
    part = lambda h: (0, h)
    return pl.pallas_call(
        mix_back_kernel,
        grid=(width // DH,),
        in_specs=[
            pl.BlockSpec((rows, slots), whole),
            pl.BlockSpec((rows, DH), part),
            pl.BlockSpec((slots, DH), whole),
            pl.BlockSpec((slots, DH), whole),
            pl.BlockSpec((rows, DH), part),
        ],
        out_specs=[
            pl.BlockSpec((rows, DH), part),
            pl.BlockSpec((slots, DH), whole),
            pl.BlockSpec((slots, DH), whole),
        ],
        out_shape=[
            jax.ShapeDtypeStruct((rows, width), jnp.float32),
            jax.ShapeDtypeStruct((slots, DH), jnp.float32),
            jax.ShapeDtypeStruct((slots, DH), jnp.float32),
        ],
        compiler_params=pltpu.CompilerParams(vmem_limit_bytes=VMEM_LIMIT),
    )(mask, queries, keys, values, grad)


def feed_kernel(feed_ref, grad_ref, gate_ref, up_ref, down_ref, bias_gate_ref, bias_up_ref, live_ref,
                hidden_ref, gate_back_ref, up_back_ref, gate_sum_ref, up_sum_ref):
    rows = feed_ref.shape[0]
    step = min(rows, 256)

    @pl.when(pl.program_id(1) == 0)
    def _():
        gate_sum_ref[...] = jnp.zeros_like(gate_sum_ref)
        up_sum_ref[...] = jnp.zeros_like(up_sum_ref)

    def part(i, carry):
        at = pl.ds(pl.multiple_of(i * step, step), step)
        feed = feed_ref[at, :]
        gate = jnp.dot(feed, gate_ref[...], preferred_element_type=jnp.float32) + bias_gate_ref[...]
        up = jnp.dot(feed, up_ref[...], preferred_element_type=jnp.float32) + bias_up_ref[...]
        back = against(grad_ref[at, :], down_ref[...])
        live = live_ref[...]
        square = gate * gate
        bend = jnp.tanh(GELU * gate * (1.0 + CUBE * square))
        half = 0.5 * (1.0 + bend)
        gelu = gate * half * live
        slope = half + 0.5 * gate * (1.0 - bend * bend) * (GELU * (1.0 + 3.0 * CUBE * square))
        hidden_ref[at, :] = (gelu * up).astype(jnp.bfloat16)
        gate_back = (back * up * slope * live).astype(jnp.bfloat16)
        up_back = (back * gelu).astype(jnp.bfloat16)
        gate_back_ref[at, :] = gate_back
        up_back_ref[at, :] = up_back
        gate_sum_ref[...] += jnp.sum(gate_back.astype(jnp.float32), axis=0, keepdims=True)
        up_sum_ref[...] += jnp.sum(up_back.astype(jnp.float32), axis=0, keepdims=True)
        return carry

    lax.fori_loop(0, rows // step, part, 0)


def feed(feed_group, grad_group, gate_up, down, bias, live):
    rows, model = feed_group.shape
    units = down.shape[0]
    wide = min(units, 256)
    blocks = units // wide
    tall = min(rows, 1024)
    buffers = {"pipeline_mode": pl.Buffered(1)} if tall == rows else {}
    tokens = lambda j, i: (i, 0)
    column = lambda j, i: (0, j)
    later = lambda j, i: (0, j + blocks)
    made = lambda j, i: (i, j)
    return pl.pallas_call(
        feed_kernel,
        grid=(blocks, rows // tall),
        in_specs=[
            pl.BlockSpec((tall, model), tokens, **buffers),
            pl.BlockSpec((tall, model), tokens, **buffers),
            pl.BlockSpec((model, wide), column),
            pl.BlockSpec((model, wide), later),
            pl.BlockSpec((wide, model), lambda j, i: (j, 0)),
            pl.BlockSpec((1, wide), column),
            pl.BlockSpec((1, wide), later),
            pl.BlockSpec((1, wide), column),
        ],
        out_specs=[
            pl.BlockSpec((tall, wide), made),
            pl.BlockSpec((tall, wide), made),
            pl.BlockSpec((tall, wide), made),
            pl.BlockSpec((1, wide), column),
            pl.BlockSpec((1, wide), column),
        ],
        out_shape=[
            jax.ShapeDtypeStruct((rows, units), jnp.bfloat16),
            jax.ShapeDtypeStruct((rows, units), jnp.bfloat16),
            jax.ShapeDtypeStruct((rows, units), jnp.bfloat16),
            jax.ShapeDtypeStruct((1, units), jnp.float32),
            jax.ShapeDtypeStruct((1, units), jnp.float32),
        ],
        compiler_params=pltpu.CompilerParams(vmem_limit_bytes=VMEM_LIMIT),
    )(feed_group, grad_group, gate_up, gate_up, down, bias, bias, live)


def middle_kernel(*refs):
    refs = list(refs)

    def take(count):
        taken = refs[:count]
        del refs[:count]
        return taken

    feed_ref, grad_ref, weight_ref, down_ref, bias_ref, live_ref = take(6)
    *leaving, down_out_ref, sums_ref, feed_grad_ref = take(6)
    hidden_ref, gate_back_ref, up_back_ref, down_rows, leave, down_leave = take(6)
    gate_weight, up_weight, down_weight, feed_rows, grad_rows = take(5)
    own_part, mate_out, mate_in, sent_out, came, swap_in = take(6)
    weight_load, row_load, mate_send, mate_receive, send, receive = take(6)
    me = lax.axis_index("context")
    chips = lax.axis_size("context") // 2
    chip, core = me // 2, lax.rem(me, 2)
    mate = me + 1 - 2 * core
    units, model = down_weight.shape
    rows, half, wide = feed_rows.shape[0], model // 2, 256
    blocks = units // wide
    full, low = jnp.float32, jnp.bfloat16
    mine = pl.ds(pl.multiple_of(core * half, LANES), half)
    theirs = pl.ds(pl.multiple_of((1 - core) * half, LANES), half)
    targets = [3 * (1 - chip // 2), lax.rem(2 + 3 * chip, 5), 1 + lax.rem(chip, 2), chip]
    inner = lax.rem(chip + 1, 4) // 2

    def token_rows(i):
        return pl.ds(pl.multiple_of(targets[i] * rows, rows), rows)

    def weight_loads(j):
        at = pl.ds(pl.multiple_of(j * wide, wide), wide)
        later = pl.ds(pl.multiple_of(units + j * wide, wide), wide)
        return [
            pltpu.make_async_copy(weight_ref.at[:, at], gate_weight.at[:, at], weight_load.at[j, 0]),
            pltpu.make_async_copy(weight_ref.at[:, later], up_weight.at[:, at], weight_load.at[j, 1]),
            pltpu.make_async_copy(down_ref.at[at], down_weight.at[at], weight_load.at[j, 2]),
        ]

    def row_loads(i):
        at = token_rows(i)
        return [
            pltpu.make_async_copy(feed_ref.at[at], feed_rows, row_load.at[i, 0]),
            pltpu.make_async_copy(grad_ref.at[at], grad_rows.at[at], row_load.at[i, 1]),
        ]

    for copy in row_loads(0):
        copy.start()
    for j in range(blocks):
        for copy in weight_loads(j):
            copy.start()
    greet((), [lax.rem(me + k, 2 * chips) for k in range(1, 2 * chips)])
    sums_ref[...] = jnp.zeros_like(sums_ref)
    to_mate, left = [], []

    def passed(which, i, chip_at):
        receiver, slot = LINE[chip_at][i]
        return to_device(
            "context",
            sent_out.at[which, i],
            came.at[which, slot],
            send.at[which, i],
            receive.at[which, slot],
            2 * receiver + core,
        )

    def arrived(which, slot):
        part = came.at[which, slot]
        to_device(
            "context", part, part, send.at[which, 0], receive.at[which, slot], mate
        ).wait_recv()
        own_part[which] += part[...].astype(full)

    def reduce(i, which, part):
        step = i
        if step >= 1:
            to_mate[step - 1].wait_send()
        mate_out[which] = part(theirs).astype(low)
        to_mate.append(
            to_device(
                "context",
                mate_out.at[which],
                mate_in.at[i % 2],
                mate_send.at[step],
                mate_receive.at[step],
                mate,
            )
        )
        to_mate[-1].start()
        own_part[which] = part(mine)
        to_mate[-1].wait_recv()
        own_part[which] += mate_in[i % 2].astype(full)
        if i + 1 == chips:
            return

        @pl.when(inner == 1)
        def _():
            arrived(which, i)

        sent_out[which, i] = own_part[which].astype(low)
        for chip_at in range(chips):

            @pl.when(chip == chip_at)
            def _(chip_at=chip_at):
                passed(which, i, chip_at).start()

    for i in range(chips):
        for copy in row_loads(i):
            copy.wait()
        at = token_rows(i)

        def block(j, carry, i=i, at=at):
            if i == 0:
                for copy in weight_loads(j):
                    copy.wait()
            cut = pl.ds(pl.multiple_of(j * wide, wide), wide)
            later = pl.ds(pl.multiple_of(units + j * wide, wide), wide)
            feed = feed_rows[...]
            gate = jnp.dot(feed, gate_weight[:, cut], preferred_element_type=full) + bias_ref[:, cut]
            up = jnp.dot(feed, up_weight[:, cut], preferred_element_type=full) + bias_ref[:, later]
            back = against(grad_rows[at, :], down_weight[cut])
            live = live_ref[:, cut]
            square = gate * gate
            bend = jnp.tanh(GELU * gate * (1.0 + CUBE * square))
            share = 0.5 * (1.0 + bend)
            gelu = gate * share * live
            slope = share + 0.5 * gate * (1.0 - bend * bend) * (GELU * (1.0 + 3.0 * CUBE * square))
            hidden_ref[at, cut] = (gelu * up).astype(low)
            gate_back = (back * up * slope * live).astype(low)
            up_back = (back * gelu).astype(low)
            gate_back_ref[at, cut] = gate_back
            up_back_ref[at, cut] = up_back
            sums_ref[0:1, cut] += jnp.sum(gate_back.astype(full), axis=0, keepdims=True)
            sums_ref[1:2, cut] += jnp.sum(up_back.astype(full), axis=0, keepdims=True)
            return carry

        lax.fori_loop(0, blocks, block, 0)
        if i + 1 < chips:
            for copy in row_loads(i + 1):
                copy.start()
        for j, made in enumerate((hidden_ref, gate_back_ref, up_back_ref)):
            left.append(pltpu.make_async_copy(made.at[at], leaving[j].at[at], leave.at[i, j]))
            left[-1].start()

        def feed_part(columns, at=at):
            return against(gate_back_ref[at, :], gate_weight[columns, :]) + against(
                up_back_ref[at, :], up_weight[columns, :]
            )

        reduce(i, 0, feed_part)
    for i in range(chips):
        at = token_rows(i)
        if i >= 2:
            left[-2].wait()
        down_rows[i % 2] = jnp.dot(
            hidden_ref[at, :], down_weight[...], preferred_element_type=full
        ).astype(low)
        left.append(pltpu.make_async_copy(down_rows.at[i % 2], down_out_ref.at[at], down_leave.at[i]))
        left[-1].start()
    tok = rows // 2
    own_rows = pl.ds(pl.multiple_of(core * tok, tok), tok)
    mate_rows = pl.ds(pl.multiple_of((1 - core) * tok, tok), tok)
    lasts = []

    def complete(which, out):
        for slot, missing in ((3, 0), (4, chips - 1)):

            @pl.when(chip != missing)
            def _(slot=slot):
                arrived(which, slot)

        lasts.append(
            to_device(
                "context",
                own_part.at[which, mate_rows],
                swap_in.at[which],
                mate_send.at[chips + which],
                mate_receive.at[chips + which],
                mate,
            )
        )
        lasts[-1].start()
        out[:, mine] = own_part[which, own_rows]

    complete(0, feed_grad_ref)
    lasts[0].wait_recv()
    feed_grad_ref[:, theirs] = swap_in[0]
    for copy in left[: 3 * chips] + left[-2:]:
        copy.wait()
    for i in range(chips - 1):
        passed(0, i, 0).wait_send()
    for copy in to_mate[-1:] + lasts:
        copy.wait_send()


def middle(number, feed_group, grad_group, gate_up, down, bias, live):
    group, model = feed_group.shape
    units, contexts = down.shape[0], lax.axis_size("context")
    chips, half = contexts // 2, model // 2
    rows = group // chips
    low, full = jnp.bfloat16, jnp.float32
    shape, dma = jax.ShapeDtypeStruct, pltpu.SemaphoreType.DMA
    vmem, hbm = pl.BlockSpec(memory_space=pltpu.VMEM), pl.BlockSpec(memory_space=pl.ANY)
    return pl.pallas_call(
        middle_kernel,
        in_specs=[hbm] * 4 + [vmem] * 2,
        out_specs=[hbm] * 4 + [vmem] * 2,
        out_shape=[shape((group, units), low)] * 3
        + [shape((group, model), low), shape((8, units), full), shape((rows // 2, model), full)],
        scratch_shapes=[pltpu.VMEM((group, units), low)] * 3
        + [pltpu.VMEM((2, rows, model), low), dma((chips, 3)), dma((chips,))]
        + [
            pltpu.VMEM((model, units), low),
            pltpu.VMEM((model, units), low),
            pltpu.VMEM((units, model), low),
            pltpu.VMEM((rows, model), low),
            pltpu.VMEM((group, model), low),
            pltpu.VMEM((1, rows, half), full),
            pltpu.VMEM((1, rows, half), low),
            pltpu.VMEM((2, rows, half), low),
            pltpu.VMEM((1, chips - 1, rows, half), low),
            pltpu.VMEM((1, chips + 1, rows, half), low),
            pltpu.VMEM((1, rows // 2, half), full),
            dma((units // 256, 3)),
            dma((chips, 2)),
            dma((chips + 1,)),
            dma((chips + 1,)),
            dma((1, chips)),
            dma((1, chips + 1)),
        ],
        cost_estimate=pl.CostEstimate(flops=0, transcendentals=0, bytes_accessed=200_000_000),
        compiler_params=pltpu.CompilerParams(
            collective_id=number, has_side_effects=True, vmem_limit_bytes=BACK_LIMIT
        ),
    )(feed_group, grad_group, gate_up, down, bias, live)


def body(
    inputs,
    doc_ids,
    cotangent,
    attn_gain,
    query_weight,
    keyval_weight,
    output_weight,
    output_bias,
    feed_gain,
    gate_up_weight,
    gate_up_bias,
    down_weight,
    down_bias,
):
    tok, model = inputs.shape
    shards, contexts = lax.axis_size("shard"), lax.axis_size("context")
    shard, place = lax.axis_index("shard"), lax.axis_index("context")
    core, chip = place % 2, place // 2
    group = tok * contexts
    owned = model // (shards * contexts)
    ff = gate_up_weight.shape[1] // 2
    width, per_shard = unit_tiles(ff, shards, contexts)
    unit_start = jnp.minimum(place * width, per_shard - width)
    units = shards * width * LANES

    shard_rows = model // shards
    block = width * LANES

    def half_of(wide):
        def pieces():
            column = lax.rem(lax.axis_index("context"), 2) * wide
            return [(0, pl.multiple_of(column, LANES), wide, 0)]

        return pieces

    def first_unit():
        return jnp.minimum(lax.axis_index("context") * width, per_shard - width) * LANES

    def gate_up_pieces():
        return [
            (0, pl.multiple_of(j * per_shard * LANES + first_unit(), LANES), block, j * block)
            for j in range(2 * shards)
        ]

    def down_pieces():
        return [(pl.multiple_of(first_unit(), LANES), 0, model, 0)]

    unit_at = unit_start * LANES + jnp.arange(block, dtype=jnp.int32)
    unit_live = jnp.tile(unit_at >= place * block, shards)[None, :].astype(jnp.float32)
    slots = jnp.arange(group, dtype=jnp.int32)
    pair_slots = chip * (2 * tok) + jnp.arange(2 * tok, dtype=jnp.int32)
    pair_docs = lax.dynamic_slice_in_dim(doc_ids, chip * (2 * tok), 2 * tok)
    distance = pair_slots[:, None] - slots[None, :]
    mask = (
        (pair_docs[:, None] == doc_ids[None, :]) & (distance >= 0) & (distance < WINDOW)
    ).astype(jnp.float32)
    angles = pair_slots.astype(jnp.float32)[:, None] * frequencies(DH)[None, :]
    cosine, sine = jnp.cos(angles), jnp.sin(angles)
    turns = (jnp.concatenate([cosine, cosine], axis=1), jnp.concatenate([-sine, sine], axis=1))
    vectors = [
        jnp.stack([attn_gain, output_bias, feed_gain, down_bias]),
        gate_up_bias.reshape(-1, shard_rows),
    ]
    vector_rows = 4 + gate_up_bias.shape[0] // shard_rows
    vector_tall = -(-vector_rows // 32) * 32
    core_cols, core_heads = keyval_weight.shape[1] // 2, query_weight.shape[1] // 2
    (vectors, keyval_half, query_half, output_half, gate_up_part, down_part), (
        queries, keyval, resid, mixed_group, feed_group, attn_group
    ) = opening(
        0,
        (
            (None, vector_tall, lambda: [(0, 0, shard_rows, 0)], shard_rows),
            (keyval_weight, shard_rows, half_of(core_cols), core_cols),
            (query_weight, shard_rows, half_of(core_heads), core_heads),
            (output_weight, shard_rows, half_of(model // 2), model // 2),
            (gate_up_weight, shard_rows, gate_up_pieces, 2 * units),
            (down_weight, block, down_pieces, model),
        ),
        vectors,
        inputs,
        mask,
        *turns,
    )
    grad_group = gather(cotangent, "context")
    vectors = vectors.reshape(shards, vector_tall, shard_rows).astype(jnp.float32)
    gain_one, gain_two, bias_down = (vectors[:, i].reshape(1, model) for i in (0, 2, 3))
    bias_gate_up = vectors[:, 4:vector_rows].reshape(2 * shards, per_shard * LANES)
    bias_gate_up = lax.dynamic_slice_in_dim(
        bias_gate_up, unit_start * LANES, block, 1
    ).reshape(1, 2 * units)
    source = inputs.astype(jnp.float32)
    keys, values = keyval[0], keyval[1]
    heads = core_heads // DH
    mixed_group, feed_group, attn_group = (
        field.reshape(group, model) for field in (mixed_group, feed_group, attn_group)
    )

    if group <= 1024 and contexts == 8:
        hidden, gate_back, up_back, down_part_out, unit_sums, feed_in_grad = middle(
            8, feed_group, grad_group, gate_up_part, down_part, bias_gate_up, unit_live
        )
        gate_sums, up_sums = unit_sums[0], unit_sums[1]
    else:
        hidden, gate_back, up_back, gate_sums, up_sums = feed(
            feed_group, grad_group, gate_up_part, down_part, bias_gate_up, unit_live
        )
        feed_part = against(
            jnp.concatenate([gate_back, up_back], axis=1), gate_up_part
        ).astype(jnp.bfloat16)
        feed_in_grad = lax.psum_scatter(feed_part, "context", scatter_dimension=0, tiled=True)
        feed_in_grad = feed_in_grad.astype(jnp.float32)
        down_part_out = jnp.dot(hidden, down_part, preferred_element_type=jnp.float32).astype(
            jnp.bfloat16
        )
    down_out = lax.psum_scatter(
        down_part_out, "context", scatter_dimension=0, tiled=True
    ).astype(jnp.float32)
    (down_sum,), _ = work(2, [(grad_group, after(hidden, feed_in_grad))])
    block_out = (resid + down_out + bias_down).astype(jnp.bfloat16)

    chips = contexts // 2
    rows_wide = -(-owned // LANES) * LANES
    head_part, keyval_part = HEADS * DH // contexts, DH // chips

    def by_owners(field):
        return field.reshape(contexts, owned, field.shape[1])

    if group <= 1024 and contexts == 8:
        gains = jnp.concatenate([gain_one, gain_two, jnp.zeros((6, model), jnp.float32)], axis=0)
        input_grad, sums, up_sum, attn_grad_rows, back_cols, down_rows, gate_rows = back(
            3,
            (output_half, query_half, keyval_half),
            feed_group,
            gate_back,
            up_back,
            by_owners(down_sum),
            (feed_in_grad, resid, cotangent, inputs, gains),
            (queries, keyval, mask, *turns),
        )
        sums = sums[:4].reshape(4 * model)
        attn_grad_rows = attn_grad_rows.reshape(group, attn_grad_rows.shape[2])
        back_cols = back_cols.reshape(group, back_cols.shape[2])
    else:
        grad_out = cotangent.astype(jnp.float32)
        resid_part, gain_two_grad = jax.vjp(rms_norm, resid, gain_two)[1](feed_in_grad)
        resid_grad = grad_out + resid_part
        attn_grad_low = resid_grad.astype(jnp.bfloat16)
        mixed_back = summed_half(
            against(swap_columns(attn_grad_low, core), output_half), core, 1
        ).astype(jnp.bfloat16)
        query_acc, key_acc, value_acc = mix_back(mask, queries, keys, values, mixed_back)
        keyval_acc = jnp.stack(
            [key_acc.reshape(contexts // 2, 2 * tok, DH), value_acc.reshape(contexts // 2, 2 * tok, DH)],
            axis=1,
        ).reshape(contexts, 2 * tok, DH).astype(jnp.bfloat16)
        attn_grad_rows = jnp.pad(
            attn_grad_low.reshape(tok, shards, contexts, owned).transpose(2, 0, 1, 3),
            ((0, 0), (0, 0), (0, 0), (0, rows_wide - owned)),
        ).reshape(contexts, tok, shards * rows_wide)
        (gate_sum,), (keyval_acc, attn_grad_rows) = work(
            3, [(feed_group, gate_back)], [keyval_acc, attn_grad_rows]
        )
        attn_grad_rows = attn_grad_rows.reshape(group, shards * rows_wide)
        keyval_acc = jnp.sum(keyval_acc.astype(jnp.float32), axis=0)
        keyval_back = jnp.where(core == 0, rotate(keyval_acc, cosine, -sine), keyval_acc).astype(
            jnp.bfloat16
        )
        query_back = (
            rotate(query_acc.reshape(2 * tok, heads, DH), cosine[:, None, :], -sine[:, None, :])
            * DH ** (-0.5)
        ).reshape(2 * tok, heads * DH).astype(jnp.bfloat16)
        attn_in_grad = summed_half(
            against(query_back, query_half) + against(keyval_back, keyval_half), core, 0
        )
        input_part, gain_one_grad = jax.vjp(rms_norm, source, gain_one)[1](attn_in_grad)
        input_grad = resid_grad + input_part

        def by_chips(field):
            return field.reshape(2 * tok, chips, field.shape[1] // chips).transpose(1, 0, 2)

        spare = max(2 * LANES - head_part - keyval_part, 0)
        back_cols = jnp.concatenate([by_chips(query_back), by_chips(keyval_back)], axis=2)
        back_cols = jnp.pad(back_cols, ((0, 0), (0, 0), (0, spare)))
        moving = [back_cols, by_owners(down_sum), by_owners(gate_sum)]
        (up_sum,), (back_cols, down_rows, gate_rows) = work(4, [(feed_group, up_back)], moving)
        back_cols = back_cols.reshape(group, back_cols.shape[2])

        sums = jnp.concatenate(
            [
                gain_one_grad.reshape(model),
                jnp.sum(attn_grad_low.astype(jnp.float32), axis=0),
                gain_two_grad.reshape(model),
                jnp.sum(grad_out, axis=0),
            ]
        )

    sums = jnp.concatenate([sums, gate_sums.reshape(units), up_sums.reshape(units)])
    unit_owned = 2 * ff // (shards * contexts)
    mine = sums[: 4 * model].reshape(4, shards, contexts, owned).transpose(2, 0, 1, 3)
    unit_sums = lax.dynamic_update_slice_in_dim(
        jnp.zeros((2 * shards, per_shard * LANES), jnp.float32),
        sums[4 * model :].reshape(2 * shards, block),
        unit_start * LANES,
        1,
    )
    unit_sums = unit_sums.reshape(shards, contexts, unit_owned).transpose(1, 0, 2)
    at = 4 * shards * owned
    wide = at + shards * unit_owned
    tall = -(-wide // (8 * LANES)) * LANES
    vectors = jnp.concatenate(
        [
            mine.reshape(contexts, at),
            unit_sums.reshape(contexts, wide - at),
            jnp.zeros((contexts, 8 * tall - wide), jnp.float32),
        ],
        axis=1,
    ).reshape(contexts, 8, tall)
    if owned % 16 == 0:
        (output_sum,), (vectors, up_rows, back_rows) = work(
            5,
            [(attn_group, back_cols), (attn_grad_rows, mixed_group)],
            [vectors, by_owners(up_sum)],
            True,
            True,
            owned,
        )
    else:
        (back_sum,), (vectors, up_rows) = work(
            5, [(attn_group, back_cols)], [vectors, by_owners(up_sum)], False, True
        )
        _, (back_rows,) = work(7, [], [by_owners(back_sum)])
        (output_sum,), _ = work(6, [(attn_grad_rows, mixed_group)])
    vectors = vectors.reshape(8 * tall)
    own = vectors[:at].reshape(4, shards, owned)
    own = lax.dynamic_index_in_dim(own, shard, 1, False)
    gate_up_bias_grad = lax.dynamic_index_in_dim(
        vectors[at:wide].reshape(shards, unit_owned), shard, 0, False
    )
    pieces = unit_pieces(contexts, shards, width, per_shard)
    down_grad, gate_up_grad, query_grad, keyval_grad, output_grad = lay(
        pieces,
        owned,
        (ff, 2 * ff, HEADS * DH, 2 * DH, model),
        down_rows,
        gate_rows,
        up_rows,
        back_rows,
        output_sum,
    )
    output_weight_grad, down_weight_grad = output_grad.T, down_grad.T
    return (
        block_out,
        input_grad,
        own[0],
        query_grad,
        keyval_grad,
        output_weight_grad,
        own[1],
        own[2],
        gate_up_grad,
        gate_up_bias_grad,
        down_weight_grad,
        own[3],
    )


def solution(mesh):
    placed = (
        P(("shard", "context"), None),
        P("shard"),
        P(("shard", "context"), None),
        P("shard"),
        P("shard", None),
        P("shard", None),
        P("shard", None),
        P("shard"),
        P("shard"),
        P("shard", None),
        P("shard"),
        P("shard", None),
        P("shard"),
    )
    return jax.shard_map(
        body,
        mesh=mesh,
        in_specs=placed,
        out_specs=(
            P(("shard", "context"), None),
            P(("shard", "context"), None),
            P(("shard", "context")),
            P(("shard", "context"), None),
            P(("shard", "context"), None),
            P(None, ("shard", "context")),
            P(("shard", "context")),
            P(("shard", "context")),
            P(("shard", "context"), None),
            P(("shard", "context")),
            P(None, ("shard", "context")),
            P(("shard", "context")),
        ),
        check_vma=False,
    )
```
